32 devices in a mesh: members: 2 (over y), lat: 4 (over z), lon: 2 (over x), chan: 2 (over core).
Axes of the slice: x: 2, y: 2, z: 4, core: 2. Of those that a mesh axis runs over, the one named last changes fastest.
Arguments:
- atmos_state: float32 [768, 96, 384], P(('members', 'lon', 'chan'), 'lat'), parts along dimension 0, may hold values from -6 to 6
- ocean_state: float32 [400, 16, 512], P('members', 'lat', ('lon', 'chan')), parts along dimension 0, may hold values from -6 to 6
- land_mask: int32 [16, 512], P('lat', ('lon', 'chan')), may hold values from 0 to 1, as said below
- spectral_filter: float32 [2, 384, 384, 96], P(None, ('lon', 'chan'), 'lat'), may hold values from -6 to 6
- atmos_gain: float32 [384], P(('lon', 'chan')), may hold values from 0.1 to 1.9
- flux_readout: float32 [8, 384], P(None, ('lon', 'chan')), may hold values from -0.3125 to 0.3125
- surface_coupling: float32 [384, 4], P(('lon', 'chan')), may hold values from -3 to 3
- surface_readout: float32 [4, 200], replicated, may hold values from -0.4375 to 0.4375
- flux_coupling: float32 [200, 8], replicated, may hold values from -2 to 2
- atmos_row_source: int32 [96, 2], P('lat'), may hold values from 0 to 15, as said below
- atmos_row_weight: float32 [96, 2], P('lat'), may hold values from 0.2 to 1
- atmos_col_source: int32 [384, 2], P(('lon', 'chan')), may hold values from 0 to 511, as said below
- atmos_col_weight: float32 [384, 2], P(('lon', 'chan')), may hold values from 0.2 to 1
- ocean_row_source: int32 [16, 2], P('lat'), may hold values from 0 to 95, as said below
- ocean_row_weight: float32 [16, 2], P('lat'), may hold values from 0.2 to 1
- ocean_col_source: int32 [512, 2], P(('lon', 'chan')), may hold values from 0 to 383, as said below
- ocean_col_weight: float32 [512, 2], P(('lon', 'chan')), may hold values from 0.2 to 1
- depth_taps: float32 [2, 200, 9], replicated, may hold values from -2 to 2
- block_gain: float32 [2, 200], replicated, may hold values from 0.1 to 1.9
- expand_weight: float32 [2, 200, 800], replicated, may hold values from -0.4375 to 0.4375
- reduce_weight: float32 [2, 800, 200], replicated, may hold values from -0.21875 to 0.21875
- layer_scale: float32 [2, 200], replicated, may hold values from 0.1 to 1.9
Outputs:
- atmos_next: float32 [768, 96, 384], P(('members', 'lon', 'chan'), 'lat'), parts along dimension 0
- ocean_next: float32 [400, 16, 512], P('members', 'lat', ('lon', 'chan')), parts along dimension 0
The draws below stay inside these ranges and needn't reach their ends.
There are 2 independent parts, one for each index of `members`. The reference program is written for one: setup_inputs(seed, part) draws one part's arguments, and reference() takes and returns one part's arrays. A program takes and returns all parts, laid end to end along the dimension named above; an argument that names none is the same for every part. Nothing has to cross between parts.
Inputs may be any that keep to these rules, and one draw needn't show every extreme that they name: `atmos_row_source`: row t holds b and b + 1, where b - (16 * t) // 96 is -1, 0 or 1 before b is clipped to 0 .. 14; the offsets -1 and 1 both occur. `atmos_col_source`: row t holds b mod 512 and (b + 1) mod 512, where b - (512 * t) // 384 is -1, 0 or 1; the offsets -1 and 1 both occur. `ocean_row_source`: row t holds b and b + 1, where b - (96 * t) // 16 is -1, 0 or 1 before b is clipped to 0 .. 94; the offsets -1 and 1 both occur. `ocean_col_source`: row t holds b mod 384 and (b + 1) mod 384, where b - (384 * t) // 512 is -1, 0 or 1; the offsets -1 and 1 both occur. `land_mask`: the first and last latitude rows are land.
All inputs are finite; a program needn't handle non-finite values.
Results may differ from the reference program's by a relative error of at most 0.0001.
Values sent between devices are 32-bit elements; how exact they have to be, the bound alone decides.
No kernel may reach another device: no remote copies, remote signals or barrier semaphores. Data moves between devices by JAX's collectives and lax.ppermute only.
A program may use at most 128 MiB of HBM per device.

```python
import jax
import jax.numpy as jnp
from jax import lax

CO = 200
HIDO = 800
CA = 384
HA = 96
WA = 384
NS = 4
NF = 8
NBLK = 2
HO = 16
WO = 512


def intersection_table(key, target, source, periodic):
    places = jnp.arange(target, dtype=jnp.int32)
    centre = places * source // target
    jitter = jax.random.randint(key, (target,), -1, 2, dtype=jnp.int32)
    middle = target // 2
    jitter = jnp.where(places == middle, -1, jnp.where(places == middle + 1, 1, jitter))
    lowest = centre + jitter
    if periodic:
        leading = jnp.mod(lowest, source)
        second = jnp.mod(lowest + 1, source)
    else:
        leading = jnp.clip(lowest, 0, source - 2)
        second = leading + 1
    return jnp.stack([leading, second], axis=1).astype(jnp.int32)


def draw_atmos_row_source(key, part):
    return intersection_table(key, HA, HO, False)


def draw_atmos_col_source(key, part):
    return intersection_table(key, WA, WO, True)


def draw_ocean_row_source(key, part):
    return intersection_table(key, HO, HA, False)


def draw_ocean_col_source(key, part):
    return intersection_table(key, WO, WA, True)


def draw_land_mask(key, part):
    cells = jax.random.randint(key, (HO, WO), 0, 4, dtype=jnp.int32)
    watery = (cells > 0).astype(jnp.int32)
    row_ids = jnp.arange(HO, dtype=jnp.int32)[:, None]
    return jnp.where((row_ids == 0) | (row_ids == HO - 1), 0, watery).astype(jnp.int32)


def block_scale(own_key, shape, cuts, low, top_value):
    def one(dim, shards_of):
        heights = jax.random.uniform(jax.random.fold_in(jax.random.fold_in(own_key, 6), dim), (shards_of,), jnp.float32, low / len(cuts), top_value / len(cuts))
        return jnp.repeat(jnp.exp(heights), shape[dim] // shards_of).reshape((-1,) + (1,) * (len(shape) - dim - 1))

    factor_of = one(*cuts[0])
    for cut in cuts[1:]:
        factor_of = factor_of * one(*cut)
    return factor_of


def normal_values(key, dims, scale, limit, shards=(), held_as=jnp.bfloat16):
    array = jax.random.normal(key, dims, jnp.float32) * scale
    if len(shards) > 0:
        array = block_scale(key, dims, shards, -0.22, 0.18) * array
    return jnp.clip(array, min=-limit, max=limit).astype(held_as)


def setup_inputs(seed: int = 0, part: int = 0) -> dict:
    streams_of = jax.random.split(jax.random.key(seed), 23)
    own_keys = jax.random.split(jax.random.fold_in(streams_of[22], part), 23)
    return {
        "atmos_state": normal_values(own_keys[0], (CA, HA, WA), 1.0, 6.0, ((0, 4), (1, 4)), jnp.float32),
        "ocean_state": normal_values(own_keys[1], (CO, HO, WO), 1.0, 6.0, ((1, 4), (2, 4)), jnp.float32),
        "land_mask": draw_land_mask(jax.random.fold_in(streams_of[22], 71), part),
        "spectral_filter": normal_values(streams_of[3], (2, CA, WA, HA), 1.0, 6.0, ((1, 4), (2, 4)), jnp.float32),
        "atmos_gain": jnp.clip(1.0 + 0.18 * jax.random.normal(streams_of[4], (CA,), jnp.float32), 0.1, 1.9),
        "flux_readout": normal_values(streams_of[5], (NF, CA), CA ** -0.5, 0.3125, ((1, 4),), jnp.float32),
        "surface_coupling": normal_values(streams_of[6], (CA, NS), NS ** -0.5, 3.0, ((0, 4),), jnp.float32),
        "surface_readout": normal_values(streams_of[7], (NS, CO), CO ** -0.5, 0.4375, (), jnp.float32),
        "flux_coupling": normal_values(streams_of[8], (CO, NF), NF ** -0.5, 2.0, (), jnp.float32),
        "atmos_row_source": draw_atmos_row_source(jax.random.fold_in(streams_of[22], 71), part),
        "atmos_row_weight": jnp.clip(0.2 + 0.8 * jax.random.uniform(streams_of[10], (HA, 2), jnp.float32) ** block_scale(streams_of[10], (HA, 2), ((0, 4),), -0.2, 0.2), 0.2, 1.0),
        "atmos_col_source": draw_atmos_col_source(jax.random.fold_in(streams_of[22], 71), part),
        "atmos_col_weight": jnp.clip(0.2 + 0.8 * jax.random.uniform(streams_of[12], (WA, 2), jnp.float32) ** block_scale(streams_of[12], (WA, 2), ((0, 4),), -0.2, 0.2), 0.2, 1.0),
        "ocean_row_source": draw_ocean_row_source(jax.random.fold_in(streams_of[22], 71), part),
        "ocean_row_weight": jnp.clip(0.2 + 0.8 * jax.random.uniform(streams_of[14], (HO, 2), jnp.float32) ** block_scale(streams_of[14], (HO, 2), ((0, 4),), -0.2, 0.2), 0.2, 1.0),
        "ocean_col_source": draw_ocean_col_source(jax.random.fold_in(streams_of[22], 71), part),
        "ocean_col_weight": jnp.clip(0.2 + 0.8 * jax.random.uniform(streams_of[16], (WO, 2), jnp.float32) ** block_scale(streams_of[16], (WO, 2), ((0, 4),), -0.2, 0.2), 0.2, 1.0),
        "depth_taps": normal_values(streams_of[17], (NBLK, CO, 9), 9 ** -0.5, 2.0, (), jnp.float32),
        "block_gain": jnp.clip(1.0 + 0.18 * jax.random.normal(streams_of[18], (NBLK, CO), jnp.float32), 0.1, 1.9),
        "expand_weight": normal_values(streams_of[19], (NBLK, CO, HIDO), CO ** -0.5, 0.4375, (), jnp.float32),
        "reduce_weight": normal_values(streams_of[20], (NBLK, HIDO, CO), HIDO ** -0.5, 0.21875, (), jnp.float32),
        "layer_scale": jnp.clip(1.0 + 0.18 * jax.random.normal(streams_of[21], (NBLK, CO), jnp.float32), 0.1, 1.9),
    }


EPSILON = 1e-05
PRECISE = lax.Precision.HIGHEST

def shares_of(weight):
    return weight / lax.optimization_barrier(jnp.sum(weight, axis=1, keepdims=True))

def regrid(field, row_source, row_weight, col_source, col_weight):
    row_share = shares_of(row_weight)
    col_share = shares_of(col_weight)
    by_rows = field[:, row_source[:, 0], :] * row_share[None, :, 0:1] + field[:, row_source[:, 1], :] * row_share[None, :, 1:2]
    return by_rows[:, :, col_source[:, 0]] * col_share[None, None, :, 0] + by_rows[:, :, col_source[:, 1]] * col_share[None, None, :, 1]

def depthwise(field, taps):
    height = field.shape[1]
    width = field.shape[2]
    padded = jnp.pad(field, ((0, 0), (1, 1), (0, 0)))
    padded = jnp.concatenate([padded[:, :, -1:], padded, padded[:, :, :1]], axis=2)
    result = jnp.zeros_like(field)
    for row_off in range(3):
        for col_off in range(3):
            result = result + taps[:, 3 * row_off + col_off][:, None, None] * padded[:, row_off:row_off + height, col_off:col_off + width]
    return result

def channel_mixer(values, gain, expand, reduce_w):
    centre = lax.optimization_barrier(jnp.mean(values, axis=0))
    spread = lax.optimization_barrier(jnp.mean(values * values, axis=0)) - centre * centre
    normed = (values - centre) * lax.rsqrt(spread + EPSILON) * gain[:, None]
    hidden = jax.nn.gelu(jnp.einsum('cd,cp->dp', expand, normed, precision=PRECISE))
    return jnp.einsum('dc,dp->cp', reduce_w, hidden, precision=PRECISE)

def reference(atmos_state, ocean_state, land_mask, spectral_filter, atmos_gain, flux_readout, surface_coupling, surface_readout, flux_coupling, atmos_row_source, atmos_row_weight, atmos_col_source, atmos_col_weight, ocean_row_source, ocean_row_weight, ocean_col_source, ocean_col_weight, depth_taps, block_gain, expand_weight, reduce_weight, layer_scale):
    centre = lax.optimization_barrier(jnp.sum(atmos_state, axis=0)) / CA
    spread = lax.optimization_barrier(jnp.sum(atmos_state * atmos_state, axis=0)) / CA - centre * centre
    normed = (atmos_state - centre) * lax.rsqrt(spread + EPSILON) * atmos_gain[:, None, None]
    spectrum = jnp.fft.fft2(normed, axes=(1, 2))
    kernel = jnp.transpose(spectral_filter[0] + 1j * spectral_filter[1], (0, 2, 1))
    filtered = jnp.real(jnp.fft.ifft2(kernel * spectrum, axes=(1, 2)))
    surface = jnp.einsum('sc,chw->shw', surface_readout, ocean_state, precision=PRECISE)
    surface_atmos = regrid(surface, atmos_row_source, atmos_row_weight, atmos_col_source, atmos_col_weight)
    atmos_next = atmos_state + filtered + jnp.einsum('cs,shw->chw', surface_coupling, surface_atmos, precision=PRECISE)
    flux = jnp.einsum('fc,chw->fhw', flux_readout, atmos_state, precision=PRECISE)
    flux_ocean = regrid(flux, ocean_row_source, ocean_row_weight, ocean_col_source, ocean_col_weight)
    ocean_mask = land_mask.astype(jnp.float32)
    current = ocean_mask * (ocean_state + jnp.einsum('cf,fhw->chw', flux_coupling, flux_ocean, precision=PRECISE))
    for which in range(NBLK):
        conv = depthwise(current, depth_taps[which])
        by_rows = jnp.transpose(conv, (1, 0, 2))
        gain = block_gain[which]
        expand = expand_weight[which]
        reduce_w = reduce_weight[which]
        update = lax.map(lambda row_vals: channel_mixer(row_vals, gain, expand, reduce_w), by_rows)
        update = jnp.transpose(update, (1, 0, 2))
        current = ocean_mask * (current + layer_scale[which][:, None, None] * update)
    return (atmos_next, current)
```

```python
import functools
import math

import jax
import jax.numpy as jnp
import ml_dtypes
import numpy as np
from jax import lax
from jax.experimental import pallas as pl
from jax.experimental.pallas import tpu as pltpu
from jax.sharding import PartitionSpec as P

CA = 384


EPSILON = 1e-05
PRECISE = lax.Precision.HIGHEST
FINE = lax.Precision.HIGH
LANES = 128
CHUNKS = 2
COLUMN = ("lon", "chan")


def padded(x, sides, width):
    for axis, dim in sides:
        count, length = (lax.axis_size(axis), x.shape[dim])
        up = [(i, (i + 1) % count) for i in range(count)]
        down = [(j, i) for i, j in up]
        last = lax.slice_in_dim(x, length - width, length, axis=dim)
        leading = lax.slice_in_dim(x, 0, width, axis=dim)
        before = lax.ppermute(last, axis, up)
        after = lax.ppermute(leading, axis, down)
        x = jnp.concatenate([before, x, after], axis=dim)
    return x


def fourier_tables(length):
    places = jnp.arange(length, dtype=jnp.int32)
    angles = (
        2.0
        * math.pi
        / length
        * jnp.mod(places[:, None] * places[None, :], length).astype(jnp.float32)
    )
    return (jnp.cos(angles), jnp.sin(angles))


def regrid_matrix(source, weight, offset, span, period):
    shares = weight / jnp.sum(weight, axis=1, keepdims=True)
    relative = source - offset
    if period > 0:
        relative = jnp.mod(relative, period)
    columns = jnp.arange(span, dtype=jnp.int32)[None, :]
    return shares[:, 0:1] * (relative[:, 0:1] == columns).astype(jnp.float32) + shares[:, 1:2] * (
        relative[:, 1:2] == columns
    ).astype(jnp.float32)


def apply_maps(field, row_map, col_map):
    by_rows = jnp.einsum("jh,shw->sjw", row_map, field, precision=PRECISE)
    return jnp.einsum("sjw,kw->sjk", by_rows, col_map, precision=PRECISE)


def grid_rims(field):
    return padded(field, (("lat", 1), (("lon", "chan"), 2)), 2)


def along_last(field, table):
    return jnp.einsum("ckh,hm->ckm", field, table, precision=PRECISE)


def global_filter(normed, spectral_filter):
    width_len = normed.shape[2]
    height_len = spectral_filter.shape[3]
    cos_w, sin_w = fourier_tables(width_len)
    cos_h, sin_h = fourier_tables(height_len)
    real_w = jnp.einsum("chn,nk->ckh", normed, cos_w, precision=PRECISE)
    imag_w = -jnp.einsum("chn,nk->ckh", normed, sin_w, precision=PRECISE)
    real_w, imag_w = (
        lax.all_to_all(real_w, "lat", split_axis=1, concat_axis=2, tiled=True),
        lax.all_to_all(imag_w, "lat", split_axis=1, concat_axis=2, tiled=True),
    )
    real_s = along_last(real_w, cos_h) + along_last(imag_w, sin_h)
    imag_s = along_last(imag_w, cos_h) - along_last(real_w, sin_h)
    kern_real = spectral_filter[0]
    kern_imag = spectral_filter[1]
    real_f = kern_real * real_s - kern_imag * imag_s
    imag_f = kern_real * imag_s + kern_imag * real_s
    real_b = (along_last(real_f, cos_h) - along_last(imag_f, sin_h)) / height_len
    imag_b = (along_last(imag_f, cos_h) + along_last(real_f, sin_h)) / height_len
    real_b, imag_b = (
        lax.all_to_all(real_b, "lat", split_axis=2, concat_axis=1, tiled=True),
        lax.all_to_all(imag_b, "lat", split_axis=2, concat_axis=1, tiled=True),
    )
    back = jnp.einsum("ckh,kn->chn", real_b, cos_w, precision=PRECISE) - jnp.einsum(
        "ckh,kn->chn", imag_b, sin_w, precision=PRECISE
    )
    return back / width_len


def flux_reach(atm_rows, ocean_rows):
    first = (-2 * atm_rows) // ocean_rows - 1
    last = (atm_rows * (ocean_rows + 1)) // ocean_rows + 2
    return -first, max(last - atm_rows + 1, 0)


def rows_around(field, before, after):
    count = lax.axis_size("lat")
    up = [(i, i + 1) for i in range(count - 1)]
    down = [(i + 1, i) for i in range(count - 1)]
    rows = field.shape[1]
    above = lax.ppermute(field[:, rows - before :], "lat", up)
    below = lax.ppermute(field[:, :after], "lat", down)
    return jnp.concatenate([above, field, below], axis=1)


def params(mib):
    return pltpu.CompilerParams(vmem_limit_bytes=mib * 2**20)


def can_deal(channels, rows, width, freqs, height, lat, members):
    return (
        members == 2
        and channels % (lat * CHUNKS * members) == 0
        and rows % 8 == 0
        and rows * lat == height
        and width % LANES == 0
        and freqs * lat == width
        and freqs == 96
        and height % 32 == 0
    )


def split_table(table):
    high = table.astype(ml_dtypes.bfloat16)
    low = (table - high.astype(np.float64)).astype(ml_dtypes.bfloat16)
    return high, low


@functools.lru_cache(maxsize=None)
def dealt_tables(height, width, lat):
    freqs = width // lat
    angle = 2.0 * np.pi / height * (np.outer(np.arange(height), np.arange(height)) % height)
    cos_h, sin_h = np.cos(angle), np.sin(angle)
    rows_on = np.block([[cos_h, sin_h], [-sin_h, cos_h]])
    rows_back = np.block([[cos_h, -sin_h], [sin_h, cos_h]])
    cols_on = np.zeros((lat, width, 2, lat, LANES))
    for z in range(lat):
        for j in range(lat):
            k = (z + j) % lat * freqs + np.arange(freqs)
            turn = 2.0 * np.pi / width * (np.outer(np.arange(width), k) % width)
            cols_on[z, :, 0, j, :freqs] = np.cos(turn)
            cols_on[z, :, 1, j, :freqs] = -np.sin(turn)
    cols_on = cols_on.reshape(lat, width, 2 * lat * LANES)
    cols_back = np.swapaxes(cols_on, 1, 2) / (height * width)
    return [split_table(t) for t in (cols_on, rows_on, rows_back, cols_back)]


def pack_kernel(count, place_ref, filter_ref, *out_refs):
    step = pl.program_id(0)
    rows = filter_ref.shape[3]
    freqs = filter_ref.shape[2]
    main, rest = rows * 3 // 4, rows // 4
    for j in range(count):

        @pl.when(step == j)
        def _(out=out_refs[j]):
            for part in range(2):
                for c in range(filter_ref.shape[1]):
                    turned = filter_ref[part, c].T
                    out[part, c, :, 0:freqs] = turned[0:main]
                    for i in range(3):
                        out[part, c, i * rest : (i + 1) * rest, freqs:LANES] = turned[
                            main:, 32 * i : 32 * (i + 1)
                        ]


def pack_filter(spectral_filter, place, lat, members, chunk):
    _, channels, freqs, height = spectral_filter.shape
    half = channels // (lat * CHUNKS * members)
    packed = (2, half, height * 3 // 4, LANES)

    def source(j, place):
        dest = lax.rem(place[0] + j, lat)
        return (0, (dest * CHUNKS + chunk) * members + place[1], 0, 0)

    return pl.pallas_call(
        functools.partial(pack_kernel, lat),
        grid_spec=pltpu.PrefetchScalarGridSpec(
            num_scalar_prefetch=1,
            grid=(lat,),
            in_specs=[pl.BlockSpec((2, half, freqs, height), source)],
            out_specs=[pl.BlockSpec(packed, lambda j, place: (0, 0, 0, 0))] * lat,
        ),
        out_shape=[jax.ShapeDtypeStruct(packed, jnp.float32)] * lat,
        compiler_params=params(32),
        name="pack_filter",
    )(place, spectral_filter)


def sums_kernel(readout_ref, state_ref, out_ref):
    channels, tile, width = state_ref.shape
    fluxes = readout_ref.shape[0]

    def add(c, totals):
        value = state_ref[c]
        new = [totals[f] + readout_ref[f, c] * value for f in range(fluxes)]
        return (*new, totals[fluxes] + value, totals[fluxes + 1] + value * value)

    zero = jnp.zeros((tile, width), jnp.float32)
    totals = lax.fori_loop(0, channels, add, (zero,) * (fluxes + 2), unroll=4)
    for i, total in enumerate(totals):
        out_ref[i] = total


def channel_sums(atmos_state, flux_readout):
    channels, rows, width = atmos_state.shape
    fluxes = flux_readout.shape[0]
    return pl.pallas_call(
        sums_kernel,
        grid=(rows // 8,),
        in_specs=[
            pl.BlockSpec(memory_space=pltpu.SMEM),
            pl.BlockSpec((channels, 8, width), lambda i: (0, i, 0)),
        ],
        out_specs=pl.BlockSpec((fluxes + 2, 8, width), lambda i: (0, i, 0)),
        out_shape=jax.ShapeDtypeStruct((fluxes + 2, rows, width), jnp.float32),
        compiler_params=params(32),
        name="channel_sums",
    )(flux_readout, atmos_state)


def norm_kernel(count, place_ref, gain_ref, sums_ref, state_ref, *out_refs):
    step = pl.program_id(0)
    part = state_ref.shape[0]
    first = (lax.rem(place_ref[0] + step, count) * CHUNKS + place_ref[2]) * part
    centre = sums_ref[0] / CA
    spread = sums_ref[1] / CA - centre * centre
    scale = lax.rsqrt(spread + EPSILON)
    for j in range(count):

        @pl.when(step == j)
        def _(out=out_refs[j]):
            for c in range(part):
                out[c] = (state_ref[c] - centre) * scale * gain_ref[first + c]


def normed_pieces(atmos_state, sums, gain, place, lat, chunk):
    channels, rows, width = atmos_state.shape
    part = channels // (lat * CHUNKS)
    place = jnp.concatenate([place, jnp.full((1,), chunk, jnp.int32)])
    return pl.pallas_call(
        functools.partial(norm_kernel, lat),
        grid_spec=pltpu.PrefetchScalarGridSpec(
            num_scalar_prefetch=1,
            grid=(lat,),
            in_specs=[
                pl.BlockSpec(memory_space=pltpu.SMEM),
                pl.BlockSpec((2, rows, width), lambda j, place: (0, 0, 0)),
                pl.BlockSpec(
                    (part, rows, width),
                    lambda j, place: (lax.rem(place[0] + j, lat) * CHUNKS + chunk, 0, 0),
                ),
            ],
            out_specs=[pl.BlockSpec((part, rows, width), lambda j, place: (0, 0, 0))] * lat,
        ),
        out_shape=[jax.ShapeDtypeStruct((part, rows, width), jnp.float32)] * lat,
        compiler_params=params(32),
        name="normed_pieces",
    )(place, gain, sums, atmos_state)


def split(value):
    high = value.astype(jnp.bfloat16)
    return high, (value - high.astype(jnp.float32)).astype(jnp.bfloat16)


def product(left, right):
    dot = functools.partial(jnp.dot, preferred_element_type=jnp.float32)
    return dot(left[0], right[0]) + (dot(left[0], right[1]) + dot(left[1], right[0]))


def unpacked(packed_ref, count, part, c):
    blocks = []
    lane = lax.broadcasted_iota(jnp.int32, (packed_ref.shape[3] // 3, LANES), 1)
    rest = packed_ref.shape[3] // 3
    for j in range(count):
        main = packed_ref[j, part, c]
        a, b, d = (
            pltpu.roll(main[i * rest : (i + 1) * rest], 32 * (i + 1), 1) for i in range(3)
        )
        tail = jnp.where(lane < 32, a, jnp.where(lane < 64, b, d))
        blocks.append(jnp.concatenate([main, tail], axis=0))
    return jnp.concatenate(blocks, axis=1)


def spectral_kernel(count, place_ref, *refs):
    pieces = refs[:count]
    own_ref, other_ref = refs[count : count + 2]
    tables = [(refs[count + 2 + 2 * i], refs[count + 3 + 2 * i]) for i in range(4)]
    outs = refs[count + 10 : 2 * count + 10]
    high_ref, low_ref = refs[2 * count + 10 :]
    part, rows, width = pieces[0].shape
    height = rows * count
    span = count * LANES
    cols_on, rows_on, rows_back, cols_back = tables
    cols_on = (cols_on[0][0], cols_on[1][0])
    cols_back = (cols_back[0][0], cols_back[1][0])
    rows_on = (rows_on[0][...], rows_on[1][...])
    rows_back = (rows_back[0][...], rows_back[1][...])

    def run(filter_ref):
        stacked = jnp.concatenate([p[...].reshape(part * rows, width) for p in pieces], axis=0)
        spectra = product(split(stacked), cols_on)
        for c in range(part):
            own = jnp.concatenate(
                [spectra[(j * part + c) * rows : (j * part + c + 1) * rows] for j in range(count)],
                axis=0,
            )
            both = jnp.concatenate([own[:, :span], own[:, span:]], axis=0)
            full = product(rows_on, split(both))
            real, imag = full[:height], full[height:]
            kern_real = unpacked(filter_ref, count, 0, c)
            kern_imag = unpacked(filter_ref, count, 1, c)
            both = jnp.concatenate(
                [kern_real * real - kern_imag * imag, kern_real * imag + kern_imag * real], axis=0
            )
            back = product(rows_back, split(both))
            high, low = split(back)
            at = slice(c * height, (c + 1) * height)
            high_ref[at, :span] = high[:height]
            high_ref[at, span:] = high[height:]
            low_ref[at, :span] = low[:height]
            low_ref[at, span:] = low[height:]
        result = product((high_ref[...], low_ref[...]), cols_back)
        result = result.reshape(part, height, width)
        for j in range(count):
            outs[j][...] = result[:, j * rows : (j + 1) * rows]

    @pl.when(pl.program_id(0) == 0)
    def _():
        run(own_ref)

    @pl.when(pl.program_id(0) == 1)
    def _():
        run(other_ref)


def filtered_pieces(pieces, own, other, place):
    lat = len(pieces)
    chunk, rows, width = pieces[0].shape
    half = chunk // 2
    height = rows * lat
    tables = [t for pair in dealt_tables(height, width, lat) for t in pair]

    def mine(i, place):
        return (lax.rem(i + place[1], 2), 0, 0)

    def table_spec(t):
        if t.ndim == 3:
            return pl.BlockSpec((1, *t.shape[1:]), lambda i, place: (place[0], 0, 0))
        return pl.BlockSpec(t.shape, lambda i, place: (0, 0))

    filter_spec = pl.BlockSpec(own.shape, lambda i, place: (0, 0, 0, 0, 0))
    piece_spec = pl.BlockSpec((half, rows, width), mine)
    return pl.pallas_call(
        functools.partial(spectral_kernel, lat),
        grid_spec=pltpu.PrefetchScalarGridSpec(
            num_scalar_prefetch=1,
            grid=(2,),
            in_specs=[piece_spec] * lat + [filter_spec] * 2 + [table_spec(t) for t in tables],
            out_specs=[piece_spec] * lat,
            scratch_shapes=[pltpu.VMEM((half * height, 2 * lat * LANES), jnp.bfloat16)] * 2,
        ),
        out_shape=[jax.ShapeDtypeStruct((chunk, rows, width), jnp.float32)] * lat,
        compiler_params=params(56),
        name="filtered_pieces",
    )(place, *pieces, own, other, *[jnp.asarray(t) for t in tables])


def join_kernel(count, chunk, place_ref, coupling_ref, fields_ref, state_ref, *refs):
    pieces, out_ref = refs[:count], refs[-1]
    step = pl.program_id(0)
    part = state_ref.shape[0]
    first = (lax.rem(place_ref[0] + step, count) * CHUNKS + chunk) * part
    for j in range(count):

        @pl.when(step == j)
        def _(piece=pieces[j]):
            for c in range(part):
                forcing = coupling_ref[first + c, 0] * fields_ref[0]
                for s in range(1, fields_ref.shape[0]):
                    forcing = forcing + coupling_ref[first + c, s] * fields_ref[s]
                out_ref[c] = state_ref[c] + piece[c] + forcing


def joined(atmos_state, pieces, coupling, fields, place, chunk, earlier):
    lat = len(pieces)
    part, rows, width = pieces[0].shape

    def here(j, place):
        return (lax.rem(place[0] + j, lat) * CHUNKS + chunk, 0, 0)

    whole = [pl.BlockSpec(p.shape, lambda j, place: (0, 0, 0)) for p in pieces]
    in_specs = [
        pl.BlockSpec(memory_space=pltpu.SMEM),
        pl.BlockSpec(fields.shape, lambda j, place: (0, 0, 0)),
        pl.BlockSpec((part, rows, width), here),
        *whole,
    ]
    operands = [place, coupling, fields, atmos_state, *pieces]
    aliases = {}
    if earlier is not None:
        aliases = {len(operands): 0}
        in_specs.append(pl.BlockSpec(memory_space=pl.ANY))
        operands.append(earlier)
    return pl.pallas_call(
        functools.partial(join_kernel, lat, chunk),
        grid_spec=pltpu.PrefetchScalarGridSpec(
            num_scalar_prefetch=1,
            grid=(lat,),
            in_specs=in_specs,
            out_specs=pl.BlockSpec((part, rows, width), here),
        ),
        out_shape=jax.ShapeDtypeStruct(atmos_state.shape, jnp.float32),
        input_output_aliases=aliases,
        compiler_params=params(32),
        name="joined",
    )(*operands)


def dealt(pieces, lat):
    return [pieces[0]] + [
        lax.ppermute(pieces[j], "lat", [(i, (i + j) % lat) for i in range(lat)])
        for j in range(1, lat)
    ][::-1]


def dealt_filter(spectral_filter, place, lat, members):
    halves = []
    for chunk in range(CHUNKS):
        pieces = dealt(pack_filter(spectral_filter, place, lat, members, chunk), lat)
        halves.append(jnp.stack(pieces))
    return [
        (own, lax.ppermute(own, "members", [(i, (i + 1) % members) for i in range(members)]))
        for own in halves
    ]


def summed_over_columns(x):
    for axis in ("chan", "lon"):
        count = lax.axis_size(axis)
        total = x
        for shift in range(1, count):
            total = total + lax.ppermute(x, axis, [(i, (i + shift) % count) for i in range(count)])
        x = total
    return x


def depthwise(field, taps):
    height = field.shape[1] - 2
    width = field.shape[2] - 2
    result = jnp.zeros((field.shape[0], height, width), jnp.float32)
    for row_off in range(3):
        for col_off in range(3):
            result = (
                result
                + taps[:, 3 * row_off + col_off][:, None, None]
                * field[:, row_off : row_off + height, col_off : col_off + width]
            )
    return result


def ocean_mixer(values, gain, expand, reduce_w):
    channels, height, width = values.shape
    flat = values.reshape(channels, height * width)
    centre = jnp.mean(flat, axis=0)
    spread = jnp.mean(flat * flat, axis=0) - centre * centre
    normed = (flat - centre) * lax.rsqrt(spread + EPSILON) * gain[:, None]
    hidden = jax.nn.gelu(jnp.einsum("cd,cp->dp", expand, normed, precision=FINE))
    update = jnp.einsum("dc,dp->cp", reduce_w, hidden, precision=FINE)
    return update.reshape(channels, height, width)


def body(
    atmos_state,
    ocean_state,
    land_mask,
    spectral_filter,
    atmos_gain,
    flux_readout,
    surface_coupling,
    surface_readout,
    flux_coupling,
    atmos_row_source,
    atmos_row_weight,
    atmos_col_source,
    atmos_col_weight,
    ocean_row_source,
    ocean_row_weight,
    ocean_col_source,
    ocean_col_weight,
    depth_taps,
    block_gain,
    expand_weight,
    reduce_weight,
    layer_scale,
):
    channels, atm_rows, width_atm = atmos_state.shape
    ocean_channels, ocean_rows, ocean_cols = ocean_state.shape
    lat, members = lax.axis_size("lat"), lax.axis_size("members")
    lat_place = lax.axis_index("lat")
    place = jnp.stack([lat_place, lax.axis_index("members")]).astype(jnp.int32)
    deal = can_deal(
        channels, atm_rows, width_atm, spectral_filter.shape[2], spectral_filter.shape[3], lat, members
    )
    if deal:
        filters = dealt_filter(spectral_filter, place, lat, members)

    ocean_mask = land_mask.astype(jnp.float32)
    row_table = jnp.concatenate([ocean_row_source.astype(jnp.float32), ocean_row_weight], axis=1)
    col_table = jnp.concatenate([ocean_col_source.astype(jnp.float32), ocean_col_weight], axis=1)
    row_table = jnp.pad(row_table, ((0, 0), (0, ocean_cols - row_table.shape[1])))
    wide = jnp.concatenate([ocean_state, ocean_mask[None], row_table[None]], axis=0)
    wide = padded(wide, (("lat", 1),), 2)
    row_table = wide[-1, :, 0:4]
    col_table = jnp.pad(col_table.T, ((0, wide.shape[1] - 4), (0, 0)))
    wide = jnp.concatenate([wide[:-1], col_table[None]], axis=0)
    wide = padded(wide, ((COLUMN, 2),), 2)
    col_table = wide[-1, 0:4].T
    state_wide, mask_wide = wide[:ocean_channels], wide[ocean_channels]

    if deal:
        sums = channel_sums(atmos_state, flux_readout)
    else:
        partial_flux = jnp.einsum("fc,chw->fhw", flux_readout, atmos_state, precision=PRECISE)
        sums = jnp.concatenate(
            [
                partial_flux,
                jnp.sum(atmos_state, axis=0)[None],
                jnp.sum(atmos_state * atmos_state, axis=0)[None],
            ],
            axis=0,
        )
    sums = summed_over_columns(sums)
    flux, stats = sums[:-2], sums[-2:]

    surface_wide = jnp.einsum("sc,chw->shw", surface_readout, state_wide, precision=PRECISE)
    row_map = regrid_matrix(
        atmos_row_source, atmos_row_weight, lat_place * ocean_rows - 2, ocean_rows + 4, 0
    )
    col_map = regrid_matrix(
        atmos_col_source,
        atmos_col_weight,
        lax.axis_index(COLUMN) * ocean_cols - 2,
        ocean_cols + 4,
        ocean_cols * lax.axis_size(COLUMN),
    )
    atmos_piece = apply_maps(surface_wide, row_map, col_map)
    fields = lax.all_gather(atmos_piece, COLUMN, axis=2, tiled=True)

    if deal:
        kinds = [
            dealt(normed_pieces(atmos_state, stats, atmos_gain, place, lat, q), lat)
            for q in range(CHUNKS)
        ]
        kinds = [
            dealt(filtered_pieces(kinds[q], *filters[q], place), lat) for q in range(CHUNKS)
        ]
        atmos_next = None
        for q in range(CHUNKS):
            atmos_next = joined(
                atmos_state, kinds[q], surface_coupling, fields, place, q, atmos_next
            )
    else:
        centre = stats[0] / CA
        spread = stats[1] / CA - centre * centre
        normed = (atmos_state - centre) * lax.rsqrt(spread + EPSILON) * atmos_gain[:, None, None]
        filtered = global_filter(normed, spectral_filter)
        forcing = jnp.einsum("cs,shw->chw", surface_coupling, fields, precision=PRECISE)
        atmos_next = atmos_state + filtered + forcing

    before, after = flux_reach(atm_rows, ocean_rows)
    flux_wide = rows_around(flux, before, after)
    row_back = regrid_matrix(
        row_table[:, 0:2].astype(jnp.int32),
        row_table[:, 2:4],
        lat_place * atm_rows - before,
        atm_rows + before + after,
        0,
    )
    col_back = regrid_matrix(
        col_table[:, 0:2].astype(jnp.int32), col_table[:, 2:4], 0, width_atm, 0
    )
    flux_ocean = apply_maps(flux_wide, row_back, col_back)
    current = mask_wide * (
        state_wide + jnp.einsum("cf,fhw->chw", flux_coupling, flux_ocean, precision=PRECISE)
    )
    update = ocean_mixer(
        depthwise(current, depth_taps[0]), block_gain[0], expand_weight[0], reduce_weight[0]
    )
    widened = mask_wide[1:-1, 1:-1] * (
        current[:, 1:-1, 1:-1] + layer_scale[0][:, None, None] * update
    )
    update = ocean_mixer(
        depthwise(widened, depth_taps[1]), block_gain[1], expand_weight[1], reduce_weight[1]
    )
    current = ocean_mask * (widened[:, 1:-1, 1:-1] + layer_scale[1][:, None, None] * update)
    return (atmos_next, current)


def solution(mesh):
    return jax.shard_map(
        body,
        mesh=mesh,
        in_specs=(
            P(("members", "lon", "chan"), "lat", None),
            P("members", "lat", ("lon", "chan")),
            P("lat", ("lon", "chan")),
            P(None, ("lon", "chan"), "lat", None),
            P(("lon", "chan")),
            P(None, ("lon", "chan")),
            P(("lon", "chan"), None),
            P(),
            P(),
            P("lat", None),
            P("lat", None),
            P(("lon", "chan"), None),
            P(("lon", "chan"), None),
            P("lat", None),
            P("lat", None),
            P(("lon", "chan"), None),
            P(("lon", "chan"), None),
            P(),
            P(),
            P(),
            P(),
            P(),
        ),
        out_specs=(
            P(("members", "lon", "chan"), "lat", None),
            P("members", "lat", ("lon", "chan")),
        ),
        check_vma=False,
    )
```

```python
import functools
import math

import jax
import jax.numpy as jnp
import ml_dtypes
import numpy as np
from jax import lax
from jax.experimental import pallas as pl
from jax.experimental.pallas import tpu as pltpu
from jax.sharding import PartitionSpec as P

CA = 384


EPSILON = 1e-05
PRECISE = lax.Precision.HIGHEST
FINE = lax.Precision.HIGH
LANES = 128
CHUNKS = 2
COLUMN = ("lon", "chan")
REACH = 16
STREAMS = 4


def padded(x, sides, width):
    for axis, dim in sides:
        count, length = (lax.axis_size(axis), x.shape[dim])
        up = [(i, (i + 1) % count) for i in range(count)]
        down = [(j, i) for i, j in up]
        last = lax.slice_in_dim(x, length - width, length, axis=dim)
        leading = lax.slice_in_dim(x, 0, width, axis=dim)
        before = lax.ppermute(last, axis, up)
        after = lax.ppermute(leading, axis, down)
        x = jnp.concatenate([before, x, after], axis=dim)
    return x


def fourier_tables(length):
    places = jnp.arange(length, dtype=jnp.int32)
    angles = (
        2.0
        * math.pi
        / length
        * jnp.mod(places[:, None] * places[None, :], length).astype(jnp.float32)
    )
    return (jnp.cos(angles), jnp.sin(angles))


def regrid_matrix(source, weight, offset, span, period):
    shares = weight / jnp.sum(weight, axis=1, keepdims=True)
    relative = source - offset
    if period > 0:
        relative = jnp.mod(relative, period)
    columns = jnp.arange(span, dtype=jnp.int32)[None, :]
    return shares[:, 0:1] * (relative[:, 0:1] == columns).astype(jnp.float32) + shares[:, 1:2] * (
        relative[:, 1:2] == columns
    ).astype(jnp.float32)


def apply_maps(field, row_map, col_map):
    by_rows = jnp.einsum("jh,shw->sjw", row_map, field, precision=PRECISE)
    return jnp.einsum("sjw,kw->sjk", by_rows, col_map, precision=PRECISE)


def grid_rims(field):
    return padded(field, (("lat", 1), (("lon", "chan"), 2)), 2)


def along_last(field, table):
    return jnp.einsum("ckh,hm->ckm", field, table, precision=PRECISE)


def global_filter(normed, spectral_filter):
    width_len = normed.shape[2]
    height_len = spectral_filter.shape[3]
    cos_w, sin_w = fourier_tables(width_len)
    cos_h, sin_h = fourier_tables(height_len)
    real_w = jnp.einsum("chn,nk->ckh", normed, cos_w, precision=PRECISE)
    imag_w = -jnp.einsum("chn,nk->ckh", normed, sin_w, precision=PRECISE)
    real_w, imag_w = (
        lax.all_to_all(real_w, "lat", split_axis=1, concat_axis=2, tiled=True),
        lax.all_to_all(imag_w, "lat", split_axis=1, concat_axis=2, tiled=True),
    )
    real_s = along_last(real_w, cos_h) + along_last(imag_w, sin_h)
    imag_s = along_last(imag_w, cos_h) - along_last(real_w, sin_h)
    kern_real = spectral_filter[0]
    kern_imag = spectral_filter[1]
    real_f = kern_real * real_s - kern_imag * imag_s
    imag_f = kern_real * imag_s + kern_imag * real_s
    real_b = (along_last(real_f, cos_h) - along_last(imag_f, sin_h)) / height_len
    imag_b = (along_last(imag_f, cos_h) + along_last(real_f, sin_h)) / height_len
    real_b, imag_b = (
        lax.all_to_all(real_b, "lat", split_axis=2, concat_axis=1, tiled=True),
        lax.all_to_all(imag_b, "lat", split_axis=2, concat_axis=1, tiled=True),
    )
    back = jnp.einsum("ckh,kn->chn", real_b, cos_w, precision=PRECISE) - jnp.einsum(
        "ckh,kn->chn", imag_b, sin_w, precision=PRECISE
    )
    return back / width_len


def flux_reach(atm_rows, ocean_rows):
    first = (-2 * atm_rows) // ocean_rows - 1
    last = (atm_rows * (ocean_rows + 1)) // ocean_rows + 2
    return -first, max(last - atm_rows + 1, 0)


def rows_around(field, before, behind):
    count = lax.axis_size("lat")
    up = [(i, i + 1) for i in range(count - 1)]
    down = [(i + 1, i) for i in range(count - 1)]
    rows = field.shape[1]
    above = lax.ppermute(field[:, rows - before :], "lat", up)
    below = lax.ppermute(field[:, :behind], "lat", down)
    return jnp.concatenate([above, field, below], axis=1)


def params(mib):
    return pltpu.CompilerParams(vmem_limit_bytes=mib * 2**20)


def can_deal(channels, rows, width, freqs, height, lat, members):
    return (
        members == 2
        and channels % (lat * CHUNKS * members) == 0
        and channels % STREAMS == 0
        and rows % 8 == 0
        and rows * lat == height
        and width % LANES == 0
        and freqs * lat == width
        and freqs == 96
        and height % 32 == 0
    )


def split_table(table):
    high = table.astype(ml_dtypes.bfloat16)
    low = (table - high.astype(np.float64)).astype(ml_dtypes.bfloat16)
    return high, low


@functools.lru_cache(maxsize=None)
def dealt_tables(height, width, lat):
    freqs = width // lat
    angle = 2.0 * np.pi / height * (np.outer(np.arange(height), np.arange(height)) % height)
    cos_h, sin_h = np.cos(angle), np.sin(angle)
    rows_on = np.block([[cos_h, sin_h], [-sin_h, cos_h]])
    rows_back = np.block([[cos_h, -sin_h], [sin_h, cos_h]])
    cols_on = np.zeros((lat, width, 2, lat, LANES))
    for z in range(lat):
        for j in range(lat):
            k = (z + j) % lat * freqs + np.arange(freqs)
            turn = 2.0 * np.pi / width * (np.outer(np.arange(width), k) % width)
            cols_on[z, :, 0, j, :freqs] = np.cos(turn)
            cols_on[z, :, 1, j, :freqs] = -np.sin(turn)
    cols_on = cols_on.reshape(lat, width, 2 * lat * LANES)
    cols_back = np.swapaxes(cols_on, 1, 2) / (height * width)
    return [split_table(t) for t in (cols_on, rows_on, rows_back, cols_back)]


def pack_kernel(place_ref, filter_ref, out_ref):
    _, channels, freqs, rows = filter_ref.shape
    main, rest = rows * 3 // 4, rows // 4
    for part in range(2):
        for c in range(channels):
            turned = filter_ref[part, c].T
            out_ref[0, part, c, :, 0:freqs] = turned[0:main]
            for i in range(3):
                out_ref[0, part, c, i * rest : (i + 1) * rest, freqs:LANES] = turned[
                    main:, 32 * i : 32 * (i + 1)
                ]


def pack_filter(spectral_filter, place, lat, members, shift):
    _, channels, freqs, height = spectral_filter.shape
    half = channels // (lat * CHUNKS * members)

    def source(q, place):
        dest = lax.rem(place[0] + shift, lat)
        return (0, (dest * CHUNKS + q) * members + place[1], 0, 0)

    shape = (CHUNKS, 2, half, height * 3 // 4, LANES)
    return pl.pallas_call(
        pack_kernel,
        grid_spec=pltpu.PrefetchScalarGridSpec(
            num_scalar_prefetch=1,
            grid=(CHUNKS,),
            in_specs=[pl.BlockSpec((2, half, freqs, height), source)],
            out_specs=pl.BlockSpec((1, *shape[1:]), lambda q, place: (q, 0, 0, 0, 0)),
        ),
        out_shape=jax.ShapeDtypeStruct(shape, jnp.float32),
        compiler_params=params(60),
        cost_estimate=pl.CostEstimate(flops=1, bytes_accessed=1, transcendentals=0),
        name="pack_filter",
    )(place, spectral_filter)


def sums_kernel(readout_ref, *refs):
    parts, (flux_ref, stats_ref) = refs[:STREAMS], refs[STREAMS:]
    channels, tile, width = parts[0].shape
    fluxes = readout_ref.shape[0]
    totals = (jnp.zeros((tile, width), jnp.float32),) * (fluxes + 2)
    for i, part in enumerate(parts):

        def add(c, totals, i=i, part=part):
            value = part[c]
            new = [totals[f] + readout_ref[f, i * channels + c] * value for f in range(fluxes)]
            return (*new, totals[fluxes] + value, totals[fluxes + 1] + value * value)

        totals = lax.fori_loop(0, channels, add, totals, unroll=4)
    for i in range(fluxes):
        flux_ref[i] = totals[i]
    stats_ref[0] = totals[fluxes]
    stats_ref[1] = totals[fluxes + 1]


def channel_sums(atmos_state, flux_readout):
    channels, rows, width = atmos_state.shape
    counts = (flux_readout.shape[0], 2)
    return pl.pallas_call(
        sums_kernel,
        grid=(rows // 8,),
        in_specs=[pl.BlockSpec(memory_space=pltpu.SMEM)]
        + [
            pl.BlockSpec((channels // STREAMS, 8, width), lambda i, s=s: (s, i, 0))
            for s in range(STREAMS)
        ],
        out_specs=[pl.BlockSpec((n, 8, width), lambda i: (0, i, 0)) for n in counts],
        out_shape=[jax.ShapeDtypeStruct((n, rows, width), jnp.float32) for n in counts],
        compiler_params=params(60),
        cost_estimate=pl.CostEstimate(flops=1, bytes_accessed=1, transcendentals=0),
        name="channel_sums",
    )(flux_readout, *[atmos_state] * STREAMS)


def norm_kernel(count, chunk, place_ref, gain_ref, sums_ref, state_ref, *out_refs):
    step = pl.program_id(0)
    part = state_ref.shape[0]
    first = (lax.rem(place_ref[0] + step, count) * CHUNKS + chunk) * part
    centre = sums_ref[0] / CA
    spread = sums_ref[1] / CA - centre * centre
    scale = lax.rsqrt(spread + EPSILON)
    for j in range(count):

        @pl.when(step == j)
        def _(out=out_refs[j]):
            for c in range(part):
                out[c] = (state_ref[c] - centre) * scale * gain_ref[first + c]


def normed_pieces(atmos_state, sums, gain, place, lat, chunk):
    channels, rows, width = atmos_state.shape
    part = channels // (lat * CHUNKS)
    return pl.pallas_call(
        functools.partial(norm_kernel, lat, chunk),
        grid_spec=pltpu.PrefetchScalarGridSpec(
            num_scalar_prefetch=1,
            grid=(lat,),
            in_specs=[
                pl.BlockSpec(memory_space=pltpu.SMEM),
                pl.BlockSpec(sums.shape, lambda j, place: (0, 0, 0)),
                pl.BlockSpec(
                    (part, rows, width),
                    lambda j, place: (lax.rem(place[0] + j, lat) * CHUNKS + chunk, 0, 0),
                ),
            ],
            out_specs=[pl.BlockSpec((part, rows, width), lambda j, place: (0, 0, 0))] * lat,
        ),
        out_shape=[jax.ShapeDtypeStruct((part, rows, width), jnp.float32)] * lat,
        compiler_params=params(60),
        name="normed_pieces",
    )(place, gain, sums, atmos_state)


def split(value):
    high = value.astype(jnp.bfloat16)
    return high, (value - high.astype(jnp.float32)).astype(jnp.bfloat16)


def product(left, right):
    dot = functools.partial(jnp.dot, preferred_element_type=jnp.float32)
    return dot(left[0], right[0]) + (dot(left[0], right[1]) + dot(left[1], right[0]))


def unpacked(packed_ref, count, part, c):
    blocks = []
    lane = lax.broadcasted_iota(jnp.int32, (packed_ref.shape[3] // 3, LANES), 1)
    rest = packed_ref.shape[3] // 3
    for j in range(count):
        main = packed_ref[j, part, c]
        a, b, d = (
            pltpu.roll(main[i * rest : (i + 1) * rest], 32 * (i + 1), 1) for i in range(3)
        )
        tail = jnp.where(lane < 32, a, jnp.where(lane < 64, b, d))
        blocks.append(jnp.concatenate([main, tail], axis=0))
    return jnp.concatenate(blocks, axis=1)


def spectral_kernel(count, place_ref, *refs):
    pieces = refs[:count]
    own_ref, other_ref = refs[count : count + 2]
    tables = [(refs[count + 2 + 2 * i], refs[count + 3 + 2 * i]) for i in range(4)]
    outs = refs[count + 10 : 2 * count + 10]
    high_ref, low_ref = refs[2 * count + 10 :]
    part, rows, width = pieces[0].shape
    height = rows * count
    span = count * LANES
    cols_on, rows_on, rows_back, cols_back = tables
    cols_on = (cols_on[0][0], cols_on[1][0])
    cols_back = (cols_back[0][0], cols_back[1][0])
    rows_on = (rows_on[0][...], rows_on[1][...])
    rows_back = (rows_back[0][...], rows_back[1][...])

    def run(filter_ref):
        stacked = jnp.concatenate([p[...].reshape(part * rows, width) for p in pieces], axis=0)
        spectra = product(split(stacked), cols_on)
        for c in range(part):
            own = jnp.concatenate(
                [spectra[(j * part + c) * rows : (j * part + c + 1) * rows] for j in range(count)],
                axis=0,
            )
            both = jnp.concatenate([own[:, :span], own[:, span:]], axis=0)
            full = product(rows_on, split(both))
            real, imag = full[:height], full[height:]
            kern_real = unpacked(filter_ref, count, 0, c)
            kern_imag = unpacked(filter_ref, count, 1, c)
            both = jnp.concatenate(
                [kern_real * real - kern_imag * imag, kern_real * imag + kern_imag * real], axis=0
            )
            back = product(rows_back, split(both))
            high, low = split(back)
            at = slice(c * height, (c + 1) * height)
            high_ref[at, :span] = high[:height]
            high_ref[at, span:] = high[height:]
            low_ref[at, :span] = low[:height]
            low_ref[at, span:] = low[height:]
        result = product((high_ref[...], low_ref[...]), cols_back)
        result = result.reshape(part, height, width)
        for j in range(count):
            outs[j][...] = result[:, j * rows : (j + 1) * rows]

    @pl.when(pl.program_id(0) == 0)
    def _():
        run(own_ref)

    @pl.when(pl.program_id(0) == 1)
    def _():
        run(other_ref)


def filtered_pieces(pieces, own, other, place):
    lat = len(pieces)
    chunk, rows, width = pieces[0].shape
    half = chunk // 2
    height = rows * lat
    tables = [t for pair in dealt_tables(height, width, lat) for t in pair]

    def mine(i, place):
        return (lax.rem(i + place[1], 2), 0, 0)

    def table_spec(t):
        if t.ndim == 3:
            return pl.BlockSpec((1, *t.shape[1:]), lambda i, place: (place[0], 0, 0))
        return pl.BlockSpec(t.shape, lambda i, place: (0, 0))

    filter_spec = pl.BlockSpec(own.shape, lambda i, place: (0, 0, 0, 0, 0))
    piece_spec = pl.BlockSpec((half, rows, width), mine)
    return pl.pallas_call(
        functools.partial(spectral_kernel, lat),
        grid_spec=pltpu.PrefetchScalarGridSpec(
            num_scalar_prefetch=1,
            grid=(2,),
            in_specs=[piece_spec] * lat + [filter_spec] * 2 + [table_spec(t) for t in tables],
            out_specs=[piece_spec] * lat,
            scratch_shapes=[pltpu.VMEM((half * height, 2 * lat * LANES), jnp.bfloat16)] * 2,
        ),
        out_shape=[jax.ShapeDtypeStruct((chunk, rows, width), jnp.float32)] * lat,
        compiler_params=params(60),
        name="filtered_pieces",
    )(place, *pieces, own, other, *[jnp.asarray(t) for t in tables])


def forced_kernel(coupling_ref, fields_ref, state_ref, out_ref):
    fields = [fields_ref[s] for s in range(fields_ref.shape[0])]

    @pl.loop(0, state_ref.shape[0], unroll=4)
    def _(c):
        value = state_ref[c]
        for s, field in enumerate(fields):
            value = value + coupling_ref[c, s] * field
        out_ref[c] = value


def forced(atmos_state, coupling, fields):
    channels, rows, width = atmos_state.shape
    block = pl.BlockSpec((channels, 8, width), lambda i: (0, i, 0))
    return pl.pallas_call(
        forced_kernel,
        grid=(rows // 8,),
        in_specs=[
            pl.BlockSpec(memory_space=pltpu.SMEM),
            pl.BlockSpec((fields.shape[0], 8, width), lambda i: (0, i, 0)),
            block,
        ],
        out_specs=block,
        out_shape=jax.ShapeDtypeStruct(atmos_state.shape, jnp.float32),
        compiler_params=params(60),
        name="forced",
    )(coupling, fields, atmos_state)


def join_kernel(count, chunk, place_ref, state_ref, *refs):
    pieces = refs[:count]
    out_ref, held, added, in_sems, piece_sems, out_sems = refs[count:]
    part = held.shape[1]
    starts = [(lax.rem(place_ref[0] + j, count) * CHUNKS + chunk) * part for j in range(count)]
    incoming, others, outgoing = [], [], []
    for j in range(count):
        here = pl.ds(starts[j], part)
        incoming.append(pltpu.make_async_copy(state_ref.at[here], held.at[j], in_sems.at[j]))
        others.append(pltpu.make_async_copy(pieces[j], added.at[j], piece_sems.at[j]))
        outgoing.append(pltpu.make_async_copy(held.at[j], out_ref.at[here], out_sems.at[j]))
    for copy in incoming + others:
        copy.start()
    for j in range(count):
        incoming[j].wait()
        others[j].wait()
        held[j] = held[j] + added[j]
        outgoing[j].start()
    for copy in outgoing:
        copy.wait()


def joined(state, pieces, place, chunk):
    lat = len(pieces)
    part, rows, width = pieces[0].shape
    hbm = pl.BlockSpec(memory_space=pl.ANY)
    return pl.pallas_call(
        functools.partial(join_kernel, lat, chunk),
        in_specs=[pl.BlockSpec(memory_space=pltpu.SMEM)] + [hbm] * (lat + 1),
        out_specs=hbm,
        out_shape=jax.ShapeDtypeStruct(state.shape, jnp.float32),
        scratch_shapes=[pltpu.VMEM((lat, part, rows, width), jnp.float32)] * 2
        + [pltpu.SemaphoreType.DMA((lat,))] * 3,
        input_output_aliases={1: 0},
        compiler_params=params(60),
        cost_estimate=pl.CostEstimate(flops=1, bytes_accessed=1, transcendentals=0),
        name="joined",
    )(place, state, *pieces)


def sent(piece, shift):
    lat = lax.axis_size("lat")
    return lax.ppermute(piece, "lat", [(i, (i + shift) % lat) for i in range(lat)])


def dealt(pieces):
    lat = len(pieces)
    return [pieces[0]] + [sent(pieces[lat - j], lat - j) for j in range(1, lat)]


def after(value, earlier):
    return lax.optimization_barrier((value, earlier))[0]


def swapped_filter(pieces):
    members = lax.axis_size("members")
    halves = [jnp.stack([p[q] for p in pieces]) for q in range(CHUNKS)]
    return [
        (own, lax.ppermute(own, "members", [(i, (i + 1) % members) for i in range(members)]))
        for own in halves
    ]


def summed_over_columns(x):
    for axis in ("chan", "lon"):
        count = lax.axis_size(axis)
        total = x
        for shift in range(1, count):
            total = total + lax.ppermute(x, axis, [(i, (i + shift) % count) for i in range(count)])
        x = total
    return x


def can_tile(ocean_channels, ocean_rows, ocean_cols, atm_rows, groups):
    before, behind = flux_reach(atm_rows, ocean_rows)
    return (
        ocean_cols == LANES
        and ocean_channels % 8 == 0
        and ocean_rows == 4
        and atm_rows % 8 == 0
        and max(before, behind) <= REACH <= atm_rows
        and groups > 1
    )


def exact(left, right):
    return jnp.dot(left, right, precision=PRECISE, preferred_element_type=jnp.float32)


def iota(shape, dim):
    return lax.broadcasted_iota(jnp.int32, shape, dim)


def table_row(source, weight, row):
    lane = iota((1, LANES), 1)
    values = [
        source[0:1, row : row + 1].astype(jnp.float32),
        source[1:2, row : row + 1].astype(jnp.float32),
        weight[0:1, row : row + 1],
        weight[1:2, row : row + 1],
    ]
    out = jnp.zeros((1, LANES), jnp.float32)
    for i, value in enumerate(values):
        out = jnp.where(lane == i, value, out)
    return out


def stacked_rows(rows):
    at = iota((8, rows[0].shape[1]), 0)
    tile = jnp.zeros((8, rows[0].shape[1]), jnp.float32)
    for i, row in enumerate(rows):
        tile = jnp.where(at == i, row, tile)
    return tile


def edges_kernel(flux_ref, state_ref, mask_ref, source_ref, weight_ref, *out_refs):
    fluxes, atm_rows, width = flux_ref.shape
    channels, rows, _ = state_ref.shape
    span = channels + 8
    source, weight = source_ref[...], weight_ref[...]
    for out, first, atm_first in (
        (out_refs[0], rows - 2, atm_rows - REACH),
        (out_refs[1], 0, 0),
    ):
        for i in range(2):
            row = first + i
            out[i * span : i * span + channels] = state_ref[:, row, :]
            out[i * span + channels : (i + 1) * span] = stacked_rows(
                [mask_ref[row : row + 1, :].astype(jnp.float32), table_row(source, weight, row)]
            )
        at = 2 * span
        for f in range(fluxes):
            for lanes in range(0, width, LANES):
                out[at : at + REACH] = flux_ref[f, atm_first : atm_first + REACH, lanes : lanes + LANES]
                at += REACH


def lat_edges(flux, ocean_state, land_mask, source, weight):
    fluxes, _, width = flux.shape
    channels = ocean_state.shape[0]
    shape = (2 * (channels + 8) + fluxes * width // LANES * REACH, LANES)
    return pl.pallas_call(
        edges_kernel,
        out_shape=[jax.ShapeDtypeStruct(shape, jnp.float32)] * 2,
        compiler_params=params(60),
        name="lat_edges",
    )(flux, ocean_state, land_mask, source, weight)


def rows_kernel(place_ref, up_ref, down_ref, flux_ref, source_ref, weight_ref, out_ref):
    fluxes, atm_rows, width = flux_ref.shape
    rows = source_ref.shape[1]
    span = (up_ref.shape[0] - fluxes * width // LANES * REACH) // 2
    source, weight = source_ref[...], weight_ref[...]
    at = span - 7
    table = stacked_rows(
        [up_ref[at : at + 1], up_ref[span + at : span + at + 1]]
        + [table_row(source, weight, r) for r in range(rows)]
        + [down_ref[at : at + 1], down_ref[span + at : span + at + 1]]
    )
    first = place_ref[0] * atm_rows - REACH
    reach = atm_rows + 2 * REACH
    spot = (iota((8, reach), 1) + first).astype(jnp.float32)
    total = table[:, 2:3] + table[:, 3:4]
    total = jnp.where(total > 0.0, total, 1.0)
    picks = jnp.where(spot == table[:, 0:1], table[:, 2:3] / total, 0.0) + jnp.where(
        spot == table[:, 1:2], table[:, 3:4] / total, 0.0
    )
    tiles = width // LANES
    for f in range(fluxes):
        parts = []
        for ref in (up_ref, down_ref):
            at = 2 * span + f * tiles * REACH
            parts.append(
                jnp.concatenate(
                    [ref[at + i * REACH : at + (i + 1) * REACH] for i in range(tiles)], axis=1
                )
            )
        field = jnp.concatenate([parts[0], flux_ref[f], parts[1]], axis=0)
        out_ref[f * 8 : (f + 1) * 8] = exact(picks, field)


def flux_rows(place, up, down, flux, source, weight):
    fluxes, atm_rows, width = flux.shape
    vmem = pl.BlockSpec(memory_space=pltpu.VMEM)
    return pl.pallas_call(
        rows_kernel,
        in_specs=[pl.BlockSpec(memory_space=pltpu.SMEM)] + [vmem] * 5,
        out_specs=vmem,
        out_shape=jax.ShapeDtypeStruct((8 * fluxes, width), jnp.float32),
        compiler_params=params(60),
        name="flux_rows",
    )(place, up, down, flux, source, weight)


def row_tile(r, rows, span, up_ref, down_ref, state_ref):
    channels = span - 8
    if r < 2:
        return up_ref[r * span : r * span + channels]
    if r < rows + 2:
        return state_ref[:, r - 2, :]
    return down_ref[(r - rows - 2) * span : (r - rows - 2) * span + channels]


def mask_row(r, rows, span, up_ref, down_ref, mask_ref):
    channels = span - 8
    if r < 2:
        return up_ref[r * span + channels : r * span + channels + 1]
    if r < rows + 2:
        return mask_ref[r - 2 : r - 1, :].astype(jnp.float32)
    at = (r - rows - 2) * span + channels
    return down_ref[at : at + 1]


def sides_kernel(up_ref, down_ref, state_ref, mask_ref, source_ref, weight_ref, first_ref, last_ref):
    channels, rows, _ = state_ref.shape
    span = channels + 8
    lane = iota((1, LANES), 1)
    first = jnp.zeros((channels, LANES), jnp.float32)
    last = jnp.zeros((channels, LANES), jnp.float32)
    first_mask = jnp.zeros((1, LANES), jnp.float32)
    last_mask = jnp.zeros((1, LANES), jnp.float32)
    for r in range(rows + 4):
        tile = row_tile(r, rows, span, up_ref, down_ref, state_ref)
        mask = mask_row(r, rows, span, up_ref, down_ref, mask_ref)
        here = (lane >= 2 * r) & (lane < 2 * r + 2)
        first = jnp.where(here, pltpu.roll(tile, 2 * r, 1), first)
        last = jnp.where(here, pltpu.roll(tile, 2 * r + 2, 1), last)
        first_mask = jnp.where(here, turned(mask, 2 * r), first_mask)
        last_mask = jnp.where(here, turned(mask, 2 * r + 2), last_mask)
    first_ref[0:channels] = first
    last_ref[0:channels] = last
    source = source_ref[...].astype(jnp.float32)
    weight = weight_ref[...]
    table = [source[0:1], source[1:2], weight[0:1], weight[1:2]]
    first_ref[channels:span] = stacked_rows([first_mask] + table)
    last_ref[channels:span] = stacked_rows([last_mask] + [turned(t, 2) for t in table])


def turned(row, shift):
    return pltpu.roll(jnp.broadcast_to(row, (8, row.shape[1])), shift, 1)[0:1]


def lon_sides(up, down, ocean_state, land_mask, source, weight):
    shape = (ocean_state.shape[0] + 8, LANES)
    return pl.pallas_call(
        sides_kernel,
        out_shape=[jax.ShapeDtypeStruct(shape, jnp.float32)] * 2,
        compiler_params=params(60),
        name="lon_sides",
    )(up, down, ocean_state, land_mask, source, weight)


def surface_kernel(
    place_ref,
    period,
    up_ref,
    down_ref,
    left_ref,
    right_ref,
    state_ref,
    readout_ref,
    row_ref,
    source_ref,
    weight_ref,
    out_ref,
    lines_ref,
):
    channels, rows, cols = state_ref.shape
    span = channels + 8
    fields, atm_rows, width = out_ref.shape
    atm_cols = source_ref.shape[1]
    readout = readout_ref[...]
    lines_ref[...] = jnp.zeros_like(lines_ref)
    for r in range(rows + 4):
        tile = row_tile(r, rows, span, up_ref, down_ref, state_ref)
        lines_ref[r * 8 : r * 8 + fields] = exact(readout, tile)
    lines = lines_ref[...]
    sides = [exact(readout, ref[0:channels]) for ref in (left_ref, right_ref)]

    table = row_ref[...]
    total = table[:, 2:3] + table[:, 3:4]
    shares = (table[:, 2:3] / total, table[:, 3:4] / total)
    start = (place_ref[0] * rows - 2).astype(jnp.float32)
    sources = (table[:, 0:1] - start, table[:, 1:2] - start)

    def row_picks(row):
        row = row.astype(jnp.float32)
        return jnp.where(row == sources[0], shares[0], 0.0) + jnp.where(row == sources[1], shares[1], 0.0)

    source, weight = source_ref[...], weight_ref[...]
    total = weight[0:1] + weight[1:2]
    relative = source - (place_ref[2] * cols - 2)
    relative = jnp.where(relative < 0, relative + period, relative)
    relative = jnp.where(relative >= period, relative - period, relative)

    def col_picks(col):
        return jnp.where(col == relative[0:1], weight[0:1] / total, 0.0) + jnp.where(
            col == relative[1:2], weight[1:2] / total, 0.0
        )

    at = iota((LANES, atm_cols), 0)
    main = col_picks(at + 2)
    side = [col_picks((at & 1)), col_picks(cols + 2 + (at & 1))]
    spread = iota((atm_cols, width), 1) - place_ref[2] * atm_cols == iota((atm_cols, width), 0)
    spread = spread.astype(jnp.float32)
    lane = iota((atm_rows, 8 * (rows + 4)), 1)
    side_lane = iota((atm_rows, LANES), 1)
    side_rows = row_picks(side_lane >> 1)
    for s in range(fields):
        picks = jnp.where((lane & 7) == s, row_picks(lane >> 3), 0.0)
        piece = exact(exact(picks, lines), main)
        for i in range(2):
            piece = piece + exact(side_rows * sides[i][s : s + 1], side[i])
        out_ref[s] = exact(piece, spread)


def surface_piece(place, up, down, left, right, ocean_state, readout, row_table, source, weight, period, width):
    rows = ocean_state.shape[1]
    vmem = pl.BlockSpec(memory_space=pltpu.VMEM)
    shape = (readout.shape[0], row_table.shape[0], width)
    return pl.pallas_call(
        lambda place_ref, *refs: surface_kernel(place_ref, period, *refs),
        in_specs=[pl.BlockSpec(memory_space=pltpu.SMEM)] + [vmem] * 9,
        out_specs=vmem,
        out_shape=jax.ShapeDtypeStruct(shape, jnp.float32),
        scratch_shapes=[pltpu.VMEM((8 * (rows + 4), LANES), jnp.float32)],
        compiler_params=params(60),
        name="surface_piece",
    )(place, up, down, left, right, ocean_state, readout, row_table, source, weight)


def ocean_kernel(
    sums_ref,
    up_ref,
    down_ref,
    left_ref,
    right_ref,
    state_ref,
    mask_ref,
    coupling_ref,
    source_ref,
    weight_ref,
    columns_ref,
    expand_ref,
    reduce_ref,
    out_ref,
):
    channels, rows, cols = state_ref.shape
    span = channels + 8
    fluxes = coupling_ref.shape[1] // 8
    width = sums_ref.shape[1]
    wide = rows + 4
    lane = iota((1, LANES), 1)
    half = LANES // 2
    is_left = lane < half
    lines = sums_ref[0 : 8 * fluxes]
    coupling = coupling_ref[...]
    spot = iota((width, LANES), 0).astype(jnp.float32)

    def col_lines(s0, s1, w0, w1):
        total = w0 + w1
        total = jnp.where(total > 0.0, total, 1.0)
        return exact(
            lines, jnp.where(spot == s0, w0 / total, 0.0) + jnp.where(spot == s1, w1 / total, 0.0)
        )

    source, weight = source_ref[...].astype(jnp.float32), weight_ref[...]
    main_lines = col_lines(source[0:1], source[1:2], weight[0:1], weight[1:2])
    of_row = iota((channels, 8 * fluxes), 1) & 7

    current, masks = [], []
    for r in range(wide):
        forcing = exact(jnp.where(of_row == r, coupling, 0.0), main_lines)
        mask = mask_row(r, rows, span, up_ref, down_ref, mask_ref)
        masks.append(mask)
        current.append(mask * (row_tile(r, rows, span, up_ref, down_ref, state_ref) + forcing))

    def side_current(ref):
        table = ref[channels + 1 : channels + 5]
        side_lines = col_lines(table[0:1], table[1:2], table[2:3], table[3:4])
        spread = jnp.zeros((8 * fluxes, LANES), jnp.float32)
        at = iota((8 * fluxes, LANES), 0) & 7
        for r in range(wide):
            here = (at == r) & (lane >= 2 * r) & (lane < 2 * r + 2)
            spread = jnp.where(here, pltpu.roll(side_lines, 2 * r, 1), spread)
        mask = ref[channels : channels + 1]
        return mask, mask * (ref[0:channels] + exact(coupling, spread))

    left_mask, left = side_current(left_ref)
    right_mask, right = side_current(right_ref)
    inner = [jnp.zeros((channels, LANES), jnp.float32)] * 2
    for r in range(wide):
        inner[0] = jnp.where(lane == 2 * r, pltpu.roll(current[r], 2 * r, 1), inner[0])
        inner[1] = jnp.where(
            lane == half + 2 * r, pltpu.roll(current[r], (half + 2 * r + 1) % LANES, 1), inner[1]
        )
    beside = [
        jnp.where(is_left, left, inner[1]),
        jnp.where(is_left, pltpu.roll(left, LANES - 1, 1), pltpu.roll(right, half, 1)),
        jnp.where(is_left, inner[0], pltpu.roll(right, half - 1, 1)),
    ]
    beside_mask = jnp.where(is_left, turned(left_mask, LANES - 1), turned(right_mask, half))

    def shifted(tile, before, behind):
        return [
            jnp.where(lane == 0, before, pltpu.roll(tile, 1, 1)),
            tile,
            jnp.where(lane == cols - 1, behind, pltpu.roll(tile, cols - 1, 1)),
        ]

    def mixer(block, conv):
        base = block * 11
        gain = columns_ref[:, base + 9 : base + 10]
        scale = columns_ref[:, base + 10 : base + 11]
        points = jnp.concatenate(conv, axis=1)
        centre = jnp.mean(points, axis=0, keepdims=True)
        spread = jnp.mean(points * points, axis=0, keepdims=True) - centre * centre
        normed = (points - centre) * lax.rsqrt(spread + EPSILON) * gain
        hidden = jax.nn.gelu(product(split(expand_ref[block].T), split(normed)))
        update = scale * product(split(reduce_ref[block]), split(hidden))
        return [update[:, i * LANES : (i + 1) * LANES] for i in range(len(conv))]

    def tap(block, i, j):
        at = block * 11 + 3 * i + j
        return columns_ref[:, at : at + 1]

    views = [
        shifted(
            current[r],
            pltpu.roll(left, (LANES - 2 * r - 1) % LANES, 1),
            pltpu.roll(right, (cols - 1 - 2 * r) % LANES, 1),
        )
        for r in range(wide)
    ]
    conv = []
    for r in range(1, wide - 1):
        conv.append(sum(tap(0, i, j) * views[r + i - 1][j] for i in range(3) for j in range(3)))
    side = jnp.zeros((channels, LANES), jnp.float32)
    for i in range(3):
        line = sum(tap(0, i, j) * beside[j] for j in range(3))
        side = side + (line if i == 1 else pltpu.roll(line, (2 - 2 * i) % LANES, 1))
    update = mixer(0, conv + [side])
    widened = [masks[r] * (current[r] + update[r - 1]) for r in range(1, wide - 1)]
    rim = beside_mask * (beside[1] + update[-1])

    views = [
        shifted(
            widened[r - 1],
            pltpu.roll(rim, (LANES - 2 * r) % LANES, 1),
            pltpu.roll(rim, (cols - 1 - half - 2 * r) % LANES, 1),
        )
        for r in range(1, wide - 1)
    ]
    conv = []
    for r in range(rows):
        conv.append(sum(tap(1, i, j) * views[r + i][j] for i in range(3) for j in range(3)))
    update = mixer(1, conv)
    for r in range(rows):
        out_ref[:, r, :] = masks[r + 2] * (widened[r + 1] + update[r])


def ocean_step(sums, up, down, left, right, ocean_state, land_mask, coupling, source, weight, columns, expand, reduce_w):
    return pl.pallas_call(
        ocean_kernel,
        out_shape=jax.ShapeDtypeStruct(ocean_state.shape, jnp.float32),
        compiler_params=params(60),
        name="ocean_step",
    )(
        sums,
        up,
        down,
        left,
        right,
        ocean_state,
        land_mask,
        jnp.repeat(coupling, 8, axis=1),
        source,
        weight,
        columns,
        expand,
        jnp.swapaxes(reduce_w, 1, 2),
    )


def depthwise(field, taps):
    height = field.shape[1] - 2
    width = field.shape[2] - 2
    result = jnp.zeros((field.shape[0], height, width), jnp.float32)
    for row_off in range(3):
        for col_off in range(3):
            result = (
                result
                + taps[:, 3 * row_off + col_off][:, None, None]
                * field[:, row_off : row_off + height, col_off : col_off + width]
            )
    return result


def ocean_mixer(values, gain, expand, reduce_w):
    channels, height, width = values.shape
    flat = values.reshape(channels, height * width)
    centre = jnp.mean(flat, axis=0)
    spread = jnp.mean(flat * flat, axis=0) - centre * centre
    normed = (flat - centre) * lax.rsqrt(spread + EPSILON) * gain[:, None]
    hidden = jax.nn.gelu(jnp.einsum("cd,cp->dp", expand, normed, precision=FINE))
    update = jnp.einsum("dc,dp->cp", reduce_w, hidden, precision=FINE)
    return update.reshape(channels, height, width)


def fast_step(
    atmos_state,
    ocean_state,
    land_mask,
    spectral_filter,
    atmos_gain,
    flux_readout,
    surface_coupling,
    surface_readout,
    flux_coupling,
    atmos_row_source,
    atmos_row_weight,
    atmos_col_source,
    atmos_col_weight,
    ocean_row_source,
    ocean_row_weight,
    ocean_col_source,
    ocean_col_weight,
    depth_taps,
    block_gain,
    expand_weight,
    reduce_weight,
    layer_scale,
):
    channels, atm_rows, width = atmos_state.shape
    lat, groups = lax.axis_size("lat"), lax.axis_size(COLUMN)
    places = [lax.axis_index("lat"), lax.axis_index("members"), lax.axis_index(COLUMN)]
    place = jnp.stack(places).astype(jnp.int32)
    members = lax.axis_size("members")
    far = lat // 2
    row_source, row_weight = ocean_row_source.T, ocean_row_weight.T
    col_source, col_weight = ocean_col_source.T, ocean_col_weight.T

    flux, stats = channel_sums(atmos_state, flux_readout)
    up, down = lat_edges(flux, ocean_state, land_mask, row_source, row_weight)
    packed, came, token = {}, {}, up
    for shift in (far, *(j for j in range(1, lat) if j != far), 0):
        packed[shift] = pack_filter(spectral_filter, after(place, token), lat, members, shift)
        token = packed[shift]
    up = lax.ppermute(up, "lat", [(i, i + 1) for i in range(lat - 1)])
    down = lax.ppermute(down, "lat", [(i + 1, i) for i in range(lat - 1)])

    came[0] = packed[0]
    for shift in range(1, lat):
        came[lat - shift] = sent(packed[shift], shift)
    stats = summed_over_columns(stats)
    fresh = [
        normed_pieces(atmos_state, stats, atmos_gain, place, lat, q) for q in range(CHUNKS)
    ]
    up, down = lax.optimization_barrier((up, down, fresh[0][0], fresh[-1][0]))[:2]
    sums = summed_over_columns(flux_rows(place, up, down, flux, row_source, row_weight))
    first, last = lon_sides(up, down, ocean_state, land_mask, col_source, col_weight)
    left = lax.ppermute(last, COLUMN, [(i, (i + 1) % groups) for i in range(groups)])
    right = lax.ppermute(first, COLUMN, [(i, (i - 1) % groups) for i in range(groups)])
    piece = surface_piece(
        place,
        up,
        down,
        left,
        right,
        ocean_state,
        surface_readout,
        jnp.concatenate([atmos_row_source.astype(jnp.float32), atmos_row_weight], axis=1),
        atmos_col_source.T,
        atmos_col_weight.T,
        ocean_state.shape[2] * groups,
        width,
    )
    atmos_next = forced(atmos_state, surface_coupling, summed_over_columns(piece))
    columns = jnp.concatenate([depth_taps, block_gain[..., None], layer_scale[..., None]], axis=2)
    ocean_next = ocean_step(
        sums,
        up,
        down,
        left,
        right,
        ocean_state,
        land_mask,
        flux_coupling,
        col_source,
        col_weight,
        jnp.concatenate([columns[0], columns[1]], axis=1),
        expand_weight,
        reduce_weight,
    )

    done = (atmos_next, ocean_next, fresh[0][0], fresh[-1][0])
    pieces, token = [], (came[lat - far], done)
    for q in range(CHUNKS):
        pieces.append(dealt(lax.optimization_barrier((*fresh[q], token))[:lat]))
        token = pieces[q][far]
    came = lax.optimization_barrier((*(came[j] for j in range(lat)), done))[:lat]
    filters = swapped_filter(came)
    pieces = [dealt(filtered_pieces(pieces[q], *filters[q], place)) for q in range(CHUNKS)]
    for q in range(CHUNKS):
        atmos_next = joined(atmos_next, pieces[q], place, q)
    return (atmos_next, ocean_next)


def general_step(
    atmos_state,
    ocean_state,
    land_mask,
    spectral_filter,
    atmos_gain,
    flux_readout,
    surface_coupling,
    surface_readout,
    flux_coupling,
    atmos_row_source,
    atmos_row_weight,
    atmos_col_source,
    atmos_col_weight,
    ocean_row_source,
    ocean_row_weight,
    ocean_col_source,
    ocean_col_weight,
    depth_taps,
    block_gain,
    expand_weight,
    reduce_weight,
    layer_scale,
):
    channels, atm_rows, width_atm = atmos_state.shape
    ocean_channels, ocean_rows, ocean_cols = ocean_state.shape
    lat_place = lax.axis_index("lat")

    ocean_mask = land_mask.astype(jnp.float32)
    row_table = jnp.concatenate([ocean_row_source.astype(jnp.float32), ocean_row_weight], axis=1)
    col_table = jnp.concatenate([ocean_col_source.astype(jnp.float32), ocean_col_weight], axis=1)
    row_table = jnp.pad(row_table, ((0, 0), (0, ocean_cols - row_table.shape[1])))
    wide = jnp.concatenate([ocean_state, ocean_mask[None], row_table[None]], axis=0)
    wide = padded(wide, (("lat", 1),), 2)
    row_table = wide[-1, :, 0:4]
    col_table = jnp.pad(col_table.T, ((0, wide.shape[1] - 4), (0, 0)))
    wide = jnp.concatenate([wide[:-1], col_table[None]], axis=0)
    wide = padded(wide, ((COLUMN, 2),), 2)
    col_table = wide[-1, 0:4].T
    state_wide, mask_wide = wide[:ocean_channels], wide[ocean_channels]

    partial_flux = jnp.einsum("fc,chw->fhw", flux_readout, atmos_state, precision=PRECISE)
    sums = jnp.concatenate(
        [
            partial_flux,
            jnp.sum(atmos_state, axis=0)[None],
            jnp.sum(atmos_state * atmos_state, axis=0)[None],
        ],
        axis=0,
    )
    sums = summed_over_columns(sums)
    flux, stats = sums[:-2], sums[-2:]

    surface_wide = jnp.einsum("sc,chw->shw", surface_readout, state_wide, precision=PRECISE)
    row_map = regrid_matrix(
        atmos_row_source, atmos_row_weight, lat_place * ocean_rows - 2, ocean_rows + 4, 0
    )
    col_map = regrid_matrix(
        atmos_col_source,
        atmos_col_weight,
        lax.axis_index(COLUMN) * ocean_cols - 2,
        ocean_cols + 4,
        ocean_cols * lax.axis_size(COLUMN),
    )
    atmos_piece = apply_maps(surface_wide, row_map, col_map)
    fields = lax.all_gather(atmos_piece, COLUMN, axis=2, tiled=True)

    centre = stats[0] / CA
    spread = stats[1] / CA - centre * centre
    normed = (atmos_state - centre) * lax.rsqrt(spread + EPSILON) * atmos_gain[:, None, None]
    filtered = global_filter(normed, spectral_filter)
    forcing = jnp.einsum("cs,shw->chw", surface_coupling, fields, precision=PRECISE)
    atmos_next = atmos_state + filtered + forcing

    before, behind = flux_reach(atm_rows, ocean_rows)
    flux_wide = rows_around(flux, before, behind)
    row_back = regrid_matrix(
        row_table[:, 0:2].astype(jnp.int32),
        row_table[:, 2:4],
        lat_place * atm_rows - before,
        atm_rows + before + behind,
        0,
    )
    col_back = regrid_matrix(
        col_table[:, 0:2].astype(jnp.int32), col_table[:, 2:4], 0, width_atm, 0
    )
    flux_ocean = apply_maps(flux_wide, row_back, col_back)
    current = mask_wide * (
        state_wide + jnp.einsum("cf,fhw->chw", flux_coupling, flux_ocean, precision=PRECISE)
    )
    update = ocean_mixer(
        depthwise(current, depth_taps[0]), block_gain[0], expand_weight[0], reduce_weight[0]
    )
    widened = mask_wide[1:-1, 1:-1] * (
        current[:, 1:-1, 1:-1] + layer_scale[0][:, None, None] * update
    )
    update = ocean_mixer(
        depthwise(widened, depth_taps[1]), block_gain[1], expand_weight[1], reduce_weight[1]
    )
    current = ocean_mask * (widened[:, 1:-1, 1:-1] + layer_scale[1][:, None, None] * update)
    return (atmos_next, current)


def body(*arrays):
    atmos_state, ocean_state, _, spectral_filter = arrays[:4]
    channels, atm_rows, width = atmos_state.shape
    lat, members, groups = (lax.axis_size(a) for a in ("lat", "members", COLUMN))
    freqs, height = spectral_filter.shape[2:]
    fast = can_deal(channels, atm_rows, width, freqs, height, lat, members) and can_tile(
        *ocean_state.shape, atm_rows, groups
    )
    return fast_step(*arrays) if fast else general_step(*arrays)


def solution(mesh):
    return jax.shard_map(
        body,
        mesh=mesh,
        in_specs=(
            P(("members", "lon", "chan"), "lat", None),
            P("members", "lat", ("lon", "chan")),
            P("lat", ("lon", "chan")),
            P(None, ("lon", "chan"), "lat", None),
            P(("lon", "chan")),
            P(None, ("lon", "chan")),
            P(("lon", "chan"), None),
            P(),
            P(),
            P("lat", None),
            P("lat", None),
            P(("lon", "chan"), None),
            P(("lon", "chan"), None),
            P("lat", None),
            P("lat", None),
            P(("lon", "chan"), None),
            P(("lon", "chan"), None),
            P(),
            P(),
            P(),
            P(),
            P(),
        ),
        out_specs=(
            P(("members", "lon", "chan"), "lat", None),
            P("members", "lat", ("lon", "chan")),
        ),
        check_vma=False,
    )
```

```python
import functools
import math

import jax
import jax.numpy as jnp
import ml_dtypes
import numpy as np
from jax import lax
from jax.experimental import pallas as pl
from jax.experimental.pallas import tpu as pltpu
from jax.sharding import PartitionSpec as P

CA = 384


EPSILON = 1e-05
PRECISE = lax.Precision.HIGHEST
FINE = lax.Precision.HIGH
LANES = 128
CHUNKS = 2
COLUMN = ("lon", "chan")
REACH = 16
STREAMS = 4


def padded(x, sides, width):
    for axis, dim in sides:
        count, length = (lax.axis_size(axis), x.shape[dim])
        up = [(i, (i + 1) % count) for i in range(count)]
        down = [(j, i) for i, j in up]
        last = lax.slice_in_dim(x, length - width, length, axis=dim)
        leading = lax.slice_in_dim(x, 0, width, axis=dim)
        before = lax.ppermute(last, axis, up)
        after = lax.ppermute(leading, axis, down)
        x = jnp.concatenate([before, x, after], axis=dim)
    return x


def fourier_tables(length):
    places = jnp.arange(length, dtype=jnp.int32)
    angles = (
        2.0
        * math.pi
        / length
        * jnp.mod(places[:, None] * places[None, :], length).astype(jnp.float32)
    )
    return (jnp.cos(angles), jnp.sin(angles))


def regrid_matrix(source, weight, offset, span, period):
    shares = weight / jnp.sum(weight, axis=1, keepdims=True)
    relative = source - offset
    if period > 0:
        relative = jnp.mod(relative, period)
    columns = jnp.arange(span, dtype=jnp.int32)[None, :]
    return shares[:, 0:1] * (relative[:, 0:1] == columns).astype(jnp.float32) + shares[:, 1:2] * (
        relative[:, 1:2] == columns
    ).astype(jnp.float32)


def apply_maps(field, row_map, col_map):
    by_rows = jnp.einsum("jh,shw->sjw", row_map, field, precision=PRECISE)
    return jnp.einsum("sjw,kw->sjk", by_rows, col_map, precision=PRECISE)


def grid_rims(field):
    return padded(field, (("lat", 1), (("lon", "chan"), 2)), 2)


def along_last(field, table):
    return jnp.einsum("ckh,hm->ckm", field, table, precision=PRECISE)


def global_filter(normed, spectral_filter):
    width_len = normed.shape[2]
    height_len = spectral_filter.shape[3]
    cos_w, sin_w = fourier_tables(width_len)
    cos_h, sin_h = fourier_tables(height_len)
    real_w = jnp.einsum("chn,nk->ckh", normed, cos_w, precision=PRECISE)
    imag_w = -jnp.einsum("chn,nk->ckh", normed, sin_w, precision=PRECISE)
    real_w, imag_w = (
        lax.all_to_all(real_w, "lat", split_axis=1, concat_axis=2, tiled=True),
        lax.all_to_all(imag_w, "lat", split_axis=1, concat_axis=2, tiled=True),
    )
    real_s = along_last(real_w, cos_h) + along_last(imag_w, sin_h)
    imag_s = along_last(imag_w, cos_h) - along_last(real_w, sin_h)
    kern_real = spectral_filter[0]
    kern_imag = spectral_filter[1]
    real_f = kern_real * real_s - kern_imag * imag_s
    imag_f = kern_real * imag_s + kern_imag * real_s
    real_b = (along_last(real_f, cos_h) - along_last(imag_f, sin_h)) / height_len
    imag_b = (along_last(imag_f, cos_h) + along_last(real_f, sin_h)) / height_len
    real_b, imag_b = (
        lax.all_to_all(real_b, "lat", split_axis=2, concat_axis=1, tiled=True),
        lax.all_to_all(imag_b, "lat", split_axis=2, concat_axis=1, tiled=True),
    )
    back = jnp.einsum("ckh,kn->chn", real_b, cos_w, precision=PRECISE) - jnp.einsum(
        "ckh,kn->chn", imag_b, sin_w, precision=PRECISE
    )
    return back / width_len


def flux_reach(atm_rows, ocean_rows):
    first = (-2 * atm_rows) // ocean_rows - 1
    last = (atm_rows * (ocean_rows + 1)) // ocean_rows + 2
    return -first, max(last - atm_rows + 1, 0)


def rows_around(field, before, behind):
    count = lax.axis_size("lat")
    up = [(i, i + 1) for i in range(count - 1)]
    down = [(i + 1, i) for i in range(count - 1)]
    rows = field.shape[1]
    above = lax.ppermute(field[:, rows - before :], "lat", up)
    below = lax.ppermute(field[:, :behind], "lat", down)
    return jnp.concatenate([above, field, below], axis=1)


def params(mib):
    return pltpu.CompilerParams(vmem_limit_bytes=mib * 2**20)


def can_deal(channels, rows, width, freqs, height, lat, members):
    return (
        members == 2
        and lat == 4
        and channels % (lat * CHUNKS * members) == 0
        and channels % STREAMS == 0
        and rows % 8 == 0
        and rows * lat == height
        and width % LANES == 0
        and freqs * lat == width
        and freqs == 96
        and height % 32 == 0
    )


def split_table(table):
    high = table.astype(ml_dtypes.bfloat16)
    low = (table - high.astype(np.float64)).astype(ml_dtypes.bfloat16)
    return high, low


@functools.lru_cache(maxsize=None)
def dealt_tables(height, width, lat):
    freqs = width // lat
    angle = 2.0 * np.pi / height * (np.outer(np.arange(height), np.arange(height)) % height)
    cos_h, sin_h = np.cos(angle), np.sin(angle)
    rows_on = np.block([[cos_h, sin_h], [-sin_h, cos_h]])
    rows_back = np.block([[cos_h, -sin_h], [sin_h, cos_h]])
    cols_on = np.zeros((lat, width, 2, lat, LANES))
    for z in range(lat):
        for j in range(lat):
            k = (z + j) % lat * freqs + np.arange(freqs)
            turn = 2.0 * np.pi / width * (np.outer(np.arange(width), k) % width)
            cols_on[z, :, 0, j, :freqs] = np.cos(turn)
            cols_on[z, :, 1, j, :freqs] = -np.sin(turn)
    cols_on = cols_on.reshape(lat, width, 2 * lat * LANES)
    cols_back = np.swapaxes(cols_on, 1, 2) / (height * width)
    return [split_table(t) for t in (cols_on, rows_on, rows_back, cols_back)]


def pack_kernel(place_ref, filter_ref, out_ref):
    _, channels, freqs, rows = filter_ref.shape
    main, rest = rows * 3 // 4, rows // 4
    for part in range(2):
        for c in range(channels):
            turned = filter_ref[part, c].T
            out_ref[0, part, c, :, 0:freqs] = turned[0:main]
            for i in range(3):
                out_ref[0, part, c, i * rest : (i + 1) * rest, freqs:LANES] = turned[
                    main:, 32 * i : 32 * (i + 1)
                ]


def pack_filter(spectral_filter, place, lat, members, shift):
    _, channels, freqs, height = spectral_filter.shape
    half = channels // (lat * CHUNKS * members)

    def source(q, place):
        dest = place[0] ^ shift
        return (0, (dest * CHUNKS + q) * members + place[1], 0, 0)

    shape = (CHUNKS, 2, half, height * 3 // 4, LANES)
    return pl.pallas_call(
        pack_kernel,
        grid_spec=pltpu.PrefetchScalarGridSpec(
            num_scalar_prefetch=1,
            grid=(CHUNKS,),
            in_specs=[pl.BlockSpec((2, half, freqs, height), source)],
            out_specs=pl.BlockSpec((1, *shape[1:]), lambda q, place: (q, 0, 0, 0, 0)),
        ),
        out_shape=jax.ShapeDtypeStruct(shape, jnp.float32),
        compiler_params=params(60),
        cost_estimate=pl.CostEstimate(flops=1, bytes_accessed=1, transcendentals=0),
        name="pack_filter",
    )(place, spectral_filter)


def sums_kernel(readout_ref, *refs):
    parts, (flux_ref, stats_ref) = refs[:STREAMS], refs[STREAMS:]
    channels, tile, width = parts[0].shape
    fluxes = readout_ref.shape[0]
    totals = (jnp.zeros((tile, width), jnp.float32),) * (fluxes + 2)
    for i, part in enumerate(parts):

        def add(c, totals, i=i, part=part):
            value = part[c]
            new = [totals[f] + readout_ref[f, i * channels + c] * value for f in range(fluxes)]
            return (*new, totals[fluxes] + value, totals[fluxes + 1] + value * value)

        totals = lax.fori_loop(0, channels, add, totals, unroll=4)
    for i in range(fluxes):
        flux_ref[i] = totals[i]
    stats_ref[0] = totals[fluxes]
    stats_ref[1] = totals[fluxes + 1]


def channel_sums(atmos_state, flux_readout):
    channels, rows, width = atmos_state.shape
    counts = (flux_readout.shape[0], 2)
    return pl.pallas_call(
        sums_kernel,
        grid=(rows // 8,),
        in_specs=[pl.BlockSpec(memory_space=pltpu.SMEM)]
        + [
            pl.BlockSpec((channels // STREAMS, 8, width), lambda i, s=s: (s, i, 0))
            for s in range(STREAMS)
        ],
        out_specs=[pl.BlockSpec((n, 8, width), lambda i: (0, i, 0)) for n in counts],
        out_shape=[jax.ShapeDtypeStruct((n, rows, width), jnp.float32) for n in counts],
        compiler_params=params(60),
        cost_estimate=pl.CostEstimate(flops=1, bytes_accessed=1, transcendentals=0),
        name="channel_sums",
    )(flux_readout, *[atmos_state] * STREAMS)


def norm_kernel(count, chunk, place_ref, gain_ref, sums_ref, state_ref, *out_refs):
    step = pl.program_id(0)
    part = state_ref.shape[0]
    first = ((place_ref[0] ^ step) * CHUNKS + chunk) * part
    centre = sums_ref[0] / CA
    spread = sums_ref[1] / CA - centre * centre
    scale = lax.rsqrt(spread + EPSILON)
    for j in range(count):

        @pl.when(step == j)
        def _(out=out_refs[j]):
            for c in range(part):
                out[c] = (state_ref[c] - centre) * scale * gain_ref[first + c]


def normed_pieces(atmos_state, sums, gain, place, lat, chunk):
    channels, rows, width = atmos_state.shape
    part = channels // (lat * CHUNKS)
    return pl.pallas_call(
        functools.partial(norm_kernel, lat, chunk),
        grid_spec=pltpu.PrefetchScalarGridSpec(
            num_scalar_prefetch=1,
            grid=(lat,),
            in_specs=[
                pl.BlockSpec(memory_space=pltpu.SMEM),
                pl.BlockSpec(sums.shape, lambda j, place: (0, 0, 0)),
                pl.BlockSpec(
                    (part, rows, width),
                    lambda j, place: ((place[0] ^ j) * CHUNKS + chunk, 0, 0),
                ),
            ],
            out_specs=[pl.BlockSpec((part, rows, width), lambda j, place: (0, 0, 0))] * lat,
        ),
        out_shape=[jax.ShapeDtypeStruct((part, rows, width), jnp.float32)] * lat,
        compiler_params=params(60),
        name="normed_pieces",
    )(place, gain, sums, atmos_state)


def split(value):
    high = value.astype(jnp.bfloat16)
    return high, (value - high.astype(jnp.float32)).astype(jnp.bfloat16)


def product(left, right):
    dot = functools.partial(jnp.dot, preferred_element_type=jnp.float32)
    return dot(left[0], right[0]) + (dot(left[0], right[1]) + dot(left[1], right[0]))


def unpacked(packed_ref, order, part, c):
    blocks = []
    lane = lax.broadcasted_iota(jnp.int32, (packed_ref.shape[3] // 3, LANES), 1)
    rest = packed_ref.shape[3] // 3
    for j in order:
        main = packed_ref[j, part, c]
        a, b, d = (
            pltpu.roll(main[i * rest : (i + 1) * rest], 32 * (i + 1), 1) for i in range(3)
        )
        tail = jnp.where(lane < 32, a, jnp.where(lane < 64, b, d))
        blocks.append(jnp.concatenate([main, tail], axis=0))
    return jnp.concatenate(blocks, axis=1)


def spectral_kernel(count, place_ref, *refs):
    pieces = refs[:count]
    own_ref, other_ref = refs[count : count + 2]
    tables = [(refs[count + 2 + 2 * i], refs[count + 3 + 2 * i]) for i in range(4)]
    outs = refs[count + 10 : 2 * count + 10]
    high_ref, low_ref = refs[2 * count + 10 :]
    part, rows, width = pieces[0].shape
    height = rows * count
    span = count * LANES
    cols_on, rows_on, rows_back, cols_back = tables
    cols_on = (cols_on[0][0], cols_on[1][0])
    cols_back = (cols_back[0][0], cols_back[1][0])
    rows_on = (rows_on[0][...], rows_on[1][...])
    rows_back = (rows_back[0][...], rows_back[1][...])

    odd = lax.rem(place_ref[0], 2) == 1
    order = [0, jnp.where(odd, 3, 1), 2, jnp.where(odd, 1, 3)]

    def ordered(values):
        return [
            values[0],
            jnp.where(odd, values[3], values[1]),
            values[2],
            jnp.where(odd, values[1], values[3]),
        ]

    def run(filter_ref):
        lines = ordered([p[...].reshape(part * rows, width) for p in pieces])
        stacked = jnp.concatenate(lines, axis=0)
        spectra = product(split(stacked), cols_on)
        for c in range(part):
            own = jnp.concatenate(
                [spectra[(j * part + c) * rows : (j * part + c + 1) * rows] for j in range(count)],
                axis=0,
            )
            both = jnp.concatenate([own[:, :span], own[:, span:]], axis=0)
            full = product(rows_on, split(both))
            real, imag = full[:height], full[height:]
            kern_real = unpacked(filter_ref, order, 0, c)
            kern_imag = unpacked(filter_ref, order, 1, c)
            both = jnp.concatenate(
                [kern_real * real - kern_imag * imag, kern_real * imag + kern_imag * real], axis=0
            )
            back = product(rows_back, split(both))
            high, low = split(back)
            at = slice(c * height, (c + 1) * height)
            high_ref[at, :span] = high[:height]
            high_ref[at, span:] = high[height:]
            low_ref[at, :span] = low[:height]
            low_ref[at, span:] = low[height:]
        result = product((high_ref[...], low_ref[...]), cols_back)
        result = result.reshape(part, height, width)
        parts = ordered([result[:, j * rows : (j + 1) * rows] for j in range(count)])
        for out, value in zip(outs, parts):
            out[...] = value

    @pl.when(pl.program_id(0) == 0)
    def _():
        run(own_ref)

    @pl.when(pl.program_id(0) == 1)
    def _():
        run(other_ref)


def filtered_pieces(pieces, own, other, place):
    lat = len(pieces)
    chunk, rows, width = pieces[0].shape
    half = chunk // 2
    height = rows * lat
    tables = [t for pair in dealt_tables(height, width, lat) for t in pair]

    def mine(i, place):
        return (lax.rem(i + place[1], 2), 0, 0)

    def table_spec(t):
        if t.ndim == 3:
            return pl.BlockSpec((1, *t.shape[1:]), lambda i, place: (place[0], 0, 0))
        return pl.BlockSpec(t.shape, lambda i, place: (0, 0))

    filter_spec = pl.BlockSpec(own.shape, lambda i, place: (0, 0, 0, 0, 0))
    piece_spec = pl.BlockSpec((half, rows, width), mine)
    return pl.pallas_call(
        functools.partial(spectral_kernel, lat),
        grid_spec=pltpu.PrefetchScalarGridSpec(
            num_scalar_prefetch=1,
            grid=(2,),
            in_specs=[piece_spec] * lat + [filter_spec] * 2 + [table_spec(t) for t in tables],
            out_specs=[piece_spec] * lat,
            scratch_shapes=[pltpu.VMEM((half * height, 2 * lat * LANES), jnp.bfloat16)] * 2,
        ),
        out_shape=[jax.ShapeDtypeStruct((chunk, rows, width), jnp.float32)] * lat,
        compiler_params=params(60),
        name="filtered_pieces",
    )(place, *pieces, own, other, *[jnp.asarray(t) for t in tables])


def forced_kernel(coupling_ref, fields_ref, state_ref, out_ref):
    fields = [fields_ref[s] for s in range(fields_ref.shape[0])]

    @pl.loop(0, state_ref.shape[0], unroll=4)
    def _(c):
        value = state_ref[c]
        for s, field in enumerate(fields):
            value = value + coupling_ref[c, s] * field
        out_ref[c] = value


def forced(atmos_state, coupling, fields):
    channels, rows, width = atmos_state.shape
    block = pl.BlockSpec((channels, 8, width), lambda i: (0, i, 0))
    return pl.pallas_call(
        forced_kernel,
        grid=(rows // 8,),
        in_specs=[
            pl.BlockSpec(memory_space=pltpu.SMEM),
            pl.BlockSpec((fields.shape[0], 8, width), lambda i: (0, i, 0)),
            block,
        ],
        out_specs=block,
        out_shape=jax.ShapeDtypeStruct(atmos_state.shape, jnp.float32),
        compiler_params=params(60),
        name="forced",
    )(coupling, fields, atmos_state)


def join_kernel(count, chunk, place_ref, state_ref, *refs):
    pieces = refs[:count]
    out_ref, held, added, in_sems, piece_sems, out_sems = refs[count:]
    part = held.shape[1]
    starts = [((place_ref[0] ^ j) * CHUNKS + chunk) * part for j in range(count)]
    incoming, others, outgoing = [], [], []
    for j in range(count):
        here = pl.ds(starts[j], part)
        incoming.append(pltpu.make_async_copy(state_ref.at[here], held.at[j], in_sems.at[j]))
        others.append(pltpu.make_async_copy(pieces[j], added.at[j], piece_sems.at[j]))
        outgoing.append(pltpu.make_async_copy(held.at[j], out_ref.at[here], out_sems.at[j]))
    for copy in incoming + others:
        copy.start()
    for j in range(count):
        incoming[j].wait()
        others[j].wait()
        held[j] = held[j] + added[j]
        outgoing[j].start()
    for copy in outgoing:
        copy.wait()


def joined(state, pieces, place, chunk):
    lat = len(pieces)
    part, rows, width = pieces[0].shape
    hbm = pl.BlockSpec(memory_space=pl.ANY)
    return pl.pallas_call(
        functools.partial(join_kernel, lat, chunk),
        in_specs=[pl.BlockSpec(memory_space=pltpu.SMEM)] + [hbm] * (lat + 1),
        out_specs=hbm,
        out_shape=jax.ShapeDtypeStruct(state.shape, jnp.float32),
        scratch_shapes=[pltpu.VMEM((lat, part, rows, width), jnp.float32)] * 2
        + [pltpu.SemaphoreType.DMA((lat,))] * 3,
        input_output_aliases={1: 0},
        compiler_params=params(60),
        cost_estimate=pl.CostEstimate(flops=1, bytes_accessed=1, transcendentals=0),
        name="joined",
    )(place, state, *pieces)


def sent(piece, step):
    lat = lax.axis_size("lat")
    return lax.ppermute(piece, "lat", [(i, i ^ step) for i in range(lat)])


def dealt(pieces):
    return [pieces[0]] + [sent(pieces[j], j) for j in range(1, len(pieces))]


def after(value, earlier):
    return lax.optimization_barrier((value, earlier))[0]


def swapped_filter(pieces):
    members = lax.axis_size("members")
    halves = [jnp.stack([p[q] for p in pieces]) for q in range(CHUNKS)]
    return [
        (own, lax.ppermute(own, "members", [(i, (i + 1) % members) for i in range(members)]))
        for own in halves
    ]


def summed_over_columns(x):
    for axis in ("chan", "lon"):
        count = lax.axis_size(axis)
        total = x
        for shift in range(1, count):
            total = total + lax.ppermute(x, axis, [(i, (i + shift) % count) for i in range(count)])
        x = total
    return x


def can_tile(ocean_channels, ocean_rows, ocean_cols, atm_rows, groups):
    before, behind = flux_reach(atm_rows, ocean_rows)
    return (
        ocean_cols == LANES
        and ocean_channels % 8 == 0
        and ocean_rows == 4
        and atm_rows % 8 == 0
        and max(before, behind) <= REACH <= atm_rows
        and groups > 1
    )


def exact(left, right):
    return jnp.dot(left, right, precision=PRECISE, preferred_element_type=jnp.float32)


def iota(shape, dim):
    return lax.broadcasted_iota(jnp.int32, shape, dim)


def table_row(source, weight, row):
    lane = iota((1, LANES), 1)
    values = [
        source[0:1, row : row + 1].astype(jnp.float32),
        source[1:2, row : row + 1].astype(jnp.float32),
        weight[0:1, row : row + 1],
        weight[1:2, row : row + 1],
    ]
    out = jnp.zeros((1, LANES), jnp.float32)
    for i, value in enumerate(values):
        out = jnp.where(lane == i, value, out)
    return out


def stacked_rows(rows):
    at = iota((8, rows[0].shape[1]), 0)
    tile = jnp.zeros((8, rows[0].shape[1]), jnp.float32)
    for i, row in enumerate(rows):
        tile = jnp.where(at == i, row, tile)
    return tile


def edges_kernel(flux_ref, state_ref, mask_ref, source_ref, weight_ref, *out_refs):
    fluxes, atm_rows, width = flux_ref.shape
    channels, rows, _ = state_ref.shape
    span = channels + 8
    source, weight = source_ref[...], weight_ref[...]
    for out, first, atm_first in (
        (out_refs[0], rows - 2, atm_rows - REACH),
        (out_refs[1], 0, 0),
    ):
        for i in range(2):
            row = first + i
            out[i * span : i * span + channels] = state_ref[:, row, :]
            out[i * span + channels : (i + 1) * span] = stacked_rows(
                [mask_ref[row : row + 1, :].astype(jnp.float32), table_row(source, weight, row)]
            )
        at = 2 * span
        for f in range(fluxes):
            for lanes in range(0, width, LANES):
                out[at : at + REACH] = flux_ref[f, atm_first : atm_first + REACH, lanes : lanes + LANES]
                at += REACH


def lat_edges(flux, ocean_state, land_mask, source, weight):
    fluxes, _, width = flux.shape
    channels = ocean_state.shape[0]
    shape = (2 * (channels + 8) + fluxes * width // LANES * REACH, LANES)
    return pl.pallas_call(
        edges_kernel,
        out_shape=[jax.ShapeDtypeStruct(shape, jnp.float32)] * 2,
        compiler_params=params(60),
        name="lat_edges",
    )(flux, ocean_state, land_mask, source, weight)


def rows_kernel(place_ref, up_ref, down_ref, flux_ref, source_ref, weight_ref, out_ref):
    fluxes, atm_rows, width = flux_ref.shape
    rows = source_ref.shape[1]
    span = (up_ref.shape[0] - fluxes * width // LANES * REACH) // 2
    source, weight = source_ref[...], weight_ref[...]
    at = span - 7
    table = stacked_rows(
        [up_ref[at : at + 1], up_ref[span + at : span + at + 1]]
        + [table_row(source, weight, r) for r in range(rows)]
        + [down_ref[at : at + 1], down_ref[span + at : span + at + 1]]
    )
    first = place_ref[0] * atm_rows - REACH
    reach = atm_rows + 2 * REACH
    spot = (iota((8, reach), 1) + first).astype(jnp.float32)
    total = table[:, 2:3] + table[:, 3:4]
    total = jnp.where(total > 0.0, total, 1.0)
    picks = jnp.where(spot == table[:, 0:1], table[:, 2:3] / total, 0.0) + jnp.where(
        spot == table[:, 1:2], table[:, 3:4] / total, 0.0
    )
    tiles = width // LANES
    for f in range(fluxes):
        parts = []
        for ref in (up_ref, down_ref):
            at = 2 * span + f * tiles * REACH
            parts.append(
                jnp.concatenate(
                    [ref[at + i * REACH : at + (i + 1) * REACH] for i in range(tiles)], axis=1
                )
            )
        field = jnp.concatenate([parts[0], flux_ref[f], parts[1]], axis=0)
        out_ref[f * 8 : (f + 1) * 8] = exact(picks, field)


def flux_rows(place, up, down, flux, source, weight):
    fluxes, atm_rows, width = flux.shape
    vmem = pl.BlockSpec(memory_space=pltpu.VMEM)
    return pl.pallas_call(
        rows_kernel,
        in_specs=[pl.BlockSpec(memory_space=pltpu.SMEM)] + [vmem] * 5,
        out_specs=vmem,
        out_shape=jax.ShapeDtypeStruct((8 * fluxes, width), jnp.float32),
        compiler_params=params(60),
        name="flux_rows",
    )(place, up, down, flux, source, weight)


def row_tile(r, rows, span, up_ref, down_ref, state_ref):
    channels = span - 8
    if r < 2:
        return up_ref[r * span : r * span + channels]
    if r < rows + 2:
        return state_ref[:, r - 2, :]
    return down_ref[(r - rows - 2) * span : (r - rows - 2) * span + channels]


def mask_row(r, rows, span, up_ref, down_ref, mask_ref):
    channels = span - 8
    if r < 2:
        return up_ref[r * span + channels : r * span + channels + 1]
    if r < rows + 2:
        return mask_ref[r - 2 : r - 1, :].astype(jnp.float32)
    at = (r - rows - 2) * span + channels
    return down_ref[at : at + 1]


def sides_kernel(up_ref, down_ref, state_ref, mask_ref, source_ref, weight_ref, first_ref, last_ref):
    channels, rows, _ = state_ref.shape
    span = channels + 8
    lane = iota((1, LANES), 1)
    first = jnp.zeros((channels, LANES), jnp.float32)
    last = jnp.zeros((channels, LANES), jnp.float32)
    first_mask = jnp.zeros((1, LANES), jnp.float32)
    last_mask = jnp.zeros((1, LANES), jnp.float32)
    for r in range(rows + 4):
        tile = row_tile(r, rows, span, up_ref, down_ref, state_ref)
        mask = mask_row(r, rows, span, up_ref, down_ref, mask_ref)
        here = (lane >= 2 * r) & (lane < 2 * r + 2)
        first = jnp.where(here, pltpu.roll(tile, 2 * r, 1), first)
        last = jnp.where(here, pltpu.roll(tile, 2 * r + 2, 1), last)
        first_mask = jnp.where(here, turned(mask, 2 * r), first_mask)
        last_mask = jnp.where(here, turned(mask, 2 * r + 2), last_mask)
    first_ref[0:channels] = first
    last_ref[0:channels] = last
    source = source_ref[...].astype(jnp.float32)
    weight = weight_ref[...]
    table = [source[0:1], source[1:2], weight[0:1], weight[1:2]]
    first_ref[channels:span] = stacked_rows([first_mask] + table)
    last_ref[channels:span] = stacked_rows([last_mask] + [turned(t, 2) for t in table])


def turned(row, shift):
    return pltpu.roll(jnp.broadcast_to(row, (8, row.shape[1])), shift, 1)[0:1]


def lon_sides(up, down, ocean_state, land_mask, source, weight):
    shape = (ocean_state.shape[0] + 8, LANES)
    return pl.pallas_call(
        sides_kernel,
        out_shape=[jax.ShapeDtypeStruct(shape, jnp.float32)] * 2,
        compiler_params=params(60),
        name="lon_sides",
    )(up, down, ocean_state, land_mask, source, weight)


def surface_kernel(
    place_ref,
    period,
    up_ref,
    down_ref,
    left_ref,
    right_ref,
    state_ref,
    readout_ref,
    row_ref,
    source_ref,
    weight_ref,
    out_ref,
    lines_ref,
):
    channels, rows, cols = state_ref.shape
    span = channels + 8
    fields, atm_rows, width = out_ref.shape
    atm_cols = source_ref.shape[1]
    readout = readout_ref[...]
    lines_ref[...] = jnp.zeros_like(lines_ref)
    for r in range(rows + 4):
        tile = row_tile(r, rows, span, up_ref, down_ref, state_ref)
        lines_ref[r * 8 : r * 8 + fields] = exact(readout, tile)
    lines = lines_ref[...]
    sides = [exact(readout, ref[0:channels]) for ref in (left_ref, right_ref)]

    table = row_ref[...]
    total = table[:, 2:3] + table[:, 3:4]
    shares = (table[:, 2:3] / total, table[:, 3:4] / total)
    start = (place_ref[0] * rows - 2).astype(jnp.float32)
    sources = (table[:, 0:1] - start, table[:, 1:2] - start)

    def row_picks(row):
        row = row.astype(jnp.float32)
        return jnp.where(row == sources[0], shares[0], 0.0) + jnp.where(row == sources[1], shares[1], 0.0)

    source, weight = source_ref[...], weight_ref[...]
    total = weight[0:1] + weight[1:2]
    relative = source - (place_ref[2] * cols - 2)
    relative = jnp.where(relative < 0, relative + period, relative)
    relative = jnp.where(relative >= period, relative - period, relative)

    def col_picks(col):
        return jnp.where(col == relative[0:1], weight[0:1] / total, 0.0) + jnp.where(
            col == relative[1:2], weight[1:2] / total, 0.0
        )

    at = iota((LANES, atm_cols), 0)
    main = col_picks(at + 2)
    side = [col_picks((at & 1)), col_picks(cols + 2 + (at & 1))]
    spread = iota((atm_cols, width), 1) - place_ref[2] * atm_cols == iota((atm_cols, width), 0)
    spread = spread.astype(jnp.float32)
    lane = iota((atm_rows, 8 * (rows + 4)), 1)
    side_lane = iota((atm_rows, LANES), 1)
    side_rows = row_picks(side_lane >> 1)
    for s in range(fields):
        picks = jnp.where((lane & 7) == s, row_picks(lane >> 3), 0.0)
        piece = exact(exact(picks, lines), main)
        for i in range(2):
            piece = piece + exact(side_rows * sides[i][s : s + 1], side[i])
        out_ref[s] = exact(piece, spread)


def surface_piece(place, up, down, left, right, ocean_state, readout, row_table, source, weight, period, width):
    rows = ocean_state.shape[1]
    vmem = pl.BlockSpec(memory_space=pltpu.VMEM)
    shape = (readout.shape[0], row_table.shape[0], width)
    return pl.pallas_call(
        lambda place_ref, *refs: surface_kernel(place_ref, period, *refs),
        in_specs=[pl.BlockSpec(memory_space=pltpu.SMEM)] + [vmem] * 9,
        out_specs=vmem,
        out_shape=jax.ShapeDtypeStruct(shape, jnp.float32),
        scratch_shapes=[pltpu.VMEM((8 * (rows + 4), LANES), jnp.float32)],
        compiler_params=params(60),
        name="surface_piece",
    )(place, up, down, left, right, ocean_state, readout, row_table, source, weight)


def ocean_kernel(
    sums_ref,
    up_ref,
    down_ref,
    left_ref,
    right_ref,
    state_ref,
    mask_ref,
    coupling_ref,
    source_ref,
    weight_ref,
    columns_ref,
    expand_ref,
    reduce_ref,
    out_ref,
):
    channels, rows, cols = state_ref.shape
    span = channels + 8
    fluxes = coupling_ref.shape[1] // 8
    width = sums_ref.shape[1]
    wide = rows + 4
    lane = iota((1, LANES), 1)
    half = LANES // 2
    is_left = lane < half
    lines = sums_ref[0 : 8 * fluxes]
    coupling = coupling_ref[...]
    spot = iota((width, LANES), 0).astype(jnp.float32)

    def col_lines(s0, s1, w0, w1):
        total = w0 + w1
        total = jnp.where(total > 0.0, total, 1.0)
        return exact(
            lines, jnp.where(spot == s0, w0 / total, 0.0) + jnp.where(spot == s1, w1 / total, 0.0)
        )

    source, weight = source_ref[...].astype(jnp.float32), weight_ref[...]
    main_lines = col_lines(source[0:1], source[1:2], weight[0:1], weight[1:2])
    of_row = iota((channels, 8 * fluxes), 1) & 7

    current, masks = [], []
    for r in range(wide):
        forcing = exact(jnp.where(of_row == r, coupling, 0.0), main_lines)
        mask = mask_row(r, rows, span, up_ref, down_ref, mask_ref)
        masks.append(mask)
        current.append(mask * (row_tile(r, rows, span, up_ref, down_ref, state_ref) + forcing))

    def side_current(ref):
        table = ref[channels + 1 : channels + 5]
        side_lines = col_lines(table[0:1], table[1:2], table[2:3], table[3:4])
        spread = jnp.zeros((8 * fluxes, LANES), jnp.float32)
        at = iota((8 * fluxes, LANES), 0) & 7
        for r in range(wide):
            here = (at == r) & (lane >= 2 * r) & (lane < 2 * r + 2)
            spread = jnp.where(here, pltpu.roll(side_lines, 2 * r, 1), spread)
        mask = ref[channels : channels + 1]
        return mask, mask * (ref[0:channels] + exact(coupling, spread))

    left_mask, left = side_current(left_ref)
    right_mask, right = side_current(right_ref)
    inner = [jnp.zeros((channels, LANES), jnp.float32)] * 2
    for r in range(wide):
        inner[0] = jnp.where(lane == 2 * r, pltpu.roll(current[r], 2 * r, 1), inner[0])
        inner[1] = jnp.where(
            lane == half + 2 * r, pltpu.roll(current[r], (half + 2 * r + 1) % LANES, 1), inner[1]
        )
    beside = [
        jnp.where(is_left, left, inner[1]),
        jnp.where(is_left, pltpu.roll(left, LANES - 1, 1), pltpu.roll(right, half, 1)),
        jnp.where(is_left, inner[0], pltpu.roll(right, half - 1, 1)),
    ]
    beside_mask = jnp.where(is_left, turned(left_mask, LANES - 1), turned(right_mask, half))

    def shifted(tile, before, behind):
        return [
            jnp.where(lane == 0, before, pltpu.roll(tile, 1, 1)),
            tile,
            jnp.where(lane == cols - 1, behind, pltpu.roll(tile, cols - 1, 1)),
        ]

    def mixer(block, conv):
        base = block * 11
        gain = columns_ref[:, base + 9 : base + 10]
        scale = columns_ref[:, base + 10 : base + 11]
        points = jnp.concatenate(conv, axis=1)
        centre = jnp.mean(points, axis=0, keepdims=True)
        spread = jnp.mean(points * points, axis=0, keepdims=True) - centre * centre
        normed = (points - centre) * lax.rsqrt(spread + EPSILON) * gain
        hidden = jax.nn.gelu(product(split(expand_ref[block].T), split(normed)))
        update = scale * product(split(reduce_ref[block]), split(hidden))
        return [update[:, i * LANES : (i + 1) * LANES] for i in range(len(conv))]

    def tap(block, i, j):
        at = block * 11 + 3 * i + j
        return columns_ref[:, at : at + 1]

    views = [
        shifted(
            current[r],
            pltpu.roll(left, (LANES - 2 * r - 1) % LANES, 1),
            pltpu.roll(right, (cols - 1 - 2 * r) % LANES, 1),
        )
        for r in range(wide)
    ]
    conv = []
    for r in range(1, wide - 1):
        conv.append(sum(tap(0, i, j) * views[r + i - 1][j] for i in range(3) for j in range(3)))
    side = jnp.zeros((channels, LANES), jnp.float32)
    for i in range(3):
        line = sum(tap(0, i, j) * beside[j] for j in range(3))
        side = side + (line if i == 1 else pltpu.roll(line, (2 - 2 * i) % LANES, 1))
    update = mixer(0, conv + [side])
    widened = [masks[r] * (current[r] + update[r - 1]) for r in range(1, wide - 1)]
    rim = beside_mask * (beside[1] + update[-1])

    views = [
        shifted(
            widened[r - 1],
            pltpu.roll(rim, (LANES - 2 * r) % LANES, 1),
            pltpu.roll(rim, (cols - 1 - half - 2 * r) % LANES, 1),
        )
        for r in range(1, wide - 1)
    ]
    conv = []
    for r in range(rows):
        conv.append(sum(tap(1, i, j) * views[r + i][j] for i in range(3) for j in range(3)))
    update = mixer(1, conv)
    for r in range(rows):
        out_ref[:, r, :] = masks[r + 2] * (widened[r + 1] + update[r])


def ocean_step(sums, up, down, left, right, ocean_state, land_mask, coupling, source, weight, columns, expand, reduce_w):
    return pl.pallas_call(
        ocean_kernel,
        out_shape=jax.ShapeDtypeStruct(ocean_state.shape, jnp.float32),
        compiler_params=params(60),
        name="ocean_step",
    )(
        sums,
        up,
        down,
        left,
        right,
        ocean_state,
        land_mask,
        jnp.repeat(coupling, 8, axis=1),
        source,
        weight,
        columns,
        expand,
        jnp.swapaxes(reduce_w, 1, 2),
    )


def depthwise(field, taps):
    height = field.shape[1] - 2
    width = field.shape[2] - 2
    result = jnp.zeros((field.shape[0], height, width), jnp.float32)
    for row_off in range(3):
        for col_off in range(3):
            result = (
                result
                + taps[:, 3 * row_off + col_off][:, None, None]
                * field[:, row_off : row_off + height, col_off : col_off + width]
            )
    return result


def ocean_mixer(values, gain, expand, reduce_w):
    channels, height, width = values.shape
    flat = values.reshape(channels, height * width)
    centre = jnp.mean(flat, axis=0)
    spread = jnp.mean(flat * flat, axis=0) - centre * centre
    normed = (flat - centre) * lax.rsqrt(spread + EPSILON) * gain[:, None]
    hidden = jax.nn.gelu(jnp.einsum("cd,cp->dp", expand, normed, precision=FINE))
    update = jnp.einsum("dc,dp->cp", reduce_w, hidden, precision=FINE)
    return update.reshape(channels, height, width)


def fast_step(
    atmos_state,
    ocean_state,
    land_mask,
    spectral_filter,
    atmos_gain,
    flux_readout,
    surface_coupling,
    surface_readout,
    flux_coupling,
    atmos_row_source,
    atmos_row_weight,
    atmos_col_source,
    atmos_col_weight,
    ocean_row_source,
    ocean_row_weight,
    ocean_col_source,
    ocean_col_weight,
    depth_taps,
    block_gain,
    expand_weight,
    reduce_weight,
    layer_scale,
):
    channels, atm_rows, width = atmos_state.shape
    lat, groups = lax.axis_size("lat"), lax.axis_size(COLUMN)
    places = [lax.axis_index("lat"), lax.axis_index("members"), lax.axis_index(COLUMN)]
    place = jnp.stack(places).astype(jnp.int32)
    members = lax.axis_size("members")
    far = lat // 2
    row_source, row_weight = ocean_row_source.T, ocean_row_weight.T
    col_source, col_weight = ocean_col_source.T, ocean_col_weight.T

    flux, stats = channel_sums(atmos_state, flux_readout)
    up, down = lat_edges(flux, ocean_state, land_mask, row_source, row_weight)
    packed, came, token = {}, {}, up
    for shift in (far, *(j for j in range(1, lat) if j != far), 0):
        packed[shift] = pack_filter(spectral_filter, after(place, token), lat, members, shift)
        token = packed[shift]
    up = lax.ppermute(up, "lat", [(i, i + 1) for i in range(lat - 1)])
    down = lax.ppermute(down, "lat", [(i + 1, i) for i in range(lat - 1)])

    came[0] = packed[0]
    for shift in range(1, lat):
        came[shift] = sent(packed[shift], shift)
    stats = summed_over_columns(stats)
    fresh = [
        normed_pieces(atmos_state, stats, atmos_gain, place, lat, q) for q in range(CHUNKS)
    ]
    up, down = lax.optimization_barrier((up, down, fresh[0][0], fresh[-1][0]))[:2]
    sums = summed_over_columns(flux_rows(place, up, down, flux, row_source, row_weight))
    first, last = lon_sides(up, down, ocean_state, land_mask, col_source, col_weight)
    left = lax.ppermute(last, COLUMN, [(i, (i + 1) % groups) for i in range(groups)])
    right = lax.ppermute(first, COLUMN, [(i, (i - 1) % groups) for i in range(groups)])
    piece = surface_piece(
        place,
        up,
        down,
        left,
        right,
        ocean_state,
        surface_readout,
        jnp.concatenate([atmos_row_source.astype(jnp.float32), atmos_row_weight], axis=1),
        atmos_col_source.T,
        atmos_col_weight.T,
        ocean_state.shape[2] * groups,
        width,
    )
    atmos_next = forced(atmos_state, surface_coupling, summed_over_columns(piece))
    columns = jnp.concatenate([depth_taps, block_gain[..., None], layer_scale[..., None]], axis=2)
    ocean_next = ocean_step(
        sums,
        up,
        down,
        left,
        right,
        ocean_state,
        land_mask,
        flux_coupling,
        col_source,
        col_weight,
        jnp.concatenate([columns[0], columns[1]], axis=1),
        expand_weight,
        reduce_weight,
    )

    done = (atmos_next, ocean_next, fresh[0][0], fresh[-1][0])
    pieces, token = [], (came[far], done)
    for q in range(CHUNKS):
        pieces.append(dealt(lax.optimization_barrier((*fresh[q], token))[:lat]))
        token = pieces[q][far]
    came = lax.optimization_barrier((*(came[j] for j in range(lat)), done))[:lat]
    filters = swapped_filter(came)
    pieces = [dealt(filtered_pieces(pieces[q], *filters[q], place)) for q in range(CHUNKS)]
    for q in range(CHUNKS):
        atmos_next = joined(atmos_next, pieces[q], place, q)
    return (atmos_next, ocean_next)


def general_step(
    atmos_state,
    ocean_state,
    land_mask,
    spectral_filter,
    atmos_gain,
    flux_readout,
    surface_coupling,
    surface_readout,
    flux_coupling,
    atmos_row_source,
    atmos_row_weight,
    atmos_col_source,
    atmos_col_weight,
    ocean_row_source,
    ocean_row_weight,
    ocean_col_source,
    ocean_col_weight,
    depth_taps,
    block_gain,
    expand_weight,
    reduce_weight,
    layer_scale,
):
    channels, atm_rows, width_atm = atmos_state.shape
    ocean_channels, ocean_rows, ocean_cols = ocean_state.shape
    lat_place = lax.axis_index("lat")

    ocean_mask = land_mask.astype(jnp.float32)
    row_table = jnp.concatenate([ocean_row_source.astype(jnp.float32), ocean_row_weight], axis=1)
    col_table = jnp.concatenate([ocean_col_source.astype(jnp.float32), ocean_col_weight], axis=1)
    row_table = jnp.pad(row_table, ((0, 0), (0, ocean_cols - row_table.shape[1])))
    wide = jnp.concatenate([ocean_state, ocean_mask[None], row_table[None]], axis=0)
    wide = padded(wide, (("lat", 1),), 2)
    row_table = wide[-1, :, 0:4]
    col_table = jnp.pad(col_table.T, ((0, wide.shape[1] - 4), (0, 0)))
    wide = jnp.concatenate([wide[:-1], col_table[None]], axis=0)
    wide = padded(wide, ((COLUMN, 2),), 2)
    col_table = wide[-1, 0:4].T
    state_wide, mask_wide = wide[:ocean_channels], wide[ocean_channels]

    partial_flux = jnp.einsum("fc,chw->fhw", flux_readout, atmos_state, precision=PRECISE)
    sums = jnp.concatenate(
        [
            partial_flux,
            jnp.sum(atmos_state, axis=0)[None],
            jnp.sum(atmos_state * atmos_state, axis=0)[None],
        ],
        axis=0,
    )
    sums = summed_over_columns(sums)
    flux, stats = sums[:-2], sums[-2:]

    surface_wide = jnp.einsum("sc,chw->shw", surface_readout, state_wide, precision=PRECISE)
    row_map = regrid_matrix(
        atmos_row_source, atmos_row_weight, lat_place * ocean_rows - 2, ocean_rows + 4, 0
    )
    col_map = regrid_matrix(
        atmos_col_source,
        atmos_col_weight,
        lax.axis_index(COLUMN) * ocean_cols - 2,
        ocean_cols + 4,
        ocean_cols * lax.axis_size(COLUMN),
    )
    atmos_piece = apply_maps(surface_wide, row_map, col_map)
    fields = lax.all_gather(atmos_piece, COLUMN, axis=2, tiled=True)

    centre = stats[0] / CA
    spread = stats[1] / CA - centre * centre
    normed = (atmos_state - centre) * lax.rsqrt(spread + EPSILON) * atmos_gain[:, None, None]
    filtered = global_filter(normed, spectral_filter)
    forcing = jnp.einsum("cs,shw->chw", surface_coupling, fields, precision=PRECISE)
    atmos_next = atmos_state + filtered + forcing

    before, behind = flux_reach(atm_rows, ocean_rows)
    flux_wide = rows_around(flux, before, behind)
    row_back = regrid_matrix(
        row_table[:, 0:2].astype(jnp.int32),
        row_table[:, 2:4],
        lat_place * atm_rows - before,
        atm_rows + before + behind,
        0,
    )
    col_back = regrid_matrix(
        col_table[:, 0:2].astype(jnp.int32), col_table[:, 2:4], 0, width_atm, 0
    )
    flux_ocean = apply_maps(flux_wide, row_back, col_back)
    current = mask_wide * (
        state_wide + jnp.einsum("cf,fhw->chw", flux_coupling, flux_ocean, precision=PRECISE)
    )
    update = ocean_mixer(
        depthwise(current, depth_taps[0]), block_gain[0], expand_weight[0], reduce_weight[0]
    )
    widened = mask_wide[1:-1, 1:-1] * (
        current[:, 1:-1, 1:-1] + layer_scale[0][:, None, None] * update
    )
    update = ocean_mixer(
        depthwise(widened, depth_taps[1]), block_gain[1], expand_weight[1], reduce_weight[1]
    )
    current = ocean_mask * (widened[:, 1:-1, 1:-1] + layer_scale[1][:, None, None] * update)
    return (atmos_next, current)


def body(*arrays):
    atmos_state, ocean_state, _, spectral_filter = arrays[:4]
    channels, atm_rows, width = atmos_state.shape
    lat, members, groups = (lax.axis_size(a) for a in ("lat", "members", COLUMN))
    freqs, height = spectral_filter.shape[2:]
    fast = can_deal(channels, atm_rows, width, freqs, height, lat, members) and can_tile(
        *ocean_state.shape, atm_rows, groups
    )
    return fast_step(*arrays) if fast else general_step(*arrays)


def solution(mesh):
    return jax.shard_map(
        body,
        mesh=mesh,
        in_specs=(
            P(("members", "lon", "chan"), "lat", None),
            P("members", "lat", ("lon", "chan")),
            P("lat", ("lon", "chan")),
            P(None, ("lon", "chan"), "lat", None),
            P(("lon", "chan")),
            P(None, ("lon", "chan")),
            P(("lon", "chan"), None),
            P(),
            P(),
            P("lat", None),
            P("lat", None),
            P(("lon", "chan"), None),
            P(("lon", "chan"), None),
            P("lat", None),
            P("lat", None),
            P(("lon", "chan"), None),
            P(("lon", "chan"), None),
            P(),
            P(),
            P(),
            P(),
            P(),
        ),
        out_specs=(
            P(("members", "lon", "chan"), "lat", None),
            P("members", "lat", ("lon", "chan")),
        ),
        check_vma=False,
    )
```

```python
import functools
import math

import jax
import jax.numpy as jnp
import ml_dtypes
import numpy as np
from jax import lax
from jax.experimental import pallas as pl
from jax.experimental.pallas import tpu as pltpu
from jax.sharding import PartitionSpec as P

CA = 384


EPSILON = 1e-05
PRECISE = lax.Precision.HIGHEST
FINE = lax.Precision.HIGH
LANES = 128
CHUNKS = 2
COLUMN = ("lon", "chan")
REACH = 16
STREAMS = 4


def padded(x, sides, width):
    for axis, dim in sides:
        count, length = (lax.axis_size(axis), x.shape[dim])
        up = [(i, (i + 1) % count) for i in range(count)]
        down = [(j, i) for i, j in up]
        last = lax.slice_in_dim(x, length - width, length, axis=dim)
        leading = lax.slice_in_dim(x, 0, width, axis=dim)
        before = lax.ppermute(last, axis, up)
        after = lax.ppermute(leading, axis, down)
        x = jnp.concatenate([before, x, after], axis=dim)
    return x


def fourier_tables(length):
    places = jnp.arange(length, dtype=jnp.int32)
    angles = (
        2.0
        * math.pi
        / length
        * jnp.mod(places[:, None] * places[None, :], length).astype(jnp.float32)
    )
    return (jnp.cos(angles), jnp.sin(angles))


def regrid_matrix(source, weight, offset, span, period):
    shares = weight / jnp.sum(weight, axis=1, keepdims=True)
    relative = source - offset
    if period > 0:
        relative = jnp.mod(relative, period)
    columns = jnp.arange(span, dtype=jnp.int32)[None, :]
    return shares[:, 0:1] * (relative[:, 0:1] == columns).astype(jnp.float32) + shares[:, 1:2] * (
        relative[:, 1:2] == columns
    ).astype(jnp.float32)


def apply_maps(field, row_map, col_map):
    by_rows = jnp.einsum("jh,shw->sjw", row_map, field, precision=PRECISE)
    return jnp.einsum("sjw,kw->sjk", by_rows, col_map, precision=PRECISE)


def grid_rims(field):
    return padded(field, (("lat", 1), (("lon", "chan"), 2)), 2)


def along_last(field, table):
    return jnp.einsum("ckh,hm->ckm", field, table, precision=PRECISE)


def global_filter(normed, spectral_filter):
    width_len = normed.shape[2]
    height_len = spectral_filter.shape[3]
    cos_w, sin_w = fourier_tables(width_len)
    cos_h, sin_h = fourier_tables(height_len)
    real_w = jnp.einsum("chn,nk->ckh", normed, cos_w, precision=PRECISE)
    imag_w = -jnp.einsum("chn,nk->ckh", normed, sin_w, precision=PRECISE)
    real_w, imag_w = (
        lax.all_to_all(real_w, "lat", split_axis=1, concat_axis=2, tiled=True),
        lax.all_to_all(imag_w, "lat", split_axis=1, concat_axis=2, tiled=True),
    )
    real_s = along_last(real_w, cos_h) + along_last(imag_w, sin_h)
    imag_s = along_last(imag_w, cos_h) - along_last(real_w, sin_h)
    kern_real = spectral_filter[0]
    kern_imag = spectral_filter[1]
    real_f = kern_real * real_s - kern_imag * imag_s
    imag_f = kern_real * imag_s + kern_imag * real_s
    real_b = (along_last(real_f, cos_h) - along_last(imag_f, sin_h)) / height_len
    imag_b = (along_last(imag_f, cos_h) + along_last(real_f, sin_h)) / height_len
    real_b, imag_b = (
        lax.all_to_all(real_b, "lat", split_axis=2, concat_axis=1, tiled=True),
        lax.all_to_all(imag_b, "lat", split_axis=2, concat_axis=1, tiled=True),
    )
    back = jnp.einsum("ckh,kn->chn", real_b, cos_w, precision=PRECISE) - jnp.einsum(
        "ckh,kn->chn", imag_b, sin_w, precision=PRECISE
    )
    return back / width_len


def flux_reach(atm_rows, ocean_rows):
    first = (-2 * atm_rows) // ocean_rows - 1
    last = (atm_rows * (ocean_rows + 1)) // ocean_rows + 2
    return -first, max(last - atm_rows + 1, 0)


def rows_around(field, before, behind):
    count = lax.axis_size("lat")
    up = [(i, i + 1) for i in range(count - 1)]
    down = [(i + 1, i) for i in range(count - 1)]
    rows = field.shape[1]
    above = lax.ppermute(field[:, rows - before :], "lat", up)
    below = lax.ppermute(field[:, :behind], "lat", down)
    return jnp.concatenate([above, field, below], axis=1)


def params(mib):
    return pltpu.CompilerParams(vmem_limit_bytes=mib * 2**20)


def can_deal(channels, rows, width, freqs, height, lat, members):
    return (
        members == 2
        and lat == 4
        and channels % (lat * CHUNKS * members) == 0
        and channels % STREAMS == 0
        and rows % 8 == 0
        and rows * lat == height
        and width % LANES == 0
        and freqs * lat == width
        and freqs == 96
        and height % 32 == 0
    )


def split_table(table):
    high = table.astype(ml_dtypes.bfloat16)
    low = (table - high.astype(np.float64)).astype(ml_dtypes.bfloat16)
    return high, low


@functools.lru_cache(maxsize=None)
def dealt_tables(height, width, lat):
    freqs = width // lat
    angle = 2.0 * np.pi / height * (np.outer(np.arange(height), np.arange(height)) % height)
    cos_h, sin_h = np.cos(angle), np.sin(angle)
    rows_on = np.block([[cos_h, sin_h], [-sin_h, cos_h]])
    rows_back = np.block([[cos_h, -sin_h], [sin_h, cos_h]])
    cols_on = np.zeros((lat, width, 2, lat, LANES))
    for z in range(lat):
        for j in range(lat):
            k = (z + j) % lat * freqs + np.arange(freqs)
            turn = 2.0 * np.pi / width * (np.outer(np.arange(width), k) % width)
            cols_on[z, :, 0, j, :freqs] = np.cos(turn)
            cols_on[z, :, 1, j, :freqs] = -np.sin(turn)
    cols_on = cols_on.reshape(lat, width, 2 * lat * LANES)
    cols_back = np.swapaxes(cols_on, 1, 2) / (height * width)
    return [split_table(t) for t in (cols_on, rows_on, rows_back, cols_back)]


def pack_kernel(place_ref, filter_ref, out_ref):
    _, channels, freqs, rows = filter_ref.shape
    main, rest = rows * 3 // 4, rows // 4
    for part in range(2):
        for c in range(channels):
            turned = filter_ref[part, c].T
            out_ref[0, part, c, :, 0:freqs] = turned[0:main]
            for i in range(3):
                out_ref[0, part, c, i * rest : (i + 1) * rest, freqs:LANES] = turned[
                    main:, 32 * i : 32 * (i + 1)
                ]


def pack_filter(spectral_filter, place, lat, members, shift):
    _, channels, freqs, height = spectral_filter.shape
    half = channels // (lat * CHUNKS * members)

    def source(q, place):
        dest = place[0] ^ shift
        return (0, (dest * CHUNKS + q) * members + place[1], 0, 0)

    shape = (CHUNKS, 2, half, height * 3 // 4, LANES)
    return pl.pallas_call(
        pack_kernel,
        grid_spec=pltpu.PrefetchScalarGridSpec(
            num_scalar_prefetch=1,
            grid=(CHUNKS,),
            in_specs=[pl.BlockSpec((2, half, freqs, height), source)],
            out_specs=pl.BlockSpec((1, *shape[1:]), lambda q, place: (q, 0, 0, 0, 0)),
        ),
        out_shape=jax.ShapeDtypeStruct(shape, jnp.float32),
        compiler_params=params(60),
        cost_estimate=pl.CostEstimate(flops=1, bytes_accessed=1, transcendentals=0),
        name="pack_filter",
    )(place, spectral_filter)


def sums_kernel(readout_ref, *refs):
    parts, (flux_ref, stats_ref) = refs[:STREAMS], refs[STREAMS:]
    channels, tile, width = parts[0].shape
    fluxes = readout_ref.shape[0]
    totals = (jnp.zeros((tile, width), jnp.float32),) * (fluxes + 2)
    for i, part in enumerate(parts):

        def add(c, totals, i=i, part=part):
            value = part[c]
            new = [totals[f] + readout_ref[f, i * channels + c] * value for f in range(fluxes)]
            return (*new, totals[fluxes] + value, totals[fluxes + 1] + value * value)

        totals = lax.fori_loop(0, channels, add, totals, unroll=4)
    for i in range(fluxes):
        flux_ref[i] = totals[i]
    stats_ref[0] = totals[fluxes]
    stats_ref[1] = totals[fluxes + 1]


def channel_sums(atmos_state, flux_readout):
    channels, rows, width = atmos_state.shape
    counts = (flux_readout.shape[0], 2)
    return pl.pallas_call(
        sums_kernel,
        grid=(rows // 8,),
        in_specs=[pl.BlockSpec(memory_space=pltpu.SMEM)]
        + [
            pl.BlockSpec((channels // STREAMS, 8, width), lambda i, s=s: (s, i, 0))
            for s in range(STREAMS)
        ],
        out_specs=[pl.BlockSpec((n, 8, width), lambda i: (0, i, 0)) for n in counts],
        out_shape=[jax.ShapeDtypeStruct((n, rows, width), jnp.float32) for n in counts],
        compiler_params=params(60),
        cost_estimate=pl.CostEstimate(flops=1, bytes_accessed=1, transcendentals=0),
        name="channel_sums",
    )(flux_readout, *[atmos_state] * STREAMS)


def norm_kernel(count, chunk, place_ref, gain_ref, sums_ref, state_ref, *out_refs):
    step = pl.program_id(0)
    part = state_ref.shape[0]
    first = ((place_ref[0] ^ step) * CHUNKS + chunk) * part
    centre = sums_ref[0] / CA
    spread = sums_ref[1] / CA - centre * centre
    scale = lax.rsqrt(spread + EPSILON)
    for j in range(count):

        @pl.when(step == j)
        def _(out=out_refs[j]):
            for c in range(part):
                out[c] = (state_ref[c] - centre) * scale * gain_ref[first + c]


def normed_pieces(atmos_state, sums, gain, place, lat, chunk):
    channels, rows, width = atmos_state.shape
    part = channels // (lat * CHUNKS)
    return pl.pallas_call(
        functools.partial(norm_kernel, lat, chunk),
        grid_spec=pltpu.PrefetchScalarGridSpec(
            num_scalar_prefetch=1,
            grid=(lat,),
            in_specs=[
                pl.BlockSpec(memory_space=pltpu.SMEM),
                pl.BlockSpec(sums.shape, lambda j, place: (0, 0, 0)),
                pl.BlockSpec(
                    (part, rows, width),
                    lambda j, place: ((place[0] ^ j) * CHUNKS + chunk, 0, 0),
                ),
            ],
            out_specs=[pl.BlockSpec((part, rows, width), lambda j, place: (0, 0, 0))] * lat,
        ),
        out_shape=[jax.ShapeDtypeStruct((part, rows, width), jnp.float32)] * lat,
        compiler_params=params(60),
        name="normed_pieces",
    )(place, gain, sums, atmos_state)


def split(value):
    high = value.astype(jnp.bfloat16)
    return high, (value - high.astype(jnp.float32)).astype(jnp.bfloat16)


def product(left, right):
    dot = functools.partial(jnp.dot, preferred_element_type=jnp.float32)
    return dot(left[0], right[0]) + (dot(left[0], right[1]) + dot(left[1], right[0]))


def unpacked(packed_ref, order, part, c):
    blocks = []
    lane = lax.broadcasted_iota(jnp.int32, (packed_ref.shape[3] // 3, LANES), 1)
    rest = packed_ref.shape[3] // 3
    for j in order:
        main = packed_ref[j, part, c]
        a, b, d = (
            pltpu.roll(main[i * rest : (i + 1) * rest], 32 * (i + 1), 1) for i in range(3)
        )
        tail = jnp.where(lane < 32, a, jnp.where(lane < 64, b, d))
        blocks.append(jnp.concatenate([main, tail], axis=0))
    return jnp.concatenate(blocks, axis=1)


def spectral_kernel(count, place_ref, *refs):
    pieces = refs[:count]
    own_ref, other_ref = refs[count : count + 2]
    tables = [(refs[count + 2 + 2 * i], refs[count + 3 + 2 * i]) for i in range(4)]
    outs = refs[count + 10 : 2 * count + 10]
    high_ref, low_ref = refs[2 * count + 10 :]
    part, rows, width = pieces[0].shape
    height = rows * count
    span = count * LANES
    cols_on, rows_on, rows_back, cols_back = tables
    cols_on = (cols_on[0][0], cols_on[1][0])
    cols_back = (cols_back[0][0], cols_back[1][0])
    rows_on = (rows_on[0][...], rows_on[1][...])
    rows_back = (rows_back[0][...], rows_back[1][...])

    odd = lax.rem(place_ref[0], 2) == 1
    order = [0, jnp.where(odd, 3, 1), 2, jnp.where(odd, 1, 3)]

    def ordered(values):
        return [
            values[0],
            jnp.where(odd, values[3], values[1]),
            values[2],
            jnp.where(odd, values[1], values[3]),
        ]

    def run(filter_ref):
        lines = ordered([p[...].reshape(part * rows, width) for p in pieces])
        stacked = jnp.concatenate(lines, axis=0)
        spectra = product(split(stacked), cols_on)
        for c in range(part):
            own = jnp.concatenate(
                [spectra[(j * part + c) * rows : (j * part + c + 1) * rows] for j in range(count)],
                axis=0,
            )
            both = jnp.concatenate([own[:, :span], own[:, span:]], axis=0)
            full = product(rows_on, split(both))
            real, imag = full[:height], full[height:]
            kern_real = unpacked(filter_ref, order, 0, c)
            kern_imag = unpacked(filter_ref, order, 1, c)
            both = jnp.concatenate(
                [kern_real * real - kern_imag * imag, kern_real * imag + kern_imag * real], axis=0
            )
            back = product(rows_back, split(both))
            high, low = split(back)
            at = slice(c * height, (c + 1) * height)
            high_ref[at, :span] = high[:height]
            high_ref[at, span:] = high[height:]
            low_ref[at, :span] = low[:height]
            low_ref[at, span:] = low[height:]
        result = product((high_ref[...], low_ref[...]), cols_back)
        result = result.reshape(part, height, width)
        parts = ordered([result[:, j * rows : (j + 1) * rows] for j in range(count)])
        for out, value in zip(outs, parts):
            out[...] = value

    @pl.when(pl.program_id(0) == 0)
    def _():
        run(own_ref)

    @pl.when(pl.program_id(0) == 1)
    def _():
        run(other_ref)


def filtered_pieces(pieces, own, other, place):
    lat = len(pieces)
    chunk, rows, width = pieces[0].shape
    half = chunk // 2
    height = rows * lat
    tables = [t for pair in dealt_tables(height, width, lat) for t in pair]

    def mine(i, place):
        return (lax.rem(i + place[1], 2), 0, 0)

    def table_spec(t):
        if t.ndim == 3:
            return pl.BlockSpec((1, *t.shape[1:]), lambda i, place: (place[0], 0, 0))
        return pl.BlockSpec(t.shape, lambda i, place: (0, 0))

    filter_spec = pl.BlockSpec(own.shape, lambda i, place: (0, 0, 0, 0, 0))
    piece_spec = pl.BlockSpec((half, rows, width), mine)
    return pl.pallas_call(
        functools.partial(spectral_kernel, lat),
        grid_spec=pltpu.PrefetchScalarGridSpec(
            num_scalar_prefetch=1,
            grid=(2,),
            in_specs=[piece_spec] * lat + [filter_spec] * 2 + [table_spec(t) for t in tables],
            out_specs=[piece_spec] * lat,
            scratch_shapes=[pltpu.VMEM((half * height, 2 * lat * LANES), jnp.bfloat16)] * 2,
        ),
        out_shape=[jax.ShapeDtypeStruct((chunk, rows, width), jnp.float32)] * lat,
        compiler_params=params(60),
        name="filtered_pieces",
    )(place, *pieces, own, other, *[jnp.asarray(t) for t in tables])


def forced_kernel(coupling_ref, fields_ref, state_ref, out_ref):
    fields = [fields_ref[s] for s in range(fields_ref.shape[0])]

    @pl.loop(0, state_ref.shape[0], unroll=4)
    def _(c):
        value = state_ref[c]
        for s, field in enumerate(fields):
            value = value + coupling_ref[c, s] * field
        out_ref[c] = value


def forced(atmos_state, coupling, fields):
    channels, rows, width = atmos_state.shape
    block = pl.BlockSpec((channels, 8, width), lambda i: (0, i, 0))
    return pl.pallas_call(
        forced_kernel,
        grid=(rows // 8,),
        in_specs=[
            pl.BlockSpec(memory_space=pltpu.SMEM),
            pl.BlockSpec((fields.shape[0], 8, width), lambda i: (0, i, 0)),
            block,
        ],
        out_specs=block,
        out_shape=jax.ShapeDtypeStruct(atmos_state.shape, jnp.float32),
        compiler_params=params(60),
        name="forced",
    )(coupling, fields, atmos_state)


def join_kernel(count, chunk, place_ref, state_ref, *refs):
    pieces = refs[:count]
    out_ref, held, added, in_sems, piece_sems, out_sems = refs[count:]
    part = held.shape[1]
    starts = [((place_ref[0] ^ j) * CHUNKS + chunk) * part for j in range(count)]
    incoming, others, outgoing = [], [], []
    for j in range(count):
        here = pl.ds(starts[j], part)
        incoming.append(pltpu.make_async_copy(state_ref.at[here], held.at[j], in_sems.at[j]))
        others.append(pltpu.make_async_copy(pieces[j], added.at[j], piece_sems.at[j]))
        outgoing.append(pltpu.make_async_copy(held.at[j], out_ref.at[here], out_sems.at[j]))
    for copy in incoming + others:
        copy.start()
    for j in range(count):
        incoming[j].wait()
        others[j].wait()
        held[j] = held[j] + added[j]
        outgoing[j].start()
    for copy in outgoing:
        copy.wait()


def joined(state, pieces, place, chunk):
    lat = len(pieces)
    part, rows, width = pieces[0].shape
    hbm = pl.BlockSpec(memory_space=pl.ANY)
    return pl.pallas_call(
        functools.partial(join_kernel, lat, chunk),
        in_specs=[pl.BlockSpec(memory_space=pltpu.SMEM)] + [hbm] * (lat + 1),
        out_specs=hbm,
        out_shape=jax.ShapeDtypeStruct(state.shape, jnp.float32),
        scratch_shapes=[pltpu.VMEM((lat, part, rows, width), jnp.float32)] * 2
        + [pltpu.SemaphoreType.DMA((lat,))] * 3,
        input_output_aliases={1: 0},
        compiler_params=params(63),
        cost_estimate=pl.CostEstimate(flops=1, bytes_accessed=1, transcendentals=0),
        name="joined",
    )(place, state, *pieces)


def sent(piece, step):
    lat = lax.axis_size("lat")
    return lax.ppermute(piece, "lat", [(i, i ^ step) for i in range(lat)])


def dealt(pieces):
    return [pieces[0]] + [sent(pieces[j], j) for j in range(1, len(pieces))]


def after(value, earlier):
    return lax.optimization_barrier((value, earlier))[0]


def swapped_filter(pieces):
    members = lax.axis_size("members")
    halves = [jnp.stack([p[q] for p in pieces]) for q in range(CHUNKS)]
    return [
        (own, lax.ppermute(own, "members", [(i, (i + 1) % members) for i in range(members)]))
        for own in halves
    ]


def summed_over_columns(x):
    for axis in ("chan", "lon"):
        count = lax.axis_size(axis)
        total = x
        for shift in range(1, count):
            total = total + lax.ppermute(x, axis, [(i, (i + shift) % count) for i in range(count)])
        x = total
    return x


def can_tile(ocean_channels, ocean_rows, ocean_cols, atm_rows, groups):
    before, behind = flux_reach(atm_rows, ocean_rows)
    return (
        ocean_cols == LANES
        and ocean_channels % 8 == 0
        and ocean_rows == 4
        and atm_rows % 8 == 0
        and max(before, behind) <= REACH <= atm_rows
        and groups > 1
    )


def exact(left, right):
    return jnp.dot(left, right, precision=PRECISE, preferred_element_type=jnp.float32)


def iota(shape, dim):
    return lax.broadcasted_iota(jnp.int32, shape, dim)


def table_row(source, weight, row):
    lane = iota((1, LANES), 1)
    values = [
        source[0:1, row : row + 1].astype(jnp.float32),
        source[1:2, row : row + 1].astype(jnp.float32),
        weight[0:1, row : row + 1],
        weight[1:2, row : row + 1],
    ]
    out = jnp.zeros((1, LANES), jnp.float32)
    for i, value in enumerate(values):
        out = jnp.where(lane == i, value, out)
    return out


def stacked_rows(rows):
    at = iota((8, rows[0].shape[1]), 0)
    tile = jnp.zeros((8, rows[0].shape[1]), jnp.float32)
    for i, row in enumerate(rows):
        tile = jnp.where(at == i, row, tile)
    return tile


def edges_kernel(flux_ref, state_ref, mask_ref, source_ref, weight_ref, *out_refs):
    fluxes, atm_rows, width = flux_ref.shape
    channels, rows, _ = state_ref.shape
    span = channels + 8
    source, weight = source_ref[...], weight_ref[...]
    for out, first, atm_first in (
        (out_refs[0], rows - 2, atm_rows - REACH),
        (out_refs[1], 0, 0),
    ):
        for i in range(2):
            row = first + i
            out[i * span : i * span + channels] = state_ref[:, row, :]
            out[i * span + channels : (i + 1) * span] = stacked_rows(
                [mask_ref[row : row + 1, :].astype(jnp.float32), table_row(source, weight, row)]
            )
        at = 2 * span
        for f in range(fluxes):
            for lanes in range(0, width, LANES):
                out[at : at + REACH] = flux_ref[f, atm_first : atm_first + REACH, lanes : lanes + LANES]
                at += REACH


def lat_edges(flux, ocean_state, land_mask, source, weight):
    fluxes, _, width = flux.shape
    channels = ocean_state.shape[0]
    shape = (2 * (channels + 8) + fluxes * width // LANES * REACH, LANES)
    return pl.pallas_call(
        edges_kernel,
        out_shape=[jax.ShapeDtypeStruct(shape, jnp.float32)] * 2,
        compiler_params=params(60),
        name="lat_edges",
    )(flux, ocean_state, land_mask, source, weight)


def rows_kernel(place_ref, up_ref, down_ref, flux_ref, source_ref, weight_ref, out_ref):
    fluxes, atm_rows, width = flux_ref.shape
    rows = source_ref.shape[1]
    span = (up_ref.shape[0] - fluxes * width // LANES * REACH) // 2
    source, weight = source_ref[...], weight_ref[...]
    at = span - 7
    table = stacked_rows(
        [up_ref[at : at + 1], up_ref[span + at : span + at + 1]]
        + [table_row(source, weight, r) for r in range(rows)]
        + [down_ref[at : at + 1], down_ref[span + at : span + at + 1]]
    )
    first = place_ref[0] * atm_rows - REACH
    reach = atm_rows + 2 * REACH
    spot = (iota((8, reach), 1) + first).astype(jnp.float32)
    total = table[:, 2:3] + table[:, 3:4]
    total = jnp.where(total > 0.0, total, 1.0)
    picks = jnp.where(spot == table[:, 0:1], table[:, 2:3] / total, 0.0) + jnp.where(
        spot == table[:, 1:2], table[:, 3:4] / total, 0.0
    )
    tiles = width // LANES
    for f in range(fluxes):
        parts = []
        for ref in (up_ref, down_ref):
            at = 2 * span + f * tiles * REACH
            parts.append(
                jnp.concatenate(
                    [ref[at + i * REACH : at + (i + 1) * REACH] for i in range(tiles)], axis=1
                )
            )
        field = jnp.concatenate([parts[0], flux_ref[f], parts[1]], axis=0)
        out_ref[f * 8 : (f + 1) * 8] = exact(picks, field)


def flux_rows(place, up, down, flux, source, weight):
    fluxes, atm_rows, width = flux.shape
    vmem = pl.BlockSpec(memory_space=pltpu.VMEM)
    return pl.pallas_call(
        rows_kernel,
        in_specs=[pl.BlockSpec(memory_space=pltpu.SMEM)] + [vmem] * 5,
        out_specs=vmem,
        out_shape=jax.ShapeDtypeStruct((8 * fluxes, width), jnp.float32),
        compiler_params=params(60),
        name="flux_rows",
    )(place, up, down, flux, source, weight)


def row_tile(r, rows, span, up_ref, down_ref, state_ref):
    channels = span - 8
    if r < 2:
        return up_ref[r * span : r * span + channels]
    if r < rows + 2:
        return state_ref[:, r - 2, :]
    return down_ref[(r - rows - 2) * span : (r - rows - 2) * span + channels]


def mask_row(r, rows, span, up_ref, down_ref, mask_ref):
    channels = span - 8
    if r < 2:
        return up_ref[r * span + channels : r * span + channels + 1]
    if r < rows + 2:
        return mask_ref[r - 2 : r - 1, :].astype(jnp.float32)
    at = (r - rows - 2) * span + channels
    return down_ref[at : at + 1]


def sides_kernel(up_ref, down_ref, state_ref, mask_ref, source_ref, weight_ref, first_ref, last_ref):
    channels, rows, _ = state_ref.shape
    span = channels + 8
    lane = iota((1, LANES), 1)
    first = jnp.zeros((channels, LANES), jnp.float32)
    last = jnp.zeros((channels, LANES), jnp.float32)
    first_mask = jnp.zeros((1, LANES), jnp.float32)
    last_mask = jnp.zeros((1, LANES), jnp.float32)
    for r in range(rows + 4):
        tile = row_tile(r, rows, span, up_ref, down_ref, state_ref)
        mask = mask_row(r, rows, span, up_ref, down_ref, mask_ref)
        here = (lane >= 2 * r) & (lane < 2 * r + 2)
        first = jnp.where(here, pltpu.roll(tile, 2 * r, 1), first)
        last = jnp.where(here, pltpu.roll(tile, 2 * r + 2, 1), last)
        first_mask = jnp.where(here, turned(mask, 2 * r), first_mask)
        last_mask = jnp.where(here, turned(mask, 2 * r + 2), last_mask)
    first_ref[0:channels] = first
    last_ref[0:channels] = last
    source = source_ref[...].astype(jnp.float32)
    weight = weight_ref[...]
    table = [source[0:1], source[1:2], weight[0:1], weight[1:2]]
    first_ref[channels:span] = stacked_rows([first_mask] + table)
    last_ref[channels:span] = stacked_rows([last_mask] + [turned(t, 2) for t in table])


def turned(row, shift):
    return pltpu.roll(jnp.broadcast_to(row, (8, row.shape[1])), shift, 1)[0:1]


def lon_sides(up, down, ocean_state, land_mask, source, weight):
    shape = (ocean_state.shape[0] + 8, LANES)
    return pl.pallas_call(
        sides_kernel,
        out_shape=[jax.ShapeDtypeStruct(shape, jnp.float32)] * 2,
        compiler_params=params(60),
        name="lon_sides",
    )(up, down, ocean_state, land_mask, source, weight)


def surface_kernel(
    place_ref,
    period,
    up_ref,
    down_ref,
    left_ref,
    right_ref,
    state_ref,
    readout_ref,
    row_ref,
    source_ref,
    weight_ref,
    out_ref,
    lines_ref,
):
    channels, rows, cols = state_ref.shape
    span = channels + 8
    fields, atm_rows, width = out_ref.shape
    atm_cols = source_ref.shape[1]
    readout = readout_ref[...]
    lines_ref[...] = jnp.zeros_like(lines_ref)
    for r in range(rows + 4):
        tile = row_tile(r, rows, span, up_ref, down_ref, state_ref)
        lines_ref[r * 8 : r * 8 + fields] = exact(readout, tile)
    lines = lines_ref[...]
    sides = [exact(readout, ref[0:channels]) for ref in (left_ref, right_ref)]

    table = row_ref[...]
    total = table[:, 2:3] + table[:, 3:4]
    shares = (table[:, 2:3] / total, table[:, 3:4] / total)
    start = (place_ref[0] * rows - 2).astype(jnp.float32)
    sources = (table[:, 0:1] - start, table[:, 1:2] - start)

    def row_picks(row):
        row = row.astype(jnp.float32)
        return jnp.where(row == sources[0], shares[0], 0.0) + jnp.where(row == sources[1], shares[1], 0.0)

    source, weight = source_ref[...], weight_ref[...]
    total = weight[0:1] + weight[1:2]
    relative = source - (place_ref[2] * cols - 2)
    relative = jnp.where(relative < 0, relative + period, relative)
    relative = jnp.where(relative >= period, relative - period, relative)

    def col_picks(col):
        return jnp.where(col == relative[0:1], weight[0:1] / total, 0.0) + jnp.where(
            col == relative[1:2], weight[1:2] / total, 0.0
        )

    at = iota((LANES, atm_cols), 0)
    main = col_picks(at + 2)
    side = [col_picks((at & 1)), col_picks(cols + 2 + (at & 1))]
    spread = iota((atm_cols, width), 1) - place_ref[2] * atm_cols == iota((atm_cols, width), 0)
    spread = spread.astype(jnp.float32)
    lane = iota((atm_rows, 8 * (rows + 4)), 1)
    side_lane = iota((atm_rows, LANES), 1)
    side_rows = row_picks(side_lane >> 1)
    for s in range(fields):
        picks = jnp.where((lane & 7) == s, row_picks(lane >> 3), 0.0)
        piece = exact(exact(picks, lines), main)
        for i in range(2):
            piece = piece + exact(side_rows * sides[i][s : s + 1], side[i])
        out_ref[s] = exact(piece, spread)


def surface_piece(place, up, down, left, right, ocean_state, readout, row_table, source, weight, period, width):
    rows = ocean_state.shape[1]
    vmem = pl.BlockSpec(memory_space=pltpu.VMEM)
    shape = (readout.shape[0], row_table.shape[0], width)
    return pl.pallas_call(
        lambda place_ref, *refs: surface_kernel(place_ref, period, *refs),
        in_specs=[pl.BlockSpec(memory_space=pltpu.SMEM)] + [vmem] * 9,
        out_specs=vmem,
        out_shape=jax.ShapeDtypeStruct(shape, jnp.float32),
        scratch_shapes=[pltpu.VMEM((8 * (rows + 4), LANES), jnp.float32)],
        compiler_params=params(60),
        name="surface_piece",
    )(place, up, down, left, right, ocean_state, readout, row_table, source, weight)


def ocean_kernel(
    sums_ref,
    up_ref,
    down_ref,
    left_ref,
    right_ref,
    state_ref,
    mask_ref,
    coupling_ref,
    source_ref,
    weight_ref,
    columns_ref,
    expand_ref,
    reduce_ref,
    out_ref,
):
    channels, rows, cols = state_ref.shape
    span = channels + 8
    fluxes = coupling_ref.shape[1] // 8
    width = sums_ref.shape[1]
    wide = rows + 4
    lane = iota((1, LANES), 1)
    half = LANES // 2
    is_left = lane < half
    lines = sums_ref[0 : 8 * fluxes]
    coupling = coupling_ref[...]
    spot = iota((width, LANES), 0).astype(jnp.float32)

    def col_lines(s0, s1, w0, w1):
        total = w0 + w1
        total = jnp.where(total > 0.0, total, 1.0)
        return exact(
            lines, jnp.where(spot == s0, w0 / total, 0.0) + jnp.where(spot == s1, w1 / total, 0.0)
        )

    source, weight = source_ref[...].astype(jnp.float32), weight_ref[...]
    main_lines = col_lines(source[0:1], source[1:2], weight[0:1], weight[1:2])
    of_row = iota((channels, 8 * fluxes), 1) & 7

    current, masks = [], []
    for r in range(wide):
        forcing = exact(jnp.where(of_row == r, coupling, 0.0), main_lines)
        mask = mask_row(r, rows, span, up_ref, down_ref, mask_ref)
        masks.append(mask)
        current.append(mask * (row_tile(r, rows, span, up_ref, down_ref, state_ref) + forcing))

    def side_current(ref):
        table = ref[channels + 1 : channels + 5]
        side_lines = col_lines(table[0:1], table[1:2], table[2:3], table[3:4])
        spread = jnp.zeros((8 * fluxes, LANES), jnp.float32)
        at = iota((8 * fluxes, LANES), 0) & 7
        for r in range(wide):
            here = (at == r) & (lane >= 2 * r) & (lane < 2 * r + 2)
            spread = jnp.where(here, pltpu.roll(side_lines, 2 * r, 1), spread)
        mask = ref[channels : channels + 1]
        return mask, mask * (ref[0:channels] + exact(coupling, spread))

    left_mask, left = side_current(left_ref)
    right_mask, right = side_current(right_ref)
    inner = [jnp.zeros((channels, LANES), jnp.float32)] * 2
    for r in range(wide):
        inner[0] = jnp.where(lane == 2 * r, pltpu.roll(current[r], 2 * r, 1), inner[0])
        inner[1] = jnp.where(
            lane == half + 2 * r, pltpu.roll(current[r], (half + 2 * r + 1) % LANES, 1), inner[1]
        )
    beside = [
        jnp.where(is_left, left, inner[1]),
        jnp.where(is_left, pltpu.roll(left, LANES - 1, 1), pltpu.roll(right, half, 1)),
        jnp.where(is_left, inner[0], pltpu.roll(right, half - 1, 1)),
    ]
    beside_mask = jnp.where(is_left, turned(left_mask, LANES - 1), turned(right_mask, half))

    def shifted(tile, before, behind):
        return [
            jnp.where(lane == 0, before, pltpu.roll(tile, 1, 1)),
            tile,
            jnp.where(lane == cols - 1, behind, pltpu.roll(tile, cols - 1, 1)),
        ]

    def mixer(block, conv):
        base = block * 11
        gain = columns_ref[:, base + 9 : base + 10]
        scale = columns_ref[:, base + 10 : base + 11]
        points = jnp.concatenate(conv, axis=1)
        centre = jnp.mean(points, axis=0, keepdims=True)
        spread = jnp.mean(points * points, axis=0, keepdims=True) - centre * centre
        normed = (points - centre) * lax.rsqrt(spread + EPSILON) * gain
        hidden = jax.nn.gelu(product(split(expand_ref[block].T), split(normed)))
        update = scale * product(split(reduce_ref[block]), split(hidden))
        return [update[:, i * LANES : (i + 1) * LANES] for i in range(len(conv))]

    def tap(block, i, j):
        at = block * 11 + 3 * i + j
        return columns_ref[:, at : at + 1]

    views = [
        shifted(
            current[r],
            pltpu.roll(left, (LANES - 2 * r - 1) % LANES, 1),
            pltpu.roll(right, (cols - 1 - 2 * r) % LANES, 1),
        )
        for r in range(wide)
    ]
    conv = []
    for r in range(1, wide - 1):
        conv.append(sum(tap(0, i, j) * views[r + i - 1][j] for i in range(3) for j in range(3)))
    side = jnp.zeros((channels, LANES), jnp.float32)
    for i in range(3):
        line = sum(tap(0, i, j) * beside[j] for j in range(3))
        side = side + (line if i == 1 else pltpu.roll(line, (2 - 2 * i) % LANES, 1))
    update = mixer(0, conv + [side])
    widened = [masks[r] * (current[r] + update[r - 1]) for r in range(1, wide - 1)]
    rim = beside_mask * (beside[1] + update[-1])

    views = [
        shifted(
            widened[r - 1],
            pltpu.roll(rim, (LANES - 2 * r) % LANES, 1),
            pltpu.roll(rim, (cols - 1 - half - 2 * r) % LANES, 1),
        )
        for r in range(1, wide - 1)
    ]
    conv = []
    for r in range(rows):
        conv.append(sum(tap(1, i, j) * views[r + i][j] for i in range(3) for j in range(3)))
    update = mixer(1, conv)
    for r in range(rows):
        out_ref[:, r, :] = masks[r + 2] * (widened[r + 1] + update[r])


def ocean_step(sums, up, down, left, right, ocean_state, land_mask, coupling, source, weight, columns, expand, reduce_w):
    return pl.pallas_call(
        ocean_kernel,
        out_shape=jax.ShapeDtypeStruct(ocean_state.shape, jnp.float32),
        compiler_params=params(60),
        name="ocean_step",
    )(
        sums,
        up,
        down,
        left,
        right,
        ocean_state,
        land_mask,
        jnp.repeat(coupling, 8, axis=1),
        source,
        weight,
        columns,
        expand,
        jnp.swapaxes(reduce_w, 1, 2),
    )


def depthwise(field, taps):
    height = field.shape[1] - 2
    width = field.shape[2] - 2
    result = jnp.zeros((field.shape[0], height, width), jnp.float32)
    for row_off in range(3):
        for col_off in range(3):
            result = (
                result
                + taps[:, 3 * row_off + col_off][:, None, None]
                * field[:, row_off : row_off + height, col_off : col_off + width]
            )
    return result


def ocean_mixer(values, gain, expand, reduce_w):
    channels, height, width = values.shape
    flat = values.reshape(channels, height * width)
    centre = jnp.mean(flat, axis=0)
    spread = jnp.mean(flat * flat, axis=0) - centre * centre
    normed = (flat - centre) * lax.rsqrt(spread + EPSILON) * gain[:, None]
    hidden = jax.nn.gelu(jnp.einsum("cd,cp->dp", expand, normed, precision=FINE))
    update = jnp.einsum("dc,dp->cp", reduce_w, hidden, precision=FINE)
    return update.reshape(channels, height, width)


def fast_step(
    atmos_state,
    ocean_state,
    land_mask,
    spectral_filter,
    atmos_gain,
    flux_readout,
    surface_coupling,
    surface_readout,
    flux_coupling,
    atmos_row_source,
    atmos_row_weight,
    atmos_col_source,
    atmos_col_weight,
    ocean_row_source,
    ocean_row_weight,
    ocean_col_source,
    ocean_col_weight,
    depth_taps,
    block_gain,
    expand_weight,
    reduce_weight,
    layer_scale,
):
    channels, atm_rows, width = atmos_state.shape
    lat, groups = lax.axis_size("lat"), lax.axis_size(COLUMN)
    places = [lax.axis_index("lat"), lax.axis_index("members"), lax.axis_index(COLUMN)]
    place = jnp.stack(places).astype(jnp.int32)
    members = lax.axis_size("members")
    far = lat // 2
    row_source, row_weight = ocean_row_source.T, ocean_row_weight.T
    col_source, col_weight = ocean_col_source.T, ocean_col_weight.T

    flux, stats = channel_sums(atmos_state, flux_readout)
    up, down = lat_edges(flux, ocean_state, land_mask, row_source, row_weight)
    packed, came, token = {}, {}, up
    for shift in (far, *(j for j in range(1, lat) if j != far), 0):
        packed[shift] = pack_filter(spectral_filter, after(place, token), lat, members, shift)
        token = packed[shift]
    up = lax.ppermute(up, "lat", [(i, i + 1) for i in range(lat - 1)])
    down = lax.ppermute(down, "lat", [(i + 1, i) for i in range(lat - 1)])

    came[0] = packed[0]
    for shift in range(1, lat):
        came[shift] = sent(packed[shift], shift)
    stats = summed_over_columns(stats)
    fresh = [
        normed_pieces(atmos_state, stats, atmos_gain, place, lat, q) for q in range(CHUNKS)
    ]
    up, down = lax.optimization_barrier((up, down, fresh[0][0], fresh[-1][0]))[:2]
    sums = summed_over_columns(flux_rows(place, up, down, flux, row_source, row_weight))
    first, last = lon_sides(up, down, ocean_state, land_mask, col_source, col_weight)
    left = lax.ppermute(last, COLUMN, [(i, (i + 1) % groups) for i in range(groups)])
    right = lax.ppermute(first, COLUMN, [(i, (i - 1) % groups) for i in range(groups)])
    piece = surface_piece(
        place,
        up,
        down,
        left,
        right,
        ocean_state,
        surface_readout,
        jnp.concatenate([atmos_row_source.astype(jnp.float32), atmos_row_weight], axis=1),
        atmos_col_source.T,
        atmos_col_weight.T,
        ocean_state.shape[2] * groups,
        width,
    )
    atmos_next = forced(atmos_state, surface_coupling, summed_over_columns(piece))
    columns = jnp.concatenate([depth_taps, block_gain[..., None], layer_scale[..., None]], axis=2)
    ocean_next = ocean_step(
        sums,
        up,
        down,
        left,
        right,
        ocean_state,
        land_mask,
        flux_coupling,
        col_source,
        col_weight,
        jnp.concatenate([columns[0], columns[1]], axis=1),
        expand_weight,
        reduce_weight,
    )

    done = (atmos_next, ocean_next, fresh[0][0], fresh[-1][0])
    pieces, token = [], (came[far], done)
    for q in range(CHUNKS):
        pieces.append(dealt(lax.optimization_barrier((*fresh[q], token))[:lat]))
        token = pieces[q][far]
    came = lax.optimization_barrier((*(came[j] for j in range(lat)), done))[:lat]
    filters = swapped_filter(came)
    pieces = [dealt(filtered_pieces(pieces[q], *filters[q], place)) for q in range(CHUNKS)]
    for q in range(CHUNKS):
        atmos_next = joined(atmos_next, pieces[q], place, q)
    return (atmos_next, ocean_next)


def general_step(
    atmos_state,
    ocean_state,
    land_mask,
    spectral_filter,
    atmos_gain,
    flux_readout,
    surface_coupling,
    surface_readout,
    flux_coupling,
    atmos_row_source,
    atmos_row_weight,
    atmos_col_source,
    atmos_col_weight,
    ocean_row_source,
    ocean_row_weight,
    ocean_col_source,
    ocean_col_weight,
    depth_taps,
    block_gain,
    expand_weight,
    reduce_weight,
    layer_scale,
):
    channels, atm_rows, width_atm = atmos_state.shape
    ocean_channels, ocean_rows, ocean_cols = ocean_state.shape
    lat_place = lax.axis_index("lat")

    ocean_mask = land_mask.astype(jnp.float32)
    row_table = jnp.concatenate([ocean_row_source.astype(jnp.float32), ocean_row_weight], axis=1)
    col_table = jnp.concatenate([ocean_col_source.astype(jnp.float32), ocean_col_weight], axis=1)
    row_table = jnp.pad(row_table, ((0, 0), (0, ocean_cols - row_table.shape[1])))
    wide = jnp.concatenate([ocean_state, ocean_mask[None], row_table[None]], axis=0)
    wide = padded(wide, (("lat", 1),), 2)
    row_table = wide[-1, :, 0:4]
    col_table = jnp.pad(col_table.T, ((0, wide.shape[1] - 4), (0, 0)))
    wide = jnp.concatenate([wide[:-1], col_table[None]], axis=0)
    wide = padded(wide, ((COLUMN, 2),), 2)
    col_table = wide[-1, 0:4].T
    state_wide, mask_wide = wide[:ocean_channels], wide[ocean_channels]

    partial_flux = jnp.einsum("fc,chw->fhw", flux_readout, atmos_state, precision=PRECISE)
    sums = jnp.concatenate(
        [
            partial_flux,
            jnp.sum(atmos_state, axis=0)[None],
            jnp.sum(atmos_state * atmos_state, axis=0)[None],
        ],
        axis=0,
    )
    sums = summed_over_columns(sums)
    flux, stats = sums[:-2], sums[-2:]

    surface_wide = jnp.einsum("sc,chw->shw", surface_readout, state_wide, precision=PRECISE)
    row_map = regrid_matrix(
        atmos_row_source, atmos_row_weight, lat_place * ocean_rows - 2, ocean_rows + 4, 0
    )
    col_map = regrid_matrix(
        atmos_col_source,
        atmos_col_weight,
        lax.axis_index(COLUMN) * ocean_cols - 2,
        ocean_cols + 4,
        ocean_cols * lax.axis_size(COLUMN),
    )
    atmos_piece = apply_maps(surface_wide, row_map, col_map)
    fields = lax.all_gather(atmos_piece, COLUMN, axis=2, tiled=True)

    centre = stats[0] / CA
    spread = stats[1] / CA - centre * centre
    normed = (atmos_state - centre) * lax.rsqrt(spread + EPSILON) * atmos_gain[:, None, None]
    filtered = global_filter(normed, spectral_filter)
    forcing = jnp.einsum("cs,shw->chw", surface_coupling, fields, precision=PRECISE)
    atmos_next = atmos_state + filtered + forcing

    before, behind = flux_reach(atm_rows, ocean_rows)
    flux_wide = rows_around(flux, before, behind)
    row_back = regrid_matrix(
        row_table[:, 0:2].astype(jnp.int32),
        row_table[:, 2:4],
        lat_place * atm_rows - before,
        atm_rows + before + behind,
        0,
    )
    col_back = regrid_matrix(
        col_table[:, 0:2].astype(jnp.int32), col_table[:, 2:4], 0, width_atm, 0
    )
    flux_ocean = apply_maps(flux_wide, row_back, col_back)
    current = mask_wide * (
        state_wide + jnp.einsum("cf,fhw->chw", flux_coupling, flux_ocean, precision=PRECISE)
    )
    update = ocean_mixer(
        depthwise(current, depth_taps[0]), block_gain[0], expand_weight[0], reduce_weight[0]
    )
    widened = mask_wide[1:-1, 1:-1] * (
        current[:, 1:-1, 1:-1] + layer_scale[0][:, None, None] * update
    )
    update = ocean_mixer(
        depthwise(widened, depth_taps[1]), block_gain[1], expand_weight[1], reduce_weight[1]
    )
    current = ocean_mask * (widened[:, 1:-1, 1:-1] + layer_scale[1][:, None, None] * update)
    return (atmos_next, current)


def body(*arrays):
    atmos_state, ocean_state, _, spectral_filter = arrays[:4]
    channels, atm_rows, width = atmos_state.shape
    lat, members, groups = (lax.axis_size(a) for a in ("lat", "members", COLUMN))
    freqs, height = spectral_filter.shape[2:]
    fast = can_deal(channels, atm_rows, width, freqs, height, lat, members) and can_tile(
        *ocean_state.shape, atm_rows, groups
    )
    return fast_step(*arrays) if fast else general_step(*arrays)


def solution(mesh):
    return jax.shard_map(
        body,
        mesh=mesh,
        in_specs=(
            P(("members", "lon", "chan"), "lat", None),
            P("members", "lat", ("lon", "chan")),
            P("lat", ("lon", "chan")),
            P(None, ("lon", "chan"), "lat", None),
            P(("lon", "chan")),
            P(None, ("lon", "chan")),
            P(("lon", "chan"), None),
            P(),
            P(),
            P("lat", None),
            P("lat", None),
            P(("lon", "chan"), None),
            P(("lon", "chan"), None),
            P("lat", None),
            P("lat", None),
            P(("lon", "chan"), None),
            P(("lon", "chan"), None),
            P(),
            P(),
            P(),
            P(),
            P(),
        ),
        out_specs=(
            P(("members", "lon", "chan"), "lat", None),
            P("members", "lat", ("lon", "chan")),
        ),
        check_vma=False,
    )
```

```python
import functools
import math

import jax
import jax.numpy as jnp
import ml_dtypes
import numpy as np
from jax import lax
from jax.experimental import pallas as pl
from jax.experimental.pallas import tpu as pltpu
from jax.sharding import PartitionSpec as P

CA = 384


EPSILON = 1e-05
PRECISE = lax.Precision.HIGHEST
FINE = lax.Precision.HIGH
LANES = 128
CHUNKS = 2
COLUMN = ("lon", "chan")
REACH = 16
STREAMS = 4


def padded(x, sides, width):
    for axis, dim in sides:
        count, length = (lax.axis_size(axis), x.shape[dim])
        up = [(i, (i + 1) % count) for i in range(count)]
        down = [(j, i) for i, j in up]
        last = lax.slice_in_dim(x, length - width, length, axis=dim)
        leading = lax.slice_in_dim(x, 0, width, axis=dim)
        before = lax.ppermute(last, axis, up)
        after = lax.ppermute(leading, axis, down)
        x = jnp.concatenate([before, x, after], axis=dim)
    return x


def fourier_tables(length):
    places = jnp.arange(length, dtype=jnp.int32)
    angles = (
        2.0
        * math.pi
        / length
        * jnp.mod(places[:, None] * places[None, :], length).astype(jnp.float32)
    )
    return (jnp.cos(angles), jnp.sin(angles))


def regrid_matrix(source, weight, offset, span, period):
    shares = weight / jnp.sum(weight, axis=1, keepdims=True)
    relative = source - offset
    if period > 0:
        relative = jnp.mod(relative, period)
    columns = jnp.arange(span, dtype=jnp.int32)[None, :]
    return shares[:, 0:1] * (relative[:, 0:1] == columns).astype(jnp.float32) + shares[:, 1:2] * (
        relative[:, 1:2] == columns
    ).astype(jnp.float32)


def apply_maps(field, row_map, col_map):
    by_rows = jnp.einsum("jh,shw->sjw", row_map, field, precision=PRECISE)
    return jnp.einsum("sjw,kw->sjk", by_rows, col_map, precision=PRECISE)


def grid_rims(field):
    return padded(field, (("lat", 1), (("lon", "chan"), 2)), 2)


def along_last(field, table):
    return jnp.einsum("ckh,hm->ckm", field, table, precision=PRECISE)


def global_filter(normed, spectral_filter):
    width_len = normed.shape[2]
    height_len = spectral_filter.shape[3]
    cos_w, sin_w = fourier_tables(width_len)
    cos_h, sin_h = fourier_tables(height_len)
    real_w = jnp.einsum("chn,nk->ckh", normed, cos_w, precision=PRECISE)
    imag_w = -jnp.einsum("chn,nk->ckh", normed, sin_w, precision=PRECISE)
    real_w, imag_w = (
        lax.all_to_all(real_w, "lat", split_axis=1, concat_axis=2, tiled=True),
        lax.all_to_all(imag_w, "lat", split_axis=1, concat_axis=2, tiled=True),
    )
    real_s = along_last(real_w, cos_h) + along_last(imag_w, sin_h)
    imag_s = along_last(imag_w, cos_h) - along_last(real_w, sin_h)
    kern_real = spectral_filter[0]
    kern_imag = spectral_filter[1]
    real_f = kern_real * real_s - kern_imag * imag_s
    imag_f = kern_real * imag_s + kern_imag * real_s
    real_b = (along_last(real_f, cos_h) - along_last(imag_f, sin_h)) / height_len
    imag_b = (along_last(imag_f, cos_h) + along_last(real_f, sin_h)) / height_len
    real_b, imag_b = (
        lax.all_to_all(real_b, "lat", split_axis=2, concat_axis=1, tiled=True),
        lax.all_to_all(imag_b, "lat", split_axis=2, concat_axis=1, tiled=True),
    )
    back = jnp.einsum("ckh,kn->chn", real_b, cos_w, precision=PRECISE) - jnp.einsum(
        "ckh,kn->chn", imag_b, sin_w, precision=PRECISE
    )
    return back / width_len


def flux_reach(atm_rows, ocean_rows):
    first = (-2 * atm_rows) // ocean_rows - 1
    last = (atm_rows * (ocean_rows + 1)) // ocean_rows + 2
    return -first, max(last - atm_rows + 1, 0)


def rows_around(field, before, behind):
    count = lax.axis_size("lat")
    up = [(i, i + 1) for i in range(count - 1)]
    down = [(i + 1, i) for i in range(count - 1)]
    rows = field.shape[1]
    above = lax.ppermute(field[:, rows - before :], "lat", up)
    below = lax.ppermute(field[:, :behind], "lat", down)
    return jnp.concatenate([above, field, below], axis=1)


def params(mib):
    return pltpu.CompilerParams(vmem_limit_bytes=mib * 2**20)


def can_deal(channels, rows, width, freqs, height, lat, members):
    return (
        members == 2
        and lat == 4
        and channels % (lat * CHUNKS * members) == 0
        and channels % STREAMS == 0
        and rows % 8 == 0
        and rows * lat == height
        and width % LANES == 0
        and freqs * lat == width
        and freqs == 96
        and height % 32 == 0
    )


def split_table(table):
    high = table.astype(ml_dtypes.bfloat16)
    low = (table - high.astype(np.float64)).astype(ml_dtypes.bfloat16)
    return high, low


@functools.lru_cache(maxsize=None)
def dealt_tables(height, width, lat):
    freqs = width // lat
    angle = 2.0 * np.pi / height * (np.outer(np.arange(height), np.arange(height)) % height)
    cos_h, sin_h = np.cos(angle), np.sin(angle)
    rows_on = np.block([[cos_h, sin_h], [-sin_h, cos_h]])
    rows_back = np.block([[cos_h, -sin_h], [sin_h, cos_h]])
    cols_on = np.zeros((lat, width, 2, lat, LANES))
    for z in range(lat):
        for j in range(lat):
            k = (z + j) % lat * freqs + np.arange(freqs)
            turn = 2.0 * np.pi / width * (np.outer(np.arange(width), k) % width)
            cols_on[z, :, 0, j, :freqs] = np.cos(turn)
            cols_on[z, :, 1, j, :freqs] = -np.sin(turn)
    cols_on = cols_on.reshape(lat, width, 2 * lat * LANES)
    cols_back = np.swapaxes(cols_on, 1, 2) / (height * width)
    return [split_table(t) for t in (cols_on, rows_on, rows_back, cols_back)]


def pack_kernel(place_ref, filter_ref, out_ref):
    _, channels, freqs, rows = filter_ref.shape
    main, rest = rows * 3 // 4, rows // 4
    for part in range(2):
        for c in range(channels):
            turned = filter_ref[part, c].T
            out_ref[0, part, c, :, 0:freqs] = turned[0:main]
            for i in range(3):
                out_ref[0, part, c, i * rest : (i + 1) * rest, freqs:LANES] = turned[
                    main:, 32 * i : 32 * (i + 1)
                ]


def pack_filter(spectral_filter, place, lat, members, shift):
    _, channels, freqs, height = spectral_filter.shape
    half = channels // (lat * CHUNKS * members)

    def source(q, place):
        dest = place[0] ^ shift
        return (0, (dest * CHUNKS + q) * members + place[1], 0, 0)

    shape = (CHUNKS, 2, half, height * 3 // 4, LANES)
    return pl.pallas_call(
        pack_kernel,
        grid_spec=pltpu.PrefetchScalarGridSpec(
            num_scalar_prefetch=1,
            grid=(CHUNKS,),
            in_specs=[pl.BlockSpec((2, half, freqs, height), source)],
            out_specs=pl.BlockSpec((1, *shape[1:]), lambda q, place: (q, 0, 0, 0, 0)),
        ),
        out_shape=jax.ShapeDtypeStruct(shape, jnp.float32),
        compiler_params=params(60),
        cost_estimate=pl.CostEstimate(flops=1, bytes_accessed=1, transcendentals=0),
        name="pack_filter",
    )(place, spectral_filter)


def sums_kernel(readout_ref, *refs):
    parts, (flux_ref, stats_ref) = refs[:STREAMS], refs[STREAMS:]
    channels, tile, width = parts[0].shape
    fluxes = readout_ref.shape[0]
    totals = (jnp.zeros((tile, width), jnp.float32),) * (fluxes + 2)
    for i, part in enumerate(parts):

        def add(c, totals, i=i, part=part):
            value = part[c]
            new = [totals[f] + readout_ref[f, i * channels + c] * value for f in range(fluxes)]
            return (*new, totals[fluxes] + value, totals[fluxes + 1] + value * value)

        totals = lax.fori_loop(0, channels, add, totals, unroll=8)
    for i in range(fluxes):
        flux_ref[i] = totals[i]
    stats_ref[0] = totals[fluxes]
    stats_ref[1] = totals[fluxes + 1]


def channel_sums(atmos_state, flux_readout):
    channels, rows, width = atmos_state.shape
    counts = (flux_readout.shape[0], 2)
    return pl.pallas_call(
        sums_kernel,
        grid=(rows // 8,),
        in_specs=[pl.BlockSpec(memory_space=pltpu.SMEM)]
        + [
            pl.BlockSpec((channels // STREAMS, 8, width), lambda i, s=s: (s, i, 0))
            for s in range(STREAMS)
        ],
        out_specs=[pl.BlockSpec((n, 8, width), lambda i: (0, i, 0)) for n in counts],
        out_shape=[jax.ShapeDtypeStruct((n, rows, width), jnp.float32) for n in counts],
        compiler_params=params(60),
        cost_estimate=pl.CostEstimate(flops=1, bytes_accessed=1, transcendentals=0),
        name="channel_sums",
    )(flux_readout, *[atmos_state] * STREAMS)


def norm_kernel(count, chunk, place_ref, gain_ref, sums_ref, state_ref, *out_refs):
    step = pl.program_id(0)
    part = state_ref.shape[0]
    first = ((place_ref[0] ^ step) * CHUNKS + chunk) * part
    centre = sums_ref[0] / CA
    spread = sums_ref[1] / CA - centre * centre
    scale = lax.rsqrt(spread + EPSILON)
    for j in range(count):

        @pl.when(step == j)
        def _(out=out_refs[j]):
            for c in range(part):
                out[c] = (state_ref[c] - centre) * scale * gain_ref[first + c]


def normed_pieces(atmos_state, sums, gain, place, lat, chunk):
    channels, rows, width = atmos_state.shape
    part = channels // (lat * CHUNKS)
    return pl.pallas_call(
        functools.partial(norm_kernel, lat, chunk),
        grid_spec=pltpu.PrefetchScalarGridSpec(
            num_scalar_prefetch=1,
            grid=(lat,),
            in_specs=[
                pl.BlockSpec(memory_space=pltpu.SMEM),
                pl.BlockSpec(sums.shape, lambda j, place: (0, 0, 0)),
                pl.BlockSpec(
                    (part, rows, width),
                    lambda j, place: ((place[0] ^ j) * CHUNKS + chunk, 0, 0),
                ),
            ],
            out_specs=[pl.BlockSpec((part, rows, width), lambda j, place: (0, 0, 0))] * lat,
        ),
        out_shape=[jax.ShapeDtypeStruct((part, rows, width), jnp.float32)] * lat,
        compiler_params=params(60),
        name="normed_pieces",
    )(place, gain, sums, atmos_state)


def split(value):
    high = value.astype(jnp.bfloat16)
    return high, (value - high.astype(jnp.float32)).astype(jnp.bfloat16)


def product(left, right):
    dot = functools.partial(jnp.dot, preferred_element_type=jnp.float32)
    return dot(left[0], right[0]) + (dot(left[0], right[1]) + dot(left[1], right[0]))


def unpacked(packed_ref, order, part, c):
    blocks = []
    lane = lax.broadcasted_iota(jnp.int32, (packed_ref.shape[3] // 3, LANES), 1)
    rest = packed_ref.shape[3] // 3
    for j in order:
        main = packed_ref[j, part, c]
        a, b, d = (
            pltpu.roll(main[i * rest : (i + 1) * rest], 32 * (i + 1), 1) for i in range(3)
        )
        tail = jnp.where(lane < 32, a, jnp.where(lane < 64, b, d))
        blocks.append(jnp.concatenate([main, tail], axis=0))
    return jnp.concatenate(blocks, axis=1)


def spectral_kernel(count, place_ref, *refs):
    pieces = refs[:count]
    own_ref, other_ref = refs[count : count + 2]
    tables = [(refs[count + 2 + 2 * i], refs[count + 3 + 2 * i]) for i in range(4)]
    outs = refs[count + 10 : 2 * count + 10]
    high_ref, low_ref = refs[2 * count + 10 :]
    part, rows, width = pieces[0].shape
    height = rows * count
    span = count * LANES
    cols_on, rows_on, rows_back, cols_back = tables
    cols_on = (cols_on[0][0], cols_on[1][0])
    cols_back = (cols_back[0][0], cols_back[1][0])
    rows_on = (rows_on[0][...], rows_on[1][...])
    rows_back = (rows_back[0][...], rows_back[1][...])

    odd = lax.rem(place_ref[0], 2) == 1
    order = [0, jnp.where(odd, 3, 1), 2, jnp.where(odd, 1, 3)]

    def ordered(values):
        return [
            values[0],
            jnp.where(odd, values[3], values[1]),
            values[2],
            jnp.where(odd, values[1], values[3]),
        ]

    def run(filter_ref):
        lines = ordered([p[...].reshape(part * rows, width) for p in pieces])
        stacked = jnp.concatenate(lines, axis=0)
        spectra = product(split(stacked), cols_on)
        for c in range(part):
            own = jnp.concatenate(
                [spectra[(j * part + c) * rows : (j * part + c + 1) * rows] for j in range(count)],
                axis=0,
            )
            both = jnp.concatenate([own[:, :span], own[:, span:]], axis=0)
            full = product(rows_on, split(both))
            real, imag = full[:height], full[height:]
            kern_real = unpacked(filter_ref, order, 0, c)
            kern_imag = unpacked(filter_ref, order, 1, c)
            both = jnp.concatenate(
                [kern_real * real - kern_imag * imag, kern_real * imag + kern_imag * real], axis=0
            )
            back = product(rows_back, split(both))
            high, low = split(back)
            at = slice(c * height, (c + 1) * height)
            high_ref[at, :span] = high[:height]
            high_ref[at, span:] = high[height:]
            low_ref[at, :span] = low[:height]
            low_ref[at, span:] = low[height:]
        result = product((high_ref[...], low_ref[...]), cols_back)
        result = result.reshape(part, height, width)
        parts = ordered([result[:, j * rows : (j + 1) * rows] for j in range(count)])
        for out, value in zip(outs, parts):
            out[...] = value

    @pl.when(pl.program_id(0) == 0)
    def _():
        run(own_ref)

    @pl.when(pl.program_id(0) == 1)
    def _():
        run(other_ref)


def filtered_pieces(pieces, own, other, place):
    lat = len(pieces)
    chunk, rows, width = pieces[0].shape
    half = chunk // 2
    height = rows * lat
    tables = [t for pair in dealt_tables(height, width, lat) for t in pair]

    def mine(i, place):
        return (lax.rem(i + place[1], 2), 0, 0)

    def table_spec(t):
        if t.ndim == 3:
            return pl.BlockSpec((1, *t.shape[1:]), lambda i, place: (place[0], 0, 0))
        return pl.BlockSpec(t.shape, lambda i, place: (0, 0))

    filter_spec = pl.BlockSpec(own.shape, lambda i, place: (0, 0, 0, 0, 0))
    piece_spec = pl.BlockSpec((half, rows, width), mine)
    return pl.pallas_call(
        functools.partial(spectral_kernel, lat),
        grid_spec=pltpu.PrefetchScalarGridSpec(
            num_scalar_prefetch=1,
            grid=(2,),
            in_specs=[piece_spec] * lat + [filter_spec] * 2 + [table_spec(t) for t in tables],
            out_specs=[piece_spec] * lat,
            scratch_shapes=[pltpu.VMEM((half * height, 2 * lat * LANES), jnp.bfloat16)] * 2,
        ),
        out_shape=[jax.ShapeDtypeStruct((chunk, rows, width), jnp.float32)] * lat,
        compiler_params=params(60),
        name="filtered_pieces",
    )(place, *pieces, own, other, *[jnp.asarray(t) for t in tables])


def forced_kernel(coupling_ref, fields_ref, state_ref, out_ref):
    fields = [fields_ref[s] for s in range(fields_ref.shape[0])]

    @pl.loop(0, state_ref.shape[0], unroll=4)
    def _(c):
        value = state_ref[c]
        for s, field in enumerate(fields):
            value = value + coupling_ref[c, s] * field
        out_ref[c] = value


def forced(atmos_state, coupling, fields):
    channels, rows, width = atmos_state.shape
    block = pl.BlockSpec((channels, 8, width), lambda i: (0, i, 0))
    return pl.pallas_call(
        forced_kernel,
        grid=(rows // 8,),
        in_specs=[
            pl.BlockSpec(memory_space=pltpu.SMEM),
            pl.BlockSpec((fields.shape[0], 8, width), lambda i: (0, i, 0)),
            block,
        ],
        out_specs=block,
        out_shape=jax.ShapeDtypeStruct(atmos_state.shape, jnp.float32),
        compiler_params=params(60),
        name="forced",
    )(coupling, fields, atmos_state)


def join_kernel(count, chunk, place_ref, state_ref, *refs):
    pieces = refs[:count]
    out_ref, held, added, in_sems, piece_sems, out_sems = refs[count:]
    part = held.shape[1]
    starts = [((place_ref[0] ^ j) * CHUNKS + chunk) * part for j in range(count)]
    incoming, others, outgoing = [], [], []
    for j in range(count):
        here = pl.ds(starts[j], part)
        incoming.append(pltpu.make_async_copy(state_ref.at[here], held.at[j], in_sems.at[j]))
        others.append(pltpu.make_async_copy(pieces[j], added.at[j], piece_sems.at[j]))
        outgoing.append(pltpu.make_async_copy(held.at[j], out_ref.at[here], out_sems.at[j]))
    for copy in incoming + others:
        copy.start()
    for j in range(count):
        incoming[j].wait()
        others[j].wait()
        held[j] = held[j] + added[j]
        outgoing[j].start()
    for copy in outgoing:
        copy.wait()


def joined(state, pieces, place, chunk):
    lat = len(pieces)
    part, rows, width = pieces[0].shape
    hbm = pl.BlockSpec(memory_space=pl.ANY)
    return pl.pallas_call(
        functools.partial(join_kernel, lat, chunk),
        in_specs=[pl.BlockSpec(memory_space=pltpu.SMEM)] + [hbm] * (lat + 1),
        out_specs=hbm,
        out_shape=jax.ShapeDtypeStruct(state.shape, jnp.float32),
        scratch_shapes=[pltpu.VMEM((lat, part, rows, width), jnp.float32)] * 2
        + [pltpu.SemaphoreType.DMA((lat,))] * 3,
        input_output_aliases={1: 0},
        compiler_params=params(60),
        cost_estimate=pl.CostEstimate(flops=1, bytes_accessed=1, transcendentals=0),
        name="joined",
    )(place, state, *pieces)


def sent(piece, step):
    lat = lax.axis_size("lat")
    return lax.ppermute(piece, "lat", [(i, i ^ step) for i in range(lat)])


def dealt(pieces):
    return [pieces[0]] + [sent(pieces[j], j) for j in range(1, len(pieces))]


def after(value, earlier):
    return lax.optimization_barrier((value, earlier))[0]


def swapped_filter(pieces):
    members = lax.axis_size("members")
    halves = [jnp.stack([p[q] for p in pieces]) for q in range(CHUNKS)]
    return [
        (own, lax.ppermute(own, "members", [(i, (i + 1) % members) for i in range(members)]))
        for own in halves
    ]


def summed_over_columns(x):
    for axis in ("chan", "lon"):
        count = lax.axis_size(axis)
        total = x
        for shift in range(1, count):
            total = total + lax.ppermute(x, axis, [(i, (i + shift) % count) for i in range(count)])
        x = total
    return x


def can_tile(ocean_channels, ocean_rows, ocean_cols, atm_rows, groups):
    before, behind = flux_reach(atm_rows, ocean_rows)
    return (
        ocean_cols == LANES
        and ocean_channels % 8 == 0
        and ocean_rows == 4
        and atm_rows % 8 == 0
        and max(before, behind) <= REACH <= atm_rows
        and groups > 1
    )


def exact(left, right):
    return jnp.dot(left, right, precision=PRECISE, preferred_element_type=jnp.float32)


def iota(shape, dim):
    return lax.broadcasted_iota(jnp.int32, shape, dim)


def table_row(source, weight, row):
    lane = iota((1, LANES), 1)
    values = [
        source[0:1, row : row + 1].astype(jnp.float32),
        source[1:2, row : row + 1].astype(jnp.float32),
        weight[0:1, row : row + 1],
        weight[1:2, row : row + 1],
    ]
    out = jnp.zeros((1, LANES), jnp.float32)
    for i, value in enumerate(values):
        out = jnp.where(lane == i, value, out)
    return out


def stacked_rows(rows):
    at = iota((8, rows[0].shape[1]), 0)
    tile = jnp.zeros((8, rows[0].shape[1]), jnp.float32)
    for i, row in enumerate(rows):
        tile = jnp.where(at == i, row, tile)
    return tile


def edges_kernel(flux_ref, state_ref, mask_ref, source_ref, weight_ref, *out_refs):
    fluxes, atm_rows, width = flux_ref.shape
    channels, rows, _ = state_ref.shape
    span = channels + 8
    source, weight = source_ref[...], weight_ref[...]
    for out, first, atm_first in (
        (out_refs[0], rows - 2, atm_rows - REACH),
        (out_refs[1], 0, 0),
    ):
        for i in range(2):
            row = first + i
            out[i * span : i * span + channels] = state_ref[:, row, :]
            out[i * span + channels : (i + 1) * span] = stacked_rows(
                [mask_ref[row : row + 1, :].astype(jnp.float32), table_row(source, weight, row)]
            )
        at = 2 * span
        for f in range(fluxes):
            for lanes in range(0, width, LANES):
                out[at : at + REACH] = flux_ref[f, atm_first : atm_first + REACH, lanes : lanes + LANES]
                at += REACH


def lat_edges(flux, ocean_state, land_mask, source, weight):
    fluxes, _, width = flux.shape
    channels = ocean_state.shape[0]
    shape = (2 * (channels + 8) + fluxes * width // LANES * REACH, LANES)
    return pl.pallas_call(
        edges_kernel,
        out_shape=[jax.ShapeDtypeStruct(shape, jnp.float32)] * 2,
        compiler_params=params(60),
        name="lat_edges",
    )(flux, ocean_state, land_mask, source, weight)


def rows_kernel(place_ref, up_ref, down_ref, flux_ref, source_ref, weight_ref, out_ref):
    fluxes, atm_rows, width = flux_ref.shape
    rows = source_ref.shape[1]
    span = (up_ref.shape[0] - fluxes * width // LANES * REACH) // 2
    source, weight = source_ref[...], weight_ref[...]
    at = span - 7
    table = stacked_rows(
        [up_ref[at : at + 1], up_ref[span + at : span + at + 1]]
        + [table_row(source, weight, r) for r in range(rows)]
        + [down_ref[at : at + 1], down_ref[span + at : span + at + 1]]
    )
    first = place_ref[0] * atm_rows - REACH
    reach = atm_rows + 2 * REACH
    spot = (iota((8, reach), 1) + first).astype(jnp.float32)
    total = table[:, 2:3] + table[:, 3:4]
    total = jnp.where(total > 0.0, total, 1.0)
    picks = jnp.where(spot == table[:, 0:1], table[:, 2:3] / total, 0.0) + jnp.where(
        spot == table[:, 1:2], table[:, 3:4] / total, 0.0
    )
    tiles = width // LANES
    for f in range(fluxes):
        parts = []
        for ref in (up_ref, down_ref):
            at = 2 * span + f * tiles * REACH
            parts.append(
                jnp.concatenate(
                    [ref[at + i * REACH : at + (i + 1) * REACH] for i in range(tiles)], axis=1
                )
            )
        field = jnp.concatenate([parts[0], flux_ref[f], parts[1]], axis=0)
        out_ref[f * 8 : (f + 1) * 8] = exact(picks, field)


def flux_rows(place, up, down, flux, source, weight):
    fluxes, atm_rows, width = flux.shape
    vmem = pl.BlockSpec(memory_space=pltpu.VMEM)
    return pl.pallas_call(
        rows_kernel,
        in_specs=[pl.BlockSpec(memory_space=pltpu.SMEM)] + [vmem] * 5,
        out_specs=vmem,
        out_shape=jax.ShapeDtypeStruct((8 * fluxes, width), jnp.float32),
        compiler_params=params(60),
        name="flux_rows",
    )(place, up, down, flux, source, weight)


def row_tile(r, rows, span, up_ref, down_ref, state_ref):
    channels = span - 8
    if r < 2:
        return up_ref[r * span : r * span + channels]
    if r < rows + 2:
        return state_ref[:, r - 2, :]
    return down_ref[(r - rows - 2) * span : (r - rows - 2) * span + channels]


def mask_row(r, rows, span, up_ref, down_ref, mask_ref):
    channels = span - 8
    if r < 2:
        return up_ref[r * span + channels : r * span + channels + 1]
    if r < rows + 2:
        return mask_ref[r - 2 : r - 1, :].astype(jnp.float32)
    at = (r - rows - 2) * span + channels
    return down_ref[at : at + 1]


def sides_kernel(up_ref, down_ref, state_ref, mask_ref, source_ref, weight_ref, first_ref, last_ref):
    channels, rows, _ = state_ref.shape
    span = channels + 8
    lane = iota((1, LANES), 1)
    first = jnp.zeros((channels, LANES), jnp.float32)
    last = jnp.zeros((channels, LANES), jnp.float32)
    first_mask = jnp.zeros((1, LANES), jnp.float32)
    last_mask = jnp.zeros((1, LANES), jnp.float32)
    for r in range(rows + 4):
        tile = row_tile(r, rows, span, up_ref, down_ref, state_ref)
        mask = mask_row(r, rows, span, up_ref, down_ref, mask_ref)
        here = (lane >= 2 * r) & (lane < 2 * r + 2)
        first = jnp.where(here, pltpu.roll(tile, 2 * r, 1), first)
        last = jnp.where(here, pltpu.roll(tile, 2 * r + 2, 1), last)
        first_mask = jnp.where(here, turned(mask, 2 * r), first_mask)
        last_mask = jnp.where(here, turned(mask, 2 * r + 2), last_mask)
    first_ref[0:channels] = first
    last_ref[0:channels] = last
    source = source_ref[...].astype(jnp.float32)
    weight = weight_ref[...]
    table = [source[0:1], source[1:2], weight[0:1], weight[1:2]]
    first_ref[channels:span] = stacked_rows([first_mask] + table)
    last_ref[channels:span] = stacked_rows([last_mask] + [turned(t, 2) for t in table])


def turned(row, shift):
    return pltpu.roll(jnp.broadcast_to(row, (8, row.shape[1])), shift, 1)[0:1]


def lon_sides(up, down, ocean_state, land_mask, source, weight):
    shape = (ocean_state.shape[0] + 8, LANES)
    return pl.pallas_call(
        sides_kernel,
        out_shape=[jax.ShapeDtypeStruct(shape, jnp.float32)] * 2,
        compiler_params=params(60),
        name="lon_sides",
    )(up, down, ocean_state, land_mask, source, weight)


def surface_kernel(
    place_ref,
    period,
    up_ref,
    down_ref,
    left_ref,
    right_ref,
    state_ref,
    readout_ref,
    row_ref,
    source_ref,
    weight_ref,
    out_ref,
    lines_ref,
):
    channels, rows, cols = state_ref.shape
    span = channels + 8
    fields, atm_rows, width = out_ref.shape
    atm_cols = source_ref.shape[1]
    readout = readout_ref[...]
    lines_ref[...] = jnp.zeros_like(lines_ref)
    for r in range(rows + 4):
        tile = row_tile(r, rows, span, up_ref, down_ref, state_ref)
        lines_ref[r * 8 : r * 8 + fields] = exact(readout, tile)
    lines = lines_ref[...]
    sides = [exact(readout, ref[0:channels]) for ref in (left_ref, right_ref)]

    table = row_ref[...]
    total = table[:, 2:3] + table[:, 3:4]
    shares = (table[:, 2:3] / total, table[:, 3:4] / total)
    start = (place_ref[0] * rows - 2).astype(jnp.float32)
    sources = (table[:, 0:1] - start, table[:, 1:2] - start)

    def row_picks(row):
        row = row.astype(jnp.float32)
        return jnp.where(row == sources[0], shares[0], 0.0) + jnp.where(row == sources[1], shares[1], 0.0)

    source, weight = source_ref[...], weight_ref[...]
    total = weight[0:1] + weight[1:2]
    relative = source - (place_ref[2] * cols - 2)
    relative = jnp.where(relative < 0, relative + period, relative)
    relative = jnp.where(relative >= period, relative - period, relative)

    def col_picks(col):
        return jnp.where(col == relative[0:1], weight[0:1] / total, 0.0) + jnp.where(
            col == relative[1:2], weight[1:2] / total, 0.0
        )

    at = iota((LANES, atm_cols), 0)
    main = col_picks(at + 2)
    side = [col_picks((at & 1)), col_picks(cols + 2 + (at & 1))]
    spread = iota((atm_cols, width), 1) - place_ref[2] * atm_cols == iota((atm_cols, width), 0)
    spread = spread.astype(jnp.float32)
    lane = iota((atm_rows, 8 * (rows + 4)), 1)
    side_lane = iota((atm_rows, LANES), 1)
    side_rows = row_picks(side_lane >> 1)
    for s in range(fields):
        picks = jnp.where((lane & 7) == s, row_picks(lane >> 3), 0.0)
        piece = exact(exact(picks, lines), main)
        for i in range(2):
            piece = piece + exact(side_rows * sides[i][s : s + 1], side[i])
        out_ref[s] = exact(piece, spread)


def surface_piece(place, up, down, left, right, ocean_state, readout, row_table, source, weight, period, width):
    rows = ocean_state.shape[1]
    vmem = pl.BlockSpec(memory_space=pltpu.VMEM)
    shape = (readout.shape[0], row_table.shape[0], width)
    return pl.pallas_call(
        lambda place_ref, *refs: surface_kernel(place_ref, period, *refs),
        in_specs=[pl.BlockSpec(memory_space=pltpu.SMEM)] + [vmem] * 9,
        out_specs=vmem,
        out_shape=jax.ShapeDtypeStruct(shape, jnp.float32),
        scratch_shapes=[pltpu.VMEM((8 * (rows + 4), LANES), jnp.float32)],
        compiler_params=params(60),
        name="surface_piece",
    )(place, up, down, left, right, ocean_state, readout, row_table, source, weight)


def ocean_kernel(
    sums_ref,
    up_ref,
    down_ref,
    left_ref,
    right_ref,
    state_ref,
    mask_ref,
    coupling_ref,
    source_ref,
    weight_ref,
    columns_ref,
    expand_ref,
    reduce_ref,
    out_ref,
):
    channels, rows, cols = state_ref.shape
    span = channels + 8
    fluxes = coupling_ref.shape[1] // 8
    width = sums_ref.shape[1]
    wide = rows + 4
    lane = iota((1, LANES), 1)
    half = LANES // 2
    is_left = lane < half
    lines = sums_ref[0 : 8 * fluxes]
    coupling = coupling_ref[...]
    spot = iota((width, LANES), 0).astype(jnp.float32)

    def col_lines(s0, s1, w0, w1):
        total = w0 + w1
        total = jnp.where(total > 0.0, total, 1.0)
        return exact(
            lines, jnp.where(spot == s0, w0 / total, 0.0) + jnp.where(spot == s1, w1 / total, 0.0)
        )

    source, weight = source_ref[...].astype(jnp.float32), weight_ref[...]
    main_lines = col_lines(source[0:1], source[1:2], weight[0:1], weight[1:2])
    of_row = iota((channels, 8 * fluxes), 1) & 7

    current, masks = [], []
    for r in range(wide):
        forcing = exact(jnp.where(of_row == r, coupling, 0.0), main_lines)
        mask = mask_row(r, rows, span, up_ref, down_ref, mask_ref)
        masks.append(mask)
        current.append(mask * (row_tile(r, rows, span, up_ref, down_ref, state_ref) + forcing))

    def side_current(ref):
        table = ref[channels + 1 : channels + 5]
        side_lines = col_lines(table[0:1], table[1:2], table[2:3], table[3:4])
        spread = jnp.zeros((8 * fluxes, LANES), jnp.float32)
        at = iota((8 * fluxes, LANES), 0) & 7
        for r in range(wide):
            here = (at == r) & (lane >= 2 * r) & (lane < 2 * r + 2)
            spread = jnp.where(here, pltpu.roll(side_lines, 2 * r, 1), spread)
        mask = ref[channels : channels + 1]
        return mask, mask * (ref[0:channels] + exact(coupling, spread))

    left_mask, left = side_current(left_ref)
    right_mask, right = side_current(right_ref)
    inner = [jnp.zeros((channels, LANES), jnp.float32)] * 2
    for r in range(wide):
        inner[0] = jnp.where(lane == 2 * r, pltpu.roll(current[r], 2 * r, 1), inner[0])
        inner[1] = jnp.where(
            lane == half + 2 * r, pltpu.roll(current[r], (half + 2 * r + 1) % LANES, 1), inner[1]
        )
    beside = [
        jnp.where(is_left, left, inner[1]),
        jnp.where(is_left, pltpu.roll(left, LANES - 1, 1), pltpu.roll(right, half, 1)),
        jnp.where(is_left, inner[0], pltpu.roll(right, half - 1, 1)),
    ]
    beside_mask = jnp.where(is_left, turned(left_mask, LANES - 1), turned(right_mask, half))

    def shifted(tile, before, behind):
        return [
            jnp.where(lane == 0, before, pltpu.roll(tile, 1, 1)),
            tile,
            jnp.where(lane == cols - 1, behind, pltpu.roll(tile, cols - 1, 1)),
        ]

    def mixer(block, conv):
        base = block * 11
        gain = columns_ref[:, base + 9 : base + 10]
        scale = columns_ref[:, base + 10 : base + 11]
        points = jnp.concatenate(conv, axis=1)
        centre = jnp.mean(points, axis=0, keepdims=True)
        spread = jnp.mean(points * points, axis=0, keepdims=True) - centre * centre
        normed = (points - centre) * lax.rsqrt(spread + EPSILON) * gain
        hidden = jax.nn.gelu(product(split(expand_ref[block].T), split(normed)))
        update = scale * product(split(reduce_ref[block]), split(hidden))
        return [update[:, i * LANES : (i + 1) * LANES] for i in range(len(conv))]

    def tap(block, i, j):
        at = block * 11 + 3 * i + j
        return columns_ref[:, at : at + 1]

    views = [
        shifted(
            current[r],
            pltpu.roll(left, (LANES - 2 * r - 1) % LANES, 1),
            pltpu.roll(right, (cols - 1 - 2 * r) % LANES, 1),
        )
        for r in range(wide)
    ]
    conv = []
    for r in range(1, wide - 1):
        conv.append(sum(tap(0, i, j) * views[r + i - 1][j] for i in range(3) for j in range(3)))
    side = jnp.zeros((channels, LANES), jnp.float32)
    for i in range(3):
        line = sum(tap(0, i, j) * beside[j] for j in range(3))
        side = side + (line if i == 1 else pltpu.roll(line, (2 - 2 * i) % LANES, 1))
    update = mixer(0, conv + [side])
    widened = [masks[r] * (current[r] + update[r - 1]) for r in range(1, wide - 1)]
    rim = beside_mask * (beside[1] + update[-1])

    views = [
        shifted(
            widened[r - 1],
            pltpu.roll(rim, (LANES - 2 * r) % LANES, 1),
            pltpu.roll(rim, (cols - 1 - half - 2 * r) % LANES, 1),
        )
        for r in range(1, wide - 1)
    ]
    conv = []
    for r in range(rows):
        conv.append(sum(tap(1, i, j) * views[r + i][j] for i in range(3) for j in range(3)))
    update = mixer(1, conv)
    for r in range(rows):
        out_ref[:, r, :] = masks[r + 2] * (widened[r + 1] + update[r])


def ocean_step(sums, up, down, left, right, ocean_state, land_mask, coupling, source, weight, columns, expand, reduce_w):
    return pl.pallas_call(
        ocean_kernel,
        out_shape=jax.ShapeDtypeStruct(ocean_state.shape, jnp.float32),
        compiler_params=params(60),
        name="ocean_step",
    )(
        sums,
        up,
        down,
        left,
        right,
        ocean_state,
        land_mask,
        jnp.repeat(coupling, 8, axis=1),
        source,
        weight,
        columns,
        expand,
        jnp.swapaxes(reduce_w, 1, 2),
    )


def depthwise(field, taps):
    height = field.shape[1] - 2
    width = field.shape[2] - 2
    result = jnp.zeros((field.shape[0], height, width), jnp.float32)
    for row_off in range(3):
        for col_off in range(3):
            result = (
                result
                + taps[:, 3 * row_off + col_off][:, None, None]
                * field[:, row_off : row_off + height, col_off : col_off + width]
            )
    return result


def ocean_mixer(values, gain, expand, reduce_w):
    channels, height, width = values.shape
    flat = values.reshape(channels, height * width)
    centre = jnp.mean(flat, axis=0)
    spread = jnp.mean(flat * flat, axis=0) - centre * centre
    normed = (flat - centre) * lax.rsqrt(spread + EPSILON) * gain[:, None]
    hidden = jax.nn.gelu(jnp.einsum("cd,cp->dp", expand, normed, precision=FINE))
    update = jnp.einsum("dc,dp->cp", reduce_w, hidden, precision=FINE)
    return update.reshape(channels, height, width)


def fast_step(
    atmos_state,
    ocean_state,
    land_mask,
    spectral_filter,
    atmos_gain,
    flux_readout,
    surface_coupling,
    surface_readout,
    flux_coupling,
    atmos_row_source,
    atmos_row_weight,
    atmos_col_source,
    atmos_col_weight,
    ocean_row_source,
    ocean_row_weight,
    ocean_col_source,
    ocean_col_weight,
    depth_taps,
    block_gain,
    expand_weight,
    reduce_weight,
    layer_scale,
):
    channels, atm_rows, width = atmos_state.shape
    lat, groups = lax.axis_size("lat"), lax.axis_size(COLUMN)
    places = [lax.axis_index("lat"), lax.axis_index("members"), lax.axis_index(COLUMN)]
    place = jnp.stack(places).astype(jnp.int32)
    members = lax.axis_size("members")
    far = lat // 2
    row_source, row_weight = ocean_row_source.T, ocean_row_weight.T
    col_source, col_weight = ocean_col_source.T, ocean_col_weight.T

    flux, stats = channel_sums(atmos_state, flux_readout)
    up, down = lat_edges(flux, ocean_state, land_mask, row_source, row_weight)
    packed, came, token = {}, {}, up
    for shift in (far, *(j for j in range(1, lat) if j != far), 0):
        packed[shift] = pack_filter(spectral_filter, after(place, token), lat, members, shift)
        token = packed[shift]
    up = lax.ppermute(up, "lat", [(i, i + 1) for i in range(lat - 1)])
    down = lax.ppermute(down, "lat", [(i + 1, i) for i in range(lat - 1)])

    came[0] = packed[0]
    for shift in range(1, lat):
        came[shift] = sent(packed[shift], shift)
    stats = summed_over_columns(stats)
    fresh = [
        normed_pieces(atmos_state, stats, atmos_gain, place, lat, q) for q in range(CHUNKS)
    ]
    up, down = lax.optimization_barrier((up, down, fresh[0][0], fresh[-1][0]))[:2]
    sums = summed_over_columns(flux_rows(place, up, down, flux, row_source, row_weight))
    first, last = lon_sides(up, down, ocean_state, land_mask, col_source, col_weight)
    left = lax.ppermute(last, COLUMN, [(i, (i + 1) % groups) for i in range(groups)])
    right = lax.ppermute(first, COLUMN, [(i, (i - 1) % groups) for i in range(groups)])
    piece = surface_piece(
        place,
        up,
        down,
        left,
        right,
        ocean_state,
        surface_readout,
        jnp.concatenate([atmos_row_source.astype(jnp.float32), atmos_row_weight], axis=1),
        atmos_col_source.T,
        atmos_col_weight.T,
        ocean_state.shape[2] * groups,
        width,
    )
    atmos_next = forced(atmos_state, surface_coupling, summed_over_columns(piece))
    columns = jnp.concatenate([depth_taps, block_gain[..., None], layer_scale[..., None]], axis=2)
    ocean_next = ocean_step(
        sums,
        up,
        down,
        left,
        right,
        ocean_state,
        land_mask,
        flux_coupling,
        col_source,
        col_weight,
        jnp.concatenate([columns[0], columns[1]], axis=1),
        expand_weight,
        reduce_weight,
    )

    done = (atmos_next, ocean_next, fresh[0][0], fresh[-1][0])
    pieces, token = [], (came[far], done)
    for q in range(CHUNKS):
        pieces.append(dealt(lax.optimization_barrier((*fresh[q], token))[:lat]))
        token = pieces[q][far]
    came = lax.optimization_barrier((*(came[j] for j in range(lat)), done))[:lat]
    filters = swapped_filter(came)
    pieces = [dealt(filtered_pieces(pieces[q], *filters[q], place)) for q in range(CHUNKS)]
    for q in range(CHUNKS):
        atmos_next = joined(atmos_next, pieces[q], place, q)
    return (atmos_next, ocean_next)


def general_step(
    atmos_state,
    ocean_state,
    land_mask,
    spectral_filter,
    atmos_gain,
    flux_readout,
    surface_coupling,
    surface_readout,
    flux_coupling,
    atmos_row_source,
    atmos_row_weight,
    atmos_col_source,
    atmos_col_weight,
    ocean_row_source,
    ocean_row_weight,
    ocean_col_source,
    ocean_col_weight,
    depth_taps,
    block_gain,
    expand_weight,
    reduce_weight,
    layer_scale,
):
    channels, atm_rows, width_atm = atmos_state.shape
    ocean_channels, ocean_rows, ocean_cols = ocean_state.shape
    lat_place = lax.axis_index("lat")

    ocean_mask = land_mask.astype(jnp.float32)
    row_table = jnp.concatenate([ocean_row_source.astype(jnp.float32), ocean_row_weight], axis=1)
    col_table = jnp.concatenate([ocean_col_source.astype(jnp.float32), ocean_col_weight], axis=1)
    row_table = jnp.pad(row_table, ((0, 0), (0, ocean_cols - row_table.shape[1])))
    wide = jnp.concatenate([ocean_state, ocean_mask[None], row_table[None]], axis=0)
    wide = padded(wide, (("lat", 1),), 2)
    row_table = wide[-1, :, 0:4]
    col_table = jnp.pad(col_table.T, ((0, wide.shape[1] - 4), (0, 0)))
    wide = jnp.concatenate([wide[:-1], col_table[None]], axis=0)
    wide = padded(wide, ((COLUMN, 2),), 2)
    col_table = wide[-1, 0:4].T
    state_wide, mask_wide = wide[:ocean_channels], wide[ocean_channels]

    partial_flux = jnp.einsum("fc,chw->fhw", flux_readout, atmos_state, precision=PRECISE)
    sums = jnp.concatenate(
        [
            partial_flux,
            jnp.sum(atmos_state, axis=0)[None],
            jnp.sum(atmos_state * atmos_state, axis=0)[None],
        ],
        axis=0,
    )
    sums = summed_over_columns(sums)
    flux, stats = sums[:-2], sums[-2:]

    surface_wide = jnp.einsum("sc,chw->shw", surface_readout, state_wide, precision=PRECISE)
    row_map = regrid_matrix(
        atmos_row_source, atmos_row_weight, lat_place * ocean_rows - 2, ocean_rows + 4, 0
    )
    col_map = regrid_matrix(
        atmos_col_source,
        atmos_col_weight,
        lax.axis_index(COLUMN) * ocean_cols - 2,
        ocean_cols + 4,
        ocean_cols * lax.axis_size(COLUMN),
    )
    atmos_piece = apply_maps(surface_wide, row_map, col_map)
    fields = lax.all_gather(atmos_piece, COLUMN, axis=2, tiled=True)

    centre = stats[0] / CA
    spread = stats[1] / CA - centre * centre
    normed = (atmos_state - centre) * lax.rsqrt(spread + EPSILON) * atmos_gain[:, None, None]
    filtered = global_filter(normed, spectral_filter)
    forcing = jnp.einsum("cs,shw->chw", surface_coupling, fields, precision=PRECISE)
    atmos_next = atmos_state + filtered + forcing

    before, behind = flux_reach(atm_rows, ocean_rows)
    flux_wide = rows_around(flux, before, behind)
    row_back = regrid_matrix(
        row_table[:, 0:2].astype(jnp.int32),
        row_table[:, 2:4],
        lat_place * atm_rows - before,
        atm_rows + before + behind,
        0,
    )
    col_back = regrid_matrix(
        col_table[:, 0:2].astype(jnp.int32), col_table[:, 2:4], 0, width_atm, 0
    )
    flux_ocean = apply_maps(flux_wide, row_back, col_back)
    current = mask_wide * (
        state_wide + jnp.einsum("cf,fhw->chw", flux_coupling, flux_ocean, precision=PRECISE)
    )
    update = ocean_mixer(
        depthwise(current, depth_taps[0]), block_gain[0], expand_weight[0], reduce_weight[0]
    )
    widened = mask_wide[1:-1, 1:-1] * (
        current[:, 1:-1, 1:-1] + layer_scale[0][:, None, None] * update
    )
    update = ocean_mixer(
        depthwise(widened, depth_taps[1]), block_gain[1], expand_weight[1], reduce_weight[1]
    )
    current = ocean_mask * (widened[:, 1:-1, 1:-1] + layer_scale[1][:, None, None] * update)
    return (atmos_next, current)


def body(*arrays):
    atmos_state, ocean_state, _, spectral_filter = arrays[:4]
    channels, atm_rows, width = atmos_state.shape
    lat, members, groups = (lax.axis_size(a) for a in ("lat", "members", COLUMN))
    freqs, height = spectral_filter.shape[2:]
    fast = can_deal(channels, atm_rows, width, freqs, height, lat, members) and can_tile(
        *ocean_state.shape, atm_rows, groups
    )
    return fast_step(*arrays) if fast else general_step(*arrays)


def solution(mesh):
    return jax.shard_map(
        body,
        mesh=mesh,
        in_specs=(
            P(("members", "lon", "chan"), "lat", None),
            P("members", "lat", ("lon", "chan")),
            P("lat", ("lon", "chan")),
            P(None, ("lon", "chan"), "lat", None),
            P(("lon", "chan")),
            P(None, ("lon", "chan")),
            P(("lon", "chan"), None),
            P(),
            P(),
            P("lat", None),
            P("lat", None),
            P(("lon", "chan"), None),
            P(("lon", "chan"), None),
            P("lat", None),
            P("lat", None),
            P(("lon", "chan"), None),
            P(("lon", "chan"), None),
            P(),
            P(),
            P(),
            P(),
            P(),
        ),
        out_specs=(
            P(("members", "lon", "chan"), "lat", None),
            P("members", "lat", ("lon", "chan")),
        ),
        check_vma=False,
    )
```
